128 devices in a mesh: ctx: 16 (over z, y_lo, core), fsdp: 8 (over y_hi, x).
Axes of the slice: x: 4, y: 4 (y_hi: 2, y_lo: 2; y = y_hi * 2 + y_lo), z: 4, core: 2. Of those that a mesh axis runs over, the one named last changes fastest.
Arguments:
- tokens: bfloat16 [8, 2048, 1024], P('fsdp', 'ctx'), may hold values from -6 to 6
- upstream: bfloat16 [8, 2048, 1024], P('fsdp', 'ctx'), may hold values from -6 to 6
- block_pairs: int32 [8, 16], P('fsdp'), may hold values from 0 to 15, as said below
- rotary_place: int32 [8, 2048], P('fsdp', 'ctx'), may hold values from 0 to 2047, as said below
- first_gain: bfloat16 [1024], P('fsdp'), may hold values from 0.25 to 1.75
- first_shift: bfloat16 [1024], P('fsdp'), may hold values from -1.25 to 1.25
- joint_weight: bfloat16 [1024, 3072], P('fsdp'), may hold values from -0.1875 to 0.1875
- joint_bias: bfloat16 [3072], P('fsdp'), may hold values from -1.75 to 1.75
- dense_weight: bfloat16 [1024, 1024], P('fsdp'), may hold values from -3 to 3
- dense_bias: bfloat16 [1024], P('fsdp'), may hold values from -1.75 to 1.75
- second_gain: bfloat16 [1024], P('fsdp'), may hold values from 0.25 to 1.75
- second_shift: bfloat16 [1024], P('fsdp'), may hold values from -1.25 to 1.25
- widen_weight: bfloat16 [1024, 4096], P('fsdp'), may hold values from -0.1875 to 0.1875
- widen_bias: bfloat16 [4096], P('fsdp'), may hold values from -3 to 3
- narrow_weight: bfloat16 [4096, 1024], P('fsdp'), may hold values from -0.09375 to 0.09375
- narrow_bias: bfloat16 [1024], P('fsdp'), may hold values from -1.75 to 1.75
Outputs:
- block_out: bfloat16 [8, 2048, 1024], P('fsdp', 'ctx')
- tokens_grad: float32 [8, 2048, 1024], P('fsdp', 'ctx')
- first_gain_grad: float32 [1024], P('fsdp')
- first_shift_grad: float32 [1024], P('fsdp')
- joint_weight_grad: float32 [1024, 3072], P('fsdp')
- joint_bias_grad: float32 [3072], P('fsdp')
- dense_weight_grad: float32 [1024, 1024], P('fsdp')
- dense_bias_grad: float32 [1024], P('fsdp')
- second_gain_grad: float32 [1024], P('fsdp')
- second_shift_grad: float32 [1024], P('fsdp')
- widen_weight_grad: float32 [1024, 4096], P('fsdp')
- widen_bias_grad: float32 [4096], P('fsdp')
- narrow_weight_grad: float32 [4096, 1024], P('fsdp')
- narrow_bias_grad: float32 [1024], P('fsdp')
The draws below stay inside these ranges and needn't reach their ends.
Inputs may be any that keep to these rules, and one draw needn't show every extreme that they name: Each row names every value once; in sequence s the rows of ctx index c hold causal blocks p and 31 - p, p = block_pairs[s, c], the lower block first. `rotary_place`: a row's causal place minus the causal place where its document begins; each sequence's first document begins at place 0, the others at places drawn from the seed; one sequence, drawn from the seed, is a single document.
All inputs are finite; a program needn't handle non-finite values.
Results may differ from the reference program's by a relative error of at most 0.024.
Values may be sent and summed in bfloat16 or wider, within the bound.
No kernel may reach another device: no remote copies, remote signals or barrier semaphores. Data moves between devices by JAX's collectives and lax.ppermute only.
A program may use at most 192 MiB of HBM per device.

```python
import math
import jax
import jax.numpy as jnp
from jax import lax

D = 1024
HEADS = 16
FF = 4096
HD = 64
ROT = 16
BLK = 64
LEN = 2048
SEQS = 8
N_CTX = 16


def dealt_pairs(key):
    seq_keys = jax.random.split(key, SEQS)
    return jax.vmap(lambda single: jax.random.permutation(single, N_CTX))(seq_keys).astype(jnp.int32)


def draw_block_pairs(key, part):
    return dealt_pairs(key)


def draw_rotary_place(key, part):
    pairs = dealt_pairs(key)
    key = jax.random.fold_in(key, 7)
    lone_key = jax.random.fold_in(key, 11)
    seq_length = 2 * N_CTX * BLK
    stored = jnp.arange(seq_length, dtype=jnp.int32)
    lone = jax.random.randint(lone_key, (), 0, SEQS)
    seq_index = jnp.arange(SEQS, dtype=jnp.int32)
    begins = jax.random.randint(key, (SEQS, seq_length), 0, max(seq_length // 4, 2)) == 0
    begins = begins & (seq_index[:, None] != lone)
    begins = begins | (stored[None, :] == 0)
    starts = lax.cummax(jnp.where(begins, stored[None, :], 0), axis=1)
    inside = stored[None, :] - starts
    holder = stored // (2 * BLK)
    within = stored % (2 * BLK)
    chosen = (holder[:, None] == jnp.arange(N_CTX, dtype=jnp.int32)[None, :]).astype(jnp.int32)
    earlier = jnp.sum(chosen[None, :, :] * pairs[:, None, :], axis=2)
    causal_block = jnp.where(within[None, :] < BLK, earlier, 2 * N_CTX - 1 - earlier)
    causal = (causal_block * BLK + within[None, :] % BLK).astype(jnp.int32)
    return jnp.take_along_axis(inside, causal, axis=1).astype(jnp.int32)


def level_of(key, shape, cuts, least, high):
    factor_of = 1.0
    for dim, shards_of in cuts:
        draws = jax.random.uniform(jax.random.fold_in(jax.random.fold_in(key, 6), dim), (shards_of,), jnp.float32, least / len(cuts), high / len(cuts))
        factor_of = factor_of * jnp.repeat(jnp.exp(draws), shape[dim] // shards_of).reshape((-1,) + (1,) * (len(shape) - 1 - dim))
    return factor_of


def noise(own_key, shape, scale, most, cuts=(), kind=jnp.bfloat16):
    result = scale * jax.random.normal(own_key, shape, jnp.float32)
    if cuts:
        result = result * level_of(own_key, shape, cuts, -0.22, 0.18)
    return jnp.clip(result, -most, most).astype(kind)


def setup_inputs(seed: int = 0) -> dict:
    splits = jax.random.split(jax.random.key(seed), 17)
    return {
        "tokens": noise(splits[0], (SEQS, LEN, D), 1.0, 6.0, ((0, 8), (1, 16))),
        "upstream": noise(splits[1], (SEQS, LEN, D), 1.0, 6.0, ((0, 8), (1, 16))),
        "block_pairs": draw_block_pairs(jax.random.fold_in(splits[16], 71), 0),
        "rotary_place": draw_rotary_place(jax.random.fold_in(splits[16], 71), 0),
        "first_gain": jnp.clip(1.0 + 0.15 * jax.random.normal(splits[4], (D,), jnp.float32), 0.25, 1.75).astype(jnp.bfloat16),
        "first_shift": noise(splits[5], (D,), 0.2, 1.25, ((0, 8),)),
        "joint_weight": noise(splits[6], (D, 3 * D), D ** -0.5, 0.1875, ((0, 8),)),
        "joint_bias": noise(splits[7], (3 * D,), 0.3, 1.75, ((0, 8),)),
        "dense_weight": noise(splits[8], (D, D), (max(D // 256, 1)) ** -0.5, 3.0, ((0, 8),)),
        "dense_bias": noise(splits[9], (D,), 0.3, 1.75, ((0, 8),)),
        "second_gain": jnp.clip(1.0 + 0.15 * jax.random.normal(splits[10], (D,), jnp.float32), 0.25, 1.75).astype(jnp.bfloat16),
        "second_shift": noise(splits[11], (D,), 0.2, 1.25, ((0, 8),)),
        "widen_weight": noise(splits[12], (D, FF), D ** -0.5, 0.1875, ((0, 8),)),
        "widen_bias": noise(splits[13], (FF,), 0.5, 3.0, ((0, 8),)),
        "narrow_weight": noise(splits[14], (FF, D), FF ** -0.5, 0.09375, ((0, 8),)),
        "narrow_bias": noise(splits[15], (D,), 0.3, 1.75, ((0, 8),)),
    }


@jax.custom_vjp
def low(v):
    return lax.optimization_barrier(v.astype(jnp.bfloat16)).astype(jnp.float32)

@jax.custom_vjp
def low_back(v):
    return v

def low_keep(v):
    return (low(v), None)

def low_pass(kept, grad):
    return (grad,)

def back_keep(v):
    return (v, None)

def back_low(kept, grad):
    return (low(grad),)
low.defvjp(low_keep, low_pass)
low_back.defvjp(back_keep, back_low)
EPSILON = 1e-05
NEGATIVE = -1e+30
ROTARY_BASE = 10000.0

def causal_places(pairs, blk):
    n_ctx = pairs.shape[1]
    stored = jnp.arange(2 * n_ctx * blk, dtype=jnp.int32)
    holder = stored // (2 * blk)
    within = stored % (2 * blk)
    chosen = (holder[:, None] == jnp.arange(n_ctx, dtype=jnp.int32)[None, :]).astype(jnp.int32)
    earlier = lax.optimization_barrier(jnp.sum(chosen[None, :, :] * pairs[:, None, :], axis=2))
    causal_block = jnp.where(within[None, :] < blk, earlier, 2 * n_ctx - 1 - earlier)
    return (causal_block * blk + within[None, :] % blk).astype(jnp.int32)

def normalize(values, gain, shift):
    center = values - lax.optimization_barrier(jnp.mean(values, axis=-1, keepdims=True))
    spread = lax.optimization_barrier(jnp.mean(center * center, axis=-1, keepdims=True))
    return center * lax.rsqrt(spread + EPSILON) * gain + shift

def rotate(tensor, cosine, sine, direction):
    half_dims = cosine.shape[-1]
    earlier = tensor[..., :half_dims]
    later = tensor[..., half_dims:2 * half_dims]
    remain = tensor[..., 2 * half_dims:]
    return jnp.concatenate([earlier * cosine - direction * later * sine, later * cosine + direction * earlier * sine, remain], axis=-1)

def rotary_tables(places, rot_dims):
    steps_idx = jnp.arange(rot_dims // 2, dtype=jnp.float32)
    inverse = ROTARY_BASE ** (-2.0 * steps_idx / rot_dims)
    angles = places.astype(jnp.float32)[..., None] * inverse
    return (jnp.cos(angles)[..., None, :], jnp.sin(angles)[..., None, :])

def sequence_layer(inputs, key_places, places, params):
    first_gain, first_shift, joint_weight, joint_bias, dense_weight, dense_bias, second_gain, second_shift, widen_weight, widen_bias, narrow_weight, narrow_bias = params
    seq_length = inputs.shape[0]
    highest = lax.Precision.HIGHEST
    first_normed = low(normalize(inputs, first_gain, first_shift))
    second_normed = low(normalize(inputs, second_gain, second_shift))
    joint = low_back(jnp.dot(first_normed, joint_weight, precision=highest) + joint_bias)
    joint = joint.reshape(seq_length, 3, HEADS, HD)
    cosine, sine = rotary_tables(places, ROT)
    queries = low(rotate(joint[:, 0], cosine, sine, 1.0))
    keys = low(rotate(joint[:, 1], cosine, sine, 1.0))
    values = low(joint[:, 2])
    span = math.gcd(seq_length, 512)
    count = seq_length // span

    def attend(index):
        query_portion = lax.dynamic_slice_in_dim(queries, index * span, span, 0)
        query_place = lax.dynamic_slice_in_dim(key_places, index * span, span, 0)
        scores = low_back(jnp.einsum('qhe,khe->hqk', query_portion, keys, precision=highest) * HD ** (-0.5))
        scores = jnp.where(key_places[None, None, :] <= query_place[None, :, None], scores, NEGATIVE)
        largest = lax.optimization_barrier(jnp.max(scores, axis=-1, keepdims=True))
        exponent = jnp.exp(scores - largest)
        probabilities = low(exponent / lax.optimization_barrier(jnp.sum(exponent, axis=-1, keepdims=True)))
        return jnp.einsum('hqk,khe->qhe', probabilities, values, precision=highest)
    attended = lax.map(jax.checkpoint(attend), jnp.arange(count, dtype=jnp.int32))
    attended = low(low_back(attended.reshape(seq_length, D)))
    dense_out = jnp.dot(attended, dense_weight, precision=highest) + dense_bias
    widened = low_back(jnp.dot(second_normed, widen_weight, precision=highest) + widen_bias)
    activated = low(jax.nn.gelu(widened, approximate=False))
    narrow_out = jnp.dot(activated, narrow_weight, precision=highest) + narrow_bias
    return inputs + dense_out + narrow_out

def reference(tokens, upstream, block_pairs, rotary_place, first_gain, first_shift, joint_weight, joint_bias, dense_weight, dense_bias, second_gain, second_shift, widen_weight, widen_bias, narrow_weight, narrow_bias):
    key_places = causal_places(block_pairs, BLK)
    params = tuple((item.astype(jnp.float32) for item in (first_gain, first_shift, joint_weight, joint_bias, dense_weight, dense_bias, second_gain, second_shift, widen_weight, widen_bias, narrow_weight, narrow_bias)))
    inputs = tokens.astype(jnp.float32)

    def forward(layer_in, layer_params):

        def single(items):
            seq_inputs, seq_keys, seq_places = items
            return sequence_layer(seq_inputs, seq_keys, seq_places, layer_params)
        return lax.map(jax.checkpoint(single), (layer_in, key_places, rotary_place))
    outputs, pullback = jax.vjp(forward, inputs, params)
    tokens_grad, grads = pullback(upstream.astype(jnp.float32))
    grad_fg, grad_fs, grad_jw, grad_jb, grad_dw, grad_db, grad_sg, grad_ss, grad_ww, grad_wb, grad_nw, grad_nb = grads
    return (outputs.astype(jnp.bfloat16), tokens_grad, grad_fg, grad_fs, grad_jw, grad_jb, grad_dw, grad_db, grad_sg, grad_ss, grad_ww, grad_wb, grad_nw, grad_nb)
```

```python
import jax
import jax.numpy as jnp
from jax import lax
from jax.experimental import pallas as pl
from jax.experimental.pallas import tpu as pltpu
from jax.sharding import PartitionSpec as P

HEADS = 16
EPSILON = 1e-05
NEGATIVE = -1e30
ROTARY_BASE = 10000.0
N_CTX = 16
N_FSDP = 8
F32 = jnp.float32
BF16 = jnp.bfloat16

UP_Z = [((i + 4) % 16, i) for i in range(16)]
DOWN_Z = [((i + 12) % 16, i) for i in range(16)]
ACROSS_Y = [(i ^ 2, i) for i in range(16)]
OTHER_CORE = [(i ^ 1, i) for i in range(16)]
TURN = [(c * 8 + f, (2 * f + (c & 1)) * 8 + (c >> 1)) for c in range(16) for f in range(8)]


def from_up(v):
    return lax.ppermute(v, "ctx", UP_Z)


def from_down(v):
    return lax.ppermute(v, "ctx", DOWN_Z)


def from_across(v):
    return lax.ppermute(v, "ctx", ACROSS_Y)


def from_core(v):
    return lax.ppermute(v, "ctx", OTHER_CORE)


def turn(v):
    return lax.ppermute(v, ("ctx", "fsdp"), TURN)


def gather_chips(own):
    rows = own.shape[0]
    a, b = 48, 96
    b10, b30, b01 = from_up(own), from_down(own), from_across(own)
    b20, b31, b11 = from_up(b10), from_down(b01), from_across(b10)
    b21 = jnp.concatenate([from_across(b20[:a]), from_up(b11[a:b]), from_down(b31[b:rows])], axis=0)
    return jnp.stack([own, b01, b10, b11, b20, b21, b30, b31])


def gather_ctx(own):
    mine = gather_chips(own)
    return jnp.concatenate([mine, from_core(mine)], axis=0)


def add(p, q):
    return (p.astype(F32) + q.astype(F32)).astype(BF16)


def scatter_ctx(parts):
    rows = parts.shape[1]
    a, b = 48, 96
    q = add(parts[:8], from_core(parts[8:]))
    q00, q01, q10, q11, q20, q21, q30, q31 = [q[i] for i in range(8)]
    r_y, r_d, r_u = from_across(q21[:a]), from_down(q21[a:b]), from_up(q21[b:rows])
    q20 = jnp.concatenate([add(q20[:a], r_y), q20[a:]], axis=0)
    q11 = jnp.concatenate([q11[:a], add(q11[a:b], r_d), q11[b:]], axis=0)
    q31 = jnp.concatenate([q31[:b], add(q31[b:], r_u)], axis=0)
    t10, t01, s10 = from_down(q20), from_up(q31), from_across(q11)
    q10 = (q10.astype(F32) + t10.astype(F32) + s10.astype(F32)).astype(BF16)
    q01 = add(q01, t01)
    r1, r2, r3 = from_down(q10), from_up(q30), from_across(q01)
    return q00.astype(F32) + r1.astype(F32) + r2.astype(F32) + r3.astype(F32)


def shift_fsdp(v, d):
    return lax.ppermute(v, "fsdp", [(i, (i + d) % N_FSDP) for i in range(N_FSDP)])


def gather_fsdp(own, f):
    rows = own.shape[0]
    out = jnp.zeros((N_FSDP * rows,) + own.shape[1:], own.dtype)
    out = lax.dynamic_update_slice_in_dim(out, own, f * rows, 0)
    for d in range(1, N_FSDP):
        got = shift_fsdp(own, d)
        out = lax.dynamic_update_slice_in_dim(out, got, ((f + N_FSDP - d) % N_FSDP) * rows, 0)
    return out


def scatter_fsdp(blocks, f):
    take = lambda d: lax.dynamic_index_in_dim(blocks, (f + d) % N_FSDP, 0, keepdims=False)
    total = take(0).astype(F32)
    for d in range(1, N_FSDP):
        total = total + shift_fsdp(take(d), d).astype(F32)
    return total


def attention_kernel(order_ref, joint_ref, table_ref, grad_ref, out_ref,
                     joint_s, table_s, grad_s, k_s, v_s, qT_s, kT_s, vT_s, gT_s,
                     oT_s, dqT_s, dkT_s, dvT_s, cosT_s, sinT_s, out_s):
    rows, hd = joint_ref.shape[0], joint_ref.shape[1] // 3
    slots, half, tile = N_CTX, rows // (2 * N_CTX), 256
    last = 2 * slots - 1
    for j in range(slots):
        p = order_ref[j]
        for h in range(2):
            src = pl.ds(j * 2 * half + h * half, half)
            dst = pl.ds(pl.multiple_of((p if h == 0 else last - p) * half, half), half)
            joint_s[dst, :] = joint_ref[src, :]
            table_s[dst, :] = table_ref[src, :]
            grad_s[dst, :] = grad_ref[src, :].astype(F32)
    scale = hd ** -0.5

    def spin(t, c, s):
        return jnp.concatenate([t[0:8] * c - t[8:16] * s, t[8:16] * c + t[0:8] * s, t[16:]], axis=0)

    for i in range(rows // tile):
        at = pl.ds(i * tile, tile)
        jT = joint_s[at, :].T
        tT = table_s[at, :].T
        c, s = tT[0:8], tT[8:16]
        cosT_s[:, at] = c
        sinT_s[:, at] = s
        qT = spin(jT[0:hd], c, s).astype(BF16)
        kT = spin(jT[hd:2 * hd], c, s).astype(BF16)
        vT = jT[2 * hd:].astype(BF16)
        qT_s[:, at] = (qT.astype(F32) * scale).astype(BF16)
        kT_s[:, at] = kT
        vT_s[:, at] = vT
        k_s[at, :] = kT.astype(F32).T.astype(BF16)
        v_s[at, :] = vT.astype(F32).T.astype(BF16)
        gT_s[:, at] = grad_s[at, :].T.astype(BF16)
    dkT_s[...] = jnp.zeros_like(dkT_s)
    dvT_s[...] = jnp.zeros_like(dvT_s)
    key_at = lax.broadcasted_iota(jnp.int32, (tile, tile), 0)
    query_at = lax.broadcasted_iota(jnp.int32, (tile, tile), 1)
    seen = key_at <= query_at
    dot = lambda a, b: jnp.dot(a, b, preferred_element_type=F32)
    dot_nt = lambda a, b: lax.dot_general(a, b, (((1,), (1,)), ((), ())), preferred_element_type=F32)
    for i in range(rows // tile):
        at = pl.ds(i * tile, tile)
        span = (i + 1) * tile
        upto = pl.ds(0, span)
        qT, gT = qT_s[:, at], gT_s[:, at]
        sT = dot(k_s[upto, :], qT)
        edge = jnp.where(seen, sT[i * tile:], NEGATIVE)
        sT = edge if i == 0 else jnp.concatenate([sT[:i * tile], edge], axis=0)
        largest = jnp.max(sT, axis=0, keepdims=True)
        e = jnp.exp(sT - largest)
        pT = e * (1.0 / jnp.sum(e, axis=0, keepdims=True))
        pT_low = pT.astype(BF16)
        dpT = dot(v_s[upto, :], gT)
        balance = jnp.sum(dpT * pT, axis=0, keepdims=True)
        dsT = (pT * (dpT - balance)).astype(BF16)
        oT_s[:, at] = dot(vT_s[:, upto], pT_low)
        dqT_s[:, at] = dot(kT_s[:, upto], dsT) * scale
        dkT_s[:, upto] += dot_nt(qT, dsT)
        dvT_s[:, upto] += dot_nt(gT, pT_low)
    for i in range(rows // tile):
        at = pl.ds(i * tile, tile)
        c, s = cosT_s[:, at], -sinT_s[:, at]
        full = jnp.concatenate(
            [spin(dqT_s[:, at], c, s), spin(dkT_s[:, at], c, s), dvT_s[:, at], oT_s[:, at]], axis=0)
        out_s[at, :] = full.T.astype(BF16)
    for j in range(slots):
        p = order_ref[j]
        for h in range(2):
            dst = pl.ds(j * 2 * half + h * half, half)
            src = pl.ds(pl.multiple_of((p if h == 0 else last - p) * half, half), half)
            out_ref[dst, :] = out_s[src, :]


def attention(order, joint, table, grad):
    rows, hd = joint.shape[0], joint.shape[1] // 3
    vmem = pl.BlockSpec(memory_space=pltpu.VMEM)
    return pl.pallas_call(
        attention_kernel,
        out_shape=jax.ShapeDtypeStruct((rows, 4 * hd), BF16),
        in_specs=[pl.BlockSpec(memory_space=pltpu.SMEM), vmem, vmem, vmem],
        out_specs=vmem,
        scratch_shapes=[
            pltpu.VMEM((rows, 3 * hd), F32),
            pltpu.VMEM((rows, 16), F32),
            pltpu.VMEM((rows, hd), F32),
            pltpu.VMEM((rows, hd), BF16),
            pltpu.VMEM((rows, hd), BF16),
            pltpu.VMEM((hd, rows), BF16),
            pltpu.VMEM((hd, rows), BF16),
            pltpu.VMEM((hd, rows), BF16),
            pltpu.VMEM((hd, rows), BF16),
            pltpu.VMEM((hd, rows), F32),
            pltpu.VMEM((hd, rows), F32),
            pltpu.VMEM((hd, rows), F32),
            pltpu.VMEM((hd, rows), F32),
            pltpu.VMEM((8, rows), F32),
            pltpu.VMEM((8, rows), F32),
            pltpu.VMEM((rows, 4 * hd), BF16),
        ],
        compiler_params=pltpu.CompilerParams(vmem_limit_bytes=48 * 1024 * 1024),
        cost_estimate=pl.CostEstimate(flops=7 * rows * rows * hd, bytes_accessed=8 << 20, transcendentals=rows * rows // 2),
    )(order, joint, table, grad)


def dot_tn(a, b):
    return lax.dot_general(a, b, (((0,), (0,)), ((), ())), preferred_element_type=F32)


def dot_nt(a, b):
    return lax.dot_general(a, b, (((1,), (1,)), ((), ())), preferred_element_type=F32)


def dot_nn(a, b):
    return jnp.dot(a, b, preferred_element_type=F32)


def shards(
    tokens, upstream, block_pairs, rotary_place,
    first_gain, first_shift, joint_weight, joint_bias, dense_weight, dense_bias,
    second_gain, second_shift, widen_weight, widen_bias, narrow_weight, narrow_bias,
):
    own_rows, width = tokens.shape[1], tokens.shape[2]
    hd = width // HEADS
    ff = widen_weight.shape[1]
    ffc = ff // N_CTX
    rows = own_rows * N_CTX
    c = lax.axis_index("ctx")
    f = lax.axis_index("fsdp")
    own_tokens, own_up = tokens[0], upstream[0]
    d_own = width // N_FSDP

    place = rotary_place[0]
    extra = jnp.concatenate([(place // 64), (place % 64)]).astype(BF16)
    extra = jnp.pad(extra[None, :], ((0, 7), (0, width - 2 * own_rows)))
    tok_all = gather_ctx(jnp.concatenate([own_tokens, extra], axis=0))

    joint_part = lax.dynamic_index_in_dim(joint_weight.reshape(d_own, 3, HEADS, hd), c, 2, keepdims=False)
    vectors = jnp.concatenate(
        [v[:, None] for v in (first_gain, first_shift, second_gain, second_shift, dense_bias, narrow_bias)]
        + [joint_bias.reshape(d_own, 3), widen_bias.reshape(d_own, 4), jnp.zeros((d_own, 51), BF16)], axis=1)
    widen_part = lax.dynamic_slice_in_dim(widen_weight, c * ffc, ffc, axis=1)
    slices = gather_fsdp(jnp.concatenate([joint_part.reshape(d_own, 3 * hd), vectors, widen_part], axis=1), f)
    odd = c % 2
    back_w = turn(jnp.concatenate([
        lax.dynamic_slice_in_dim(dense_weight, odd * hd, hd, axis=0),
        lax.dynamic_slice_in_dim(narrow_weight, odd * ffc, ffc, axis=0)], axis=0))
    dense_w, narrow_w = back_w[:hd], back_w[hd:]

    tok_dep, own_up_late = lax.optimization_barrier((tok_all, own_up))
    up_all = gather_ctx(own_up_late).reshape(rows, width)
    x = tok_dep[:, :own_rows].reshape(rows, width).astype(F32)
    place_all = (tok_dep[:, own_rows, :own_rows].astype(F32) * 64.0
                 + tok_dep[:, own_rows, own_rows:2 * own_rows].astype(F32)).reshape(rows)
    steps = jnp.arange(8, dtype=F32)
    angles = place_all[:, None] * (ROTARY_BASE ** (-2.0 * steps / 16))
    table = jnp.concatenate([jnp.cos(angles), jnp.sin(angles)], axis=1)
    slot = jnp.arange(N_CTX)
    dz, dy, dc = (slot % 8) // 2, slot % 2, slot // 8
    source = ((c // 4 + dz) % 4) * 4 + (((c // 2) % 2 + dy) % 2) * 2 + (c % 2 + dc) % 2
    order = jnp.sum((source[:, None] == slot[None, :]) * block_pairs[0][None, :], axis=1).astype(jnp.int32)

    wj = slices[:, :3 * hd].astype(F32)
    ww = slices[:, 4 * hd:].astype(F32)
    vec = slices[:, 3 * hd:4 * hd].astype(F32)
    g1, s1, g2, s2 = vec[:, 0:1], vec[:, 1:2], vec[:, 2:3], vec[:, 3:4]
    dense_b, narrow_b = vec[:, 4], vec[:, 5]
    jb_full = vec[:, 6:9].reshape(3, HEADS, hd)
    wb_full = vec[:, 9:13].reshape(ff)
    jb_own = lax.dynamic_index_in_dim(jb_full, c, 1, keepdims=False).reshape(3 * hd)
    wb_own = lax.dynamic_slice_in_dim(wb_full, c * ffc, ffc)
    wj_g = (g1 * wj).astype(BF16)
    ww_g = (g2 * ww).astype(BF16)
    joint_add = jnp.sum(s1 * wj, axis=0) + jb_own
    widen_add = jnp.sum(s2 * ww, axis=0) + wb_own

    center = x - jnp.mean(x, axis=-1, keepdims=True)
    xhat = (center * lax.rsqrt(jnp.mean(center * center, axis=-1, keepdims=True) + EPSILON)).astype(BF16)
    joint = dot_nn(xhat, wj_g) + joint_add
    widened = dot_nn(xhat, ww_g) + widen_add
    phi = 0.5 * (1.0 + lax.erf(widened * (0.5 ** 0.5)))
    act = (widened * phi).astype(BF16)
    slope = phi + widened * jnp.exp(-0.5 * widened * widened) * 0.3989422804014327
    att_grad = dot_nt(up_all, dense_w).astype(BF16)
    wg = (dot_nt(up_all, narrow_w) * slope).astype(BF16)

    m_w = dot_tn(xhat, wg)
    d_n = dot_tn(up_all, act)
    wb_grad = jnp.sum(wg.astype(F32), axis=0)
    up_sum = jnp.sum(up_all.astype(F32), axis=0)
    early_rows = jnp.concatenate([m_w, d_n], axis=1).reshape(N_FSDP, d_own, 2 * ffc)
    early_vec = jnp.concatenate([
        jnp.broadcast_to(wb_grad[None, :], (N_FSDP, ffc)), up_sum.reshape(N_FSDP, d_own),
        jnp.zeros((N_FSDP, ffc - d_own), F32)], axis=1)
    early = jnp.concatenate([early_rows, jnp.pad(early_vec[:, None, :], ((0, 0), (0, 7), (0, 0)))], axis=1).astype(BF16)
    early = scatter_fsdp(early, f)
    bias_grad = early[d_own, ffc:ffc + d_own]
    early_n = turn(early[:d_own, ffc:].astype(BF16))
    early_all = lax.all_gather(
        jnp.concatenate([early[:, :ffc].astype(BF16), jnp.pad(early_n, ((0, 8), (0, 0)))], axis=1), "ctx", axis=0)

    mixed = attention(order, joint, table, att_grad)

    m_j = dot_tn(xhat, mixed)[:, :3 * hd]
    d_d = dot_tn(up_all, mixed)[:, 3 * hd:]
    jb_grad = jnp.sum(mixed.astype(F32), axis=0)
    late = jnp.concatenate([m_j, d_d], axis=1).reshape(N_FSDP, d_own, 4 * hd)
    late = jnp.concatenate([late, jnp.broadcast_to(
        jnp.pad(jb_grad[None, :], ((0, 7), (0, 0)))[None], (N_FSDP, 8, 4 * hd))], axis=1).astype(BF16)
    late = scatter_fsdp(late, f)
    late_d = turn(late[:d_own, 3 * hd:].astype(BF16))
    late_all = lax.all_gather(
        jnp.concatenate([late[:, :3 * hd].astype(BF16), jnp.pad(late_d, ((0, 8), (0, 0)))], axis=1), "ctx", axis=0)

    u = (dot_nt(mixed[:, :3 * hd], wj_g) + dot_nt(wg, ww_g)).astype(BF16)
    u_own = scatter_ctx(u.reshape(N_CTX, own_rows, width))
    out = (dot_nn(mixed[:, 3 * hd:], dense_w) + dot_nn(act, narrow_w)).astype(BF16)
    out_own = scatter_ctx(out.reshape(N_CTX, own_rows, width))
    own_x = own_tokens.astype(F32)
    block_out = (own_x + out_own + dense_b + narrow_b).astype(BF16)
    own_center = own_x - jnp.mean(own_x, axis=-1, keepdims=True)
    own_rstd = lax.rsqrt(jnp.mean(own_center * own_center, axis=-1, keepdims=True) + EPSILON)
    own_xhat = own_center * own_rstd
    tokens_grad = own_up.astype(F32) + own_rstd * (
        u_own - jnp.mean(u_own, axis=-1, keepdims=True)
        - own_xhat * jnp.mean(u_own * own_xhat, axis=-1, keepdims=True))

    early_all = early_all.astype(F32)
    late_all = late_all.astype(F32)
    m_w = jnp.transpose(early_all[:, :d_own, :ffc], (1, 0, 2)).reshape(d_own, ff)
    wb_grad = early_all[:, d_own, :ffc].reshape(ff)
    widen_grad = second_gain.astype(F32)[:, None] * m_w + second_shift.astype(F32)[:, None] * wb_grad[None, :]
    widen_f = widen_weight.astype(F32)
    g2_grad = jnp.sum(widen_f * m_w, axis=1)
    s2_grad = jnp.sum(widen_f * wb_grad[None, :], axis=1)
    narrow_grad = jnp.transpose(
        early_all[:, :d_own, ffc:].reshape(N_FSDP, 2, d_own, ffc), (1, 3, 0, 2)).reshape(2 * ffc, width)
    m_j = jnp.transpose(late_all[:, :d_own, :3 * hd].reshape(N_CTX, d_own, 3, hd), (1, 2, 0, 3)).reshape(d_own, 3 * width)
    jb_grad = jnp.transpose(late_all[:, d_own, :3 * hd].reshape(N_CTX, 3, hd), (1, 0, 2)).reshape(3 * width)
    joint_grad = first_gain.astype(F32)[:, None] * m_j + first_shift.astype(F32)[:, None] * jb_grad[None, :]
    joint_f = joint_weight.astype(F32)
    g1_grad = jnp.sum(joint_f * m_j, axis=1)
    s1_grad = jnp.sum(joint_f * jb_grad[None, :], axis=1)
    dense_grad = jnp.transpose(
        late_all[:, :d_own, 3 * hd:].reshape(N_FSDP, 2, d_own, hd), (1, 3, 0, 2)).reshape(2 * hd, width)
    jb_shard = lax.dynamic_slice_in_dim(jb_grad, f * (3 * d_own), 3 * d_own)
    wb_shard = lax.dynamic_slice_in_dim(wb_grad, f * (ff // N_FSDP), ff // N_FSDP)
    return (
        block_out[None], tokens_grad[None], g1_grad, s1_grad, joint_grad, jb_shard,
        dense_grad, bias_grad, g2_grad, s2_grad, widen_grad, wb_shard, narrow_grad, bias_grad,
    )


def solution(mesh):
    rows = P("fsdp", "ctx", None)
    vec, mat = P("fsdp"), P("fsdp", None)
    in_specs = (rows, rows, mat, P("fsdp", "ctx"), vec, vec, mat, vec, mat, vec, vec, vec, mat, vec, mat, vec)
    out_specs = (rows, rows, vec, vec, mat, vec, mat, vec, vec, vec, mat, vec, mat, vec)
    return jax.shard_map(shards, mesh=mesh, in_specs=in_specs, out_specs=out_specs, check_vma=False)
```

```python
import jax
import jax.numpy as jnp
from jax import lax
from jax.experimental import pallas as pl
from jax.experimental.pallas import tpu as pltpu
from jax.sharding import PartitionSpec as P

HEADS = 16
EPSILON = 1e-05
NEGATIVE = -1e30
ROTARY_BASE = 10000.0
N_CTX = 16
N_FSDP = 8
F32 = jnp.float32
BF16 = jnp.bfloat16

OTHER_CORE = [(i ^ 1, i) for i in range(16)]
SAME_CORE = [list(range(0, 16, 2)), list(range(1, 16, 2))]
TURN = [(c * 8 + f, (2 * f + (c & 1)) * 8 + (c >> 1)) for c in range(16) for f in range(8)]


def turn(v):
    return lax.ppermute(v, ("ctx", "fsdp"), TURN)


def dot_tn(a, b):
    return lax.dot_general(a, b, (((0,), (0,)), ((), ())), preferred_element_type=F32)


def dot_nt(a, b):
    return lax.dot_general(a, b, (((1,), (1,)), ((), ())), preferred_element_type=F32)


def dot_nn(a, b):
    return jnp.dot(a, b, preferred_element_type=F32)


def project_kernel(x_ref, up_ref, wj_ref, ww_ref, add_ref, back_ref, xhat_ref, joint_ref, grad_ref, act_ref, wg_ref):
    block, width = x_ref.shape[0] * x_ref.shape[1], x_ref.shape[2]
    x = x_ref[...].reshape(block, width).astype(F32)
    center = x - jnp.mean(x, axis=-1, keepdims=True)
    xhat = (center * lax.rsqrt(jnp.mean(center * center, axis=-1, keepdims=True) + EPSILON)).astype(BF16)
    xhat_ref[...] = xhat
    wide = wj_ref.shape[1]
    joint_ref[...] = dot_nn(xhat, wj_ref[...]) + add_ref[0:1, :wide]
    widened = dot_nn(xhat, ww_ref[...]) + add_ref[0:1, wide:]
    phi = 0.5 * (1.0 + lax.erf(widened * (0.5 ** 0.5)))
    act_ref[...] = (widened * phi).astype(BF16)
    slope = phi + widened * jnp.exp(-0.5 * widened * widened) * 0.3989422804014327
    up = up_ref[...].reshape(block, width)
    hd = back_ref.shape[0] - ww_ref.shape[1]
    grad_ref[...] = dot_nt(up, back_ref[0:hd, :])
    wg_ref[...] = (dot_nt(up, back_ref[hd:, :]) * slope).astype(BF16)


def project(both, wj, ww, add, back):
    slots, _, width = both.shape
    own, per = 128, 2
    rows, block = slots * own, per * own
    wide, ffc = wj.shape[1], ww.shape[1]
    hd = back.shape[0] - ffc
    whole = lambda a: pl.BlockSpec(a.shape, lambda i: (0, 0))
    tall = lambda n: pl.BlockSpec((block, n), lambda i: (i, 0))
    return pl.pallas_call(
        project_kernel,
        grid=(slots // per,),
        in_specs=[
            pl.BlockSpec((per, own, width), lambda i: (i, 0, 0)),
            pl.BlockSpec((per, own, width), lambda i: (i, 1, 0)),
            whole(wj), whole(ww), whole(add), whole(back)],
        out_specs=[tall(width), tall(wide), tall(hd), tall(ffc), tall(ffc)],
        out_shape=[
            jax.ShapeDtypeStruct((rows, width), BF16), jax.ShapeDtypeStruct((rows, wide), F32),
            jax.ShapeDtypeStruct((rows, hd), F32), jax.ShapeDtypeStruct((rows, ffc), BF16),
            jax.ShapeDtypeStruct((rows, ffc), BF16)],
        compiler_params=pltpu.CompilerParams(vmem_limit_bytes=48 * 1024 * 1024),
        cost_estimate=pl.CostEstimate(flops=2 * rows * width * 832, bytes_accessed=20 << 20, transcendentals=rows * 512),
    )(both, both, wj, ww, add, back)


def grads_kernel(xhat_ref, up_ref, mixed_ref, act_ref, wg_ref, out_ref):
    rows = xhat_ref.shape[0]
    n, m, k = xhat_ref.shape[1], mixed_ref.shape[1], act_ref.shape[1]
    hd = m // 4
    xhat = xhat_ref[...]
    up = up_ref[...].reshape(rows, n)
    mixed, act, wg = mixed_ref[...], act_ref[...], wg_ref[...]
    lane = lax.broadcasted_iota(jnp.int32, (n, m), 1)
    out_ref[0, 0:n, 0:m] = jnp.where(lane < 3 * hd, dot_tn(xhat, mixed), dot_tn(up, mixed)).astype(BF16)
    out_ref[0, 0:n, m:m + k] = dot_tn(xhat, wg).astype(BF16)
    out_ref[0, 0:n, m + k:] = dot_tn(up, act).astype(BF16)
    ones = jnp.ones((16, rows), BF16)
    out_ref[0, n:, 0:m] = dot_nn(ones, mixed).astype(BF16)
    out_ref[0, n:, m:m + k] = dot_nn(ones, wg).astype(BF16)
    out_ref[0, n:, m + k:m + k + n] = dot_nn(ones, up).astype(BF16)
    out_ref[0, n:, m + k + n:] = jnp.zeros((16, k - n), BF16)


def grads(xhat, both, mixed, act, wg):
    rows, width = xhat.shape
    n = width // N_FSDP
    total = mixed.shape[1] + act.shape[1] + wg.shape[1]
    whole = lambda a: pl.BlockSpec(a.shape, lambda i: (0, 0))
    return pl.pallas_call(
        grads_kernel,
        grid=(N_FSDP,),
        in_specs=[
            pl.BlockSpec((rows, n), lambda i: (0, i)),
            pl.BlockSpec((both.shape[0], 128, n), lambda i: (0, 1, i)),
            whole(mixed), whole(act), whole(wg)],
        out_specs=pl.BlockSpec((1, n + 16, total), lambda i: (i, 0, 0)),
        out_shape=jax.ShapeDtypeStruct((N_FSDP, n + 16, total), BF16),
        compiler_params=pltpu.CompilerParams(vmem_limit_bytes=48 * 1024 * 1024),
        cost_estimate=pl.CostEstimate(flops=2 * rows * width * 1024, bytes_accessed=14 << 20, transcendentals=0),
    )(xhat, both, mixed, act, wg)


def spread_kernel(core_ref, mixed_ref, wg_ref, act_ref, wj_ref, ww_ref, dense_ref, narrow_ref, mine_ref, other_ref):
    width = wj_ref.shape[0]
    half = mine_ref.shape[1]
    mixed = mixed_ref[...]
    u = (dot_nt(mixed, wj_ref[...]) + dot_nt(wg_ref[...], ww_ref[...])).astype(BF16)
    out = (dot_nn(mixed, dense_ref[...]) + dot_nn(act_ref[...], narrow_ref[...])).astype(BF16)

    def put(low_ref, high_ref):
        for ref, at in ((low_ref, 0), (high_ref, half)):
            ref[0, :, :width] = u[at:at + half]
            ref[0, :, width:] = out[at:at + half]

    @pl.when(core_ref[0] == 0)
    def _():
        put(mine_ref, other_ref)

    @pl.when(core_ref[0] != 0)
    def _():
        put(other_ref, mine_ref)


def spread(core, mixed, wg, act, wj, ww, dense, narrow):
    rows, width = mixed.shape[0], wj.shape[0]
    own = rows // N_CTX
    whole = lambda a: pl.BlockSpec(a.shape, lambda i: (0, 0))
    tall = lambda a: pl.BlockSpec((2 * own, a.shape[1]), lambda i: (i, 0))
    shape = jax.ShapeDtypeStruct((N_CTX // 2, own, 2 * width), BF16)
    return pl.pallas_call(
        spread_kernel,
        grid=(N_CTX // 2,),
        in_specs=[pl.BlockSpec(memory_space=pltpu.SMEM), tall(mixed), tall(wg), tall(act),
                  whole(wj), whole(ww), whole(dense), whole(narrow)],
        out_specs=[pl.BlockSpec((1, own, 2 * width), lambda i: (i, 0, 0))] * 2,
        out_shape=[shape, shape],
        compiler_params=pltpu.CompilerParams(vmem_limit_bytes=48 * 1024 * 1024),
        cost_estimate=pl.CostEstimate(flops=2 * rows * width * 1024, bytes_accessed=14 << 20, transcendentals=0),
    )(core, mixed, wg, act, wj, ww, dense, narrow)


def attention_kernel(order_ref, joint_ref, table_ref, grad_ref, out_ref,
                     joint_s, table_s, grad_s, k_s, v_s, qT_s, kT_s, vT_s, gT_s,
                     oT_s, dqT_s, dkT_s, dvT_s, cosT_s, sinT_s, out_s):
    rows, hd = joint_ref.shape[0], joint_ref.shape[1] // 4
    slots, half, tile = N_CTX, rows // (2 * N_CTX), 256
    last = 2 * slots - 1
    for j in range(slots):
        p = order_ref[j]
        for h in range(2):
            src = pl.ds(j * 2 * half + h * half, half)
            dst = pl.ds(pl.multiple_of((p if h == 0 else last - p) * half, half), half)
            joint_s[dst, :] = joint_ref[src, :]
            table_s[dst, :] = table_ref[src, :]
            grad_s[dst, :] = grad_ref[src, :]
    scale = hd ** -0.5

    def spin(t, c, s):
        return jnp.concatenate([t[0:8] * c - t[8:16] * s, t[8:16] * c + t[0:8] * s, t[16:]], axis=0)

    for i in range(rows // tile):
        at = pl.ds(i * tile, tile)
        jT = joint_s[at, :].T
        tT = table_s[at, :].T
        c, s = tT[0:8], tT[8:16]
        cosT_s[:, at] = c
        sinT_s[:, at] = s
        qT = spin(jT[0:hd], c, s).astype(BF16)
        kT = spin(jT[hd:2 * hd], c, s).astype(BF16)
        vT = jT[2 * hd:3 * hd].astype(BF16)
        qT_s[:, at] = (qT.astype(F32) * scale).astype(BF16)
        kT_s[:, at] = kT
        vT_s[:, at] = vT
        k_s[at, :] = kT.astype(F32).T.astype(BF16)
        v_s[at, :] = vT.astype(F32).T.astype(BF16)
        gT_s[:, at] = grad_s[at, :].T.astype(BF16)
    dkT_s[...] = jnp.zeros_like(dkT_s)
    dvT_s[...] = jnp.zeros_like(dvT_s)
    key_at = lax.broadcasted_iota(jnp.int32, (tile, tile), 0)
    query_at = lax.broadcasted_iota(jnp.int32, (tile, tile), 1)
    seen = key_at <= query_at
    dot = lambda a, b: jnp.dot(a, b, preferred_element_type=F32)
    dot_nt = lambda a, b: lax.dot_general(a, b, (((1,), (1,)), ((), ())), preferred_element_type=F32)
    for i in range(rows // tile):
        at = pl.ds(i * tile, tile)
        span = (i + 1) * tile
        upto = pl.ds(0, span)
        qT, gT = qT_s[:, at], gT_s[:, at]
        sT = dot(k_s[upto, :], qT)
        edge = jnp.where(seen, sT[i * tile:], NEGATIVE)
        sT = edge if i == 0 else jnp.concatenate([sT[:i * tile], edge], axis=0)
        largest = jnp.max(sT, axis=0, keepdims=True)
        e = jnp.exp(sT - largest)
        pT = e * (1.0 / jnp.sum(e, axis=0, keepdims=True))
        pT_low = pT.astype(BF16)
        dpT = dot(v_s[upto, :], gT)
        balance = jnp.sum(dpT * pT, axis=0, keepdims=True)
        dsT = (pT * (dpT - balance)).astype(BF16)
        oT_s[:, at] = dot(vT_s[:, upto], pT_low)
        dqT_s[:, at] = dot(kT_s[:, upto], dsT) * scale
        dkT_s[:, upto] += dot_nt(qT, dsT)
        dvT_s[:, upto] += dot_nt(gT, pT_low)
    for i in range(rows // tile):
        at = pl.ds(i * tile, tile)
        c, s = cosT_s[:, at], -sinT_s[:, at]
        full = jnp.concatenate(
            [spin(dqT_s[:, at], c, s), spin(dkT_s[:, at], c, s), dvT_s[:, at], oT_s[:, at]], axis=0)
        out_s[at, :] = full.T.astype(BF16)
    for j in range(slots):
        p = order_ref[j]
        for h in range(2):
            dst = pl.ds(j * 2 * half + h * half, half)
            src = pl.ds(pl.multiple_of((p if h == 0 else last - p) * half, half), half)
            out_ref[dst, :] = out_s[src, :]


def attention(order, joint, table, grad):
    rows, hd = joint.shape[0], joint.shape[1] // 4
    vmem = pl.BlockSpec(memory_space=pltpu.VMEM)
    return pl.pallas_call(
        attention_kernel,
        out_shape=jax.ShapeDtypeStruct((rows, 4 * hd), BF16),
        in_specs=[pl.BlockSpec(memory_space=pltpu.SMEM), vmem, vmem, vmem],
        out_specs=vmem,
        scratch_shapes=[
            pltpu.VMEM((rows, 4 * hd), F32),
            pltpu.VMEM((rows, 16), F32),
            pltpu.VMEM((rows, hd), F32),
            pltpu.VMEM((rows, hd), BF16),
            pltpu.VMEM((rows, hd), BF16),
            pltpu.VMEM((hd, rows), BF16),
            pltpu.VMEM((hd, rows), BF16),
            pltpu.VMEM((hd, rows), BF16),
            pltpu.VMEM((hd, rows), BF16),
            pltpu.VMEM((hd, rows), F32),
            pltpu.VMEM((hd, rows), F32),
            pltpu.VMEM((hd, rows), F32),
            pltpu.VMEM((hd, rows), F32),
            pltpu.VMEM((8, rows), F32),
            pltpu.VMEM((8, rows), F32),
            pltpu.VMEM((rows, 4 * hd), BF16),
        ],
        compiler_params=pltpu.CompilerParams(vmem_limit_bytes=48 * 1024 * 1024),
        cost_estimate=pl.CostEstimate(flops=7 * rows * rows * hd, bytes_accessed=8 << 20, transcendentals=rows * rows // 2),
    )(order, joint, table, grad)


def shards(
    tokens, upstream, block_pairs, rotary_place,
    first_gain, first_shift, joint_weight, joint_bias, dense_weight, dense_bias,
    second_gain, second_shift, widen_weight, widen_bias, narrow_weight, narrow_bias,
):
    own_rows, width = tokens.shape[1], tokens.shape[2]
    hd = width // HEADS
    ff = widen_weight.shape[1]
    ffc = ff // N_CTX
    rows = own_rows * N_CTX
    c = lax.axis_index("ctx")
    f = lax.axis_index("fsdp")
    own_tokens, own_up = tokens[0], upstream[0]
    d_own = width // N_FSDP

    place = rotary_place[0]
    extra = jnp.concatenate([place // 64, place % 64]).astype(BF16)
    extra = jnp.pad(extra[None, :], ((0, 15), (0, width - 2 * own_rows)))
    both = lax.all_gather(jnp.concatenate([own_tokens, own_up, extra], axis=0), "ctx", axis=0)

    joint_part = lax.dynamic_index_in_dim(joint_weight.reshape(d_own, 3, HEADS, hd), c, 2, keepdims=False)
    vectors = jnp.concatenate(
        [v[:, None] for v in (first_gain, first_shift, second_gain, second_shift, dense_bias, narrow_bias)]
        + [joint_bias.reshape(d_own, 3), widen_bias.reshape(d_own, 4), jnp.zeros((d_own, 51), BF16)], axis=1)
    widen_part = lax.dynamic_slice_in_dim(widen_weight, c * ffc, ffc, axis=1)
    part = jnp.concatenate([joint_part.reshape(d_own, 3 * hd), vectors, widen_part], axis=1)
    slices = lax.all_to_all(jnp.broadcast_to(part[None], (N_FSDP,) + part.shape), "fsdp", 0, 0, tiled=True)
    slices = slices.reshape(width, part.shape[1])
    odd = c % 2
    back_w = turn(jnp.concatenate([
        lax.dynamic_slice_in_dim(dense_weight, odd * hd, hd, axis=0),
        lax.dynamic_slice_in_dim(narrow_weight, odd * ffc, ffc, axis=0)], axis=0))
    dense_w, narrow_w = back_w[:hd], back_w[hd:]

    coded = both[:, 2 * own_rows, :2 * own_rows].astype(F32)
    place_all = (coded[:, :own_rows] * 64.0 + coded[:, own_rows:]).reshape(rows)
    steps = jnp.arange(8, dtype=F32)
    angles = place_all[:, None] * (ROTARY_BASE ** (-2.0 * steps / 16))
    table = jnp.concatenate([jnp.cos(angles), jnp.sin(angles)], axis=1)
    order = block_pairs[0]

    wj = slices[:, :4 * hd].astype(F32)
    ww = slices[:, 4 * hd:].astype(F32)
    vec = slices[:, 3 * hd:4 * hd].astype(F32)
    g1, s1, g2, s2 = vec[:, 0:1], vec[:, 1:2], vec[:, 2:3], vec[:, 3:4]
    dense_b, narrow_b = vec[:, 4], vec[:, 5]
    jb_full = vec[:, 6:9].reshape(3, HEADS, hd)
    wb_full = vec[:, 9:13].reshape(ff)
    jb_own = lax.dynamic_index_in_dim(jb_full, c, 1, keepdims=False).reshape(3 * hd)
    wb_own = lax.dynamic_slice_in_dim(wb_full, c * ffc, ffc)
    wj = jnp.where(jnp.arange(4 * hd)[None, :] < 3 * hd, wj, 0.0)
    wj_g = (g1 * wj).astype(BF16)
    ww_g = (g2 * ww).astype(BF16)
    shifted = jnp.concatenate([
        jnp.sum(s1 * wj, axis=0) + jnp.pad(jb_own, (0, hd)), jnp.sum(s2 * ww, axis=0) + wb_own])[None, :]
    dense_p = jnp.pad(dense_w, ((3 * hd, 0), (0, 0)))

    xhat, joint, att_grad, act, wg = project(both, wj_g, ww_g, shifted, back_w)

    mixed = attention(order, joint, table, att_grad)

    mine, other = spread((c % 2)[None], mixed, wg, act, wj_g, ww_g, dense_p, narrow_w)
    chip = (mine.astype(F32) + lax.ppermute(other, "ctx", OTHER_CORE).astype(F32)).astype(BF16)
    summed = lax.all_to_all(chip, "ctx", 0, 0, tiled=True, axis_index_groups=SAME_CORE)
    summed = jnp.sum(summed.astype(F32), axis=0)
    u_own, out_own = summed[:, :width], summed[:, width:]

    parts = lax.all_to_all(grads(xhat, both, mixed, act, wg), "fsdp", 0, 0, tiled=True)
    parts = jnp.sum(parts.astype(F32), axis=0)
    bias_grad = parts[d_own, 4 * hd + ffc:4 * hd + ffc + d_own]
    low = parts.astype(BF16)
    turned = turn(jnp.concatenate([low[:, 3 * hd:4 * hd], low[:, 4 * hd + ffc:]], axis=1))
    grads_all = lax.all_gather(jnp.concatenate([
        low[:, :3 * hd], turned[:, :hd], low[:, 4 * hd:4 * hd + ffc], turned[:, hd:]], axis=1), "ctx", axis=0)

    own_x = own_tokens.astype(F32)
    block_out = (own_x + out_own + dense_b + narrow_b).astype(BF16)
    own_center = own_x - jnp.mean(own_x, axis=-1, keepdims=True)
    own_rstd = lax.rsqrt(jnp.mean(own_center * own_center, axis=-1, keepdims=True) + EPSILON)
    own_xhat = own_center * own_rstd
    tokens_grad = own_up.astype(F32) + own_rstd * (
        u_own - jnp.mean(u_own, axis=-1, keepdims=True)
        - own_xhat * jnp.mean(u_own * own_xhat, axis=-1, keepdims=True))

    late_all = grads_all[:, :, :4 * hd].astype(F32)
    early_all = grads_all[:, :, 4 * hd:].astype(F32)
    m_w = jnp.transpose(early_all[:, :d_own, :ffc], (1, 0, 2)).reshape(d_own, ff)
    wb_grad = early_all[:, d_own, :ffc].reshape(ff)
    widen_grad = second_gain.astype(F32)[:, None] * m_w + second_shift.astype(F32)[:, None] * wb_grad[None, :]
    widen_f = widen_weight.astype(F32)
    g2_grad = jnp.sum(widen_f * m_w, axis=1)
    s2_grad = jnp.sum(widen_f * wb_grad[None, :], axis=1)
    narrow_grad = jnp.transpose(
        early_all[:, :d_own, ffc:].reshape(N_FSDP, 2, d_own, ffc), (1, 3, 0, 2)).reshape(2 * ffc, width)
    m_j = jnp.transpose(late_all[:, :d_own, :3 * hd].reshape(N_CTX, d_own, 3, hd), (1, 2, 0, 3)).reshape(d_own, 3 * width)
    jb_grad = jnp.transpose(late_all[:, d_own, :3 * hd].reshape(N_CTX, 3, hd), (1, 0, 2)).reshape(3 * width)
    joint_grad = first_gain.astype(F32)[:, None] * m_j + first_shift.astype(F32)[:, None] * jb_grad[None, :]
    joint_f = joint_weight.astype(F32)
    g1_grad = jnp.sum(joint_f * m_j, axis=1)
    s1_grad = jnp.sum(joint_f * jb_grad[None, :], axis=1)
    dense_grad = jnp.transpose(
        late_all[:, :d_own, 3 * hd:].reshape(N_FSDP, 2, d_own, hd), (1, 3, 0, 2)).reshape(2 * hd, width)
    jb_shard = lax.dynamic_slice_in_dim(jb_grad, f * (3 * d_own), 3 * d_own)
    wb_shard = lax.dynamic_slice_in_dim(wb_grad, f * (ff // N_FSDP), ff // N_FSDP)
    return (
        block_out[None], tokens_grad[None], g1_grad, s1_grad, joint_grad, jb_shard,
        dense_grad, bias_grad, g2_grad, s2_grad, widen_grad, wb_shard, narrow_grad, bias_grad,
    )


def solution(mesh):
    rows = P("fsdp", "ctx", None)
    vec, mat = P("fsdp"), P("fsdp", None)
    in_specs = (rows, rows, mat, P("fsdp", "ctx"), vec, vec, mat, vec, mat, vec, vec, vec, mat, vec, mat, vec)
    out_specs = (rows, rows, vec, vec, mat, vec, mat, vec, vec, vec, mat, vec, mat, vec)
    return jax.shard_map(shards, mesh=mesh, in_specs=in_specs, out_specs=out_specs, check_vma=False)
```

```python
import jax
import jax.numpy as jnp
from jax import lax
from jax.experimental import pallas as pl
from jax.experimental.pallas import tpu as pltpu
from jax.sharding import PartitionSpec as P

HEADS = 16
EPSILON = 1e-05
NEGATIVE = -1e30
ROTARY_BASE = 10000.0
N_CTX = 16
N_FSDP = 8
F32 = jnp.float32
BF16 = jnp.bfloat16

UP_Z = [((i + 4) % 16, i) for i in range(16)]
DOWN_Z = [((i + 12) % 16, i) for i in range(16)]
ACROSS_Y = [(i ^ 2, i) for i in range(16)]
OTHER_CORE = [(i ^ 1, i) for i in range(16)]
SAME_CORE = [list(range(0, 16, 2)), list(range(1, 16, 2))]
CHIPS = [(0, 0), (1, 0), (3, 0), (0, 1), (2, 0), (3, 1), (1, 1), (2, 1)]
TURN = [(c * 8 + f, (2 * f + (c & 1)) * 8 + (c >> 1)) for c in range(16) for f in range(8)]


def move(v, way):
    return lax.ppermute(v, "ctx", way)


def turn(v):
    return lax.ppermute(v, ("ctx", "fsdp"), TURN)


def gather_chips(own):
    mine = lax.all_to_all(jnp.broadcast_to(own[None], (N_CTX // 2,) + own.shape), "ctx", 0, 0, tiled=True,
                          axis_index_groups=SAME_CORE)
    return mine, move(mine, OTHER_CORE)


def dot_tn(a, b):
    return lax.dot_general(a, b, (((0,), (0,)), ((), ())), preferred_element_type=F32)


def dot_nt(a, b):
    return lax.dot_general(a, b, (((1,), (1,)), ((), ())), preferred_element_type=F32)


def dot_nn(a, b):
    return jnp.dot(a, b, preferred_element_type=F32)


def project_kernel(x_ref, up_ref, wj_ref, ww_ref, add_ref, back_ref, *refs):
    xhat_ref, joint_ref, grad_ref, act_ref, wg_ref, keep_ref = refs[-6:]
    x = x_ref[0].astype(F32)
    center = x - jnp.mean(x, axis=-1, keepdims=True)
    xhat = (center * lax.rsqrt(jnp.mean(center * center, axis=-1, keepdims=True) + EPSILON)).astype(BF16)
    xhat_ref[...] = xhat
    wide = wj_ref.shape[1]
    joint_ref[...] = dot_nn(xhat, wj_ref[...]) + add_ref[0:1, :wide]
    widened = dot_nn(xhat, ww_ref[...]) + add_ref[0:1, wide:]
    phi = 0.5 * (1.0 + lax.erf(widened * (0.5 ** 0.5)))
    act_ref[...] = (widened * phi).astype(BF16)
    slope = phi + widened * jnp.exp(-0.5 * widened * widened) * 0.3989422804014327
    up = up_ref[0]
    keep_ref[...] = up
    hd = back_ref.shape[0] - ww_ref.shape[1]
    grad_ref[...] = dot_nt(up, back_ref[0:hd, :])
    wg_ref[...] = (dot_nt(up, back_ref[hd:, :]) * slope).astype(BF16)


def project(group, first, wj, ww, add, back, done):
    slots, _, width = group.shape
    own = 128
    rows = N_CTX * own
    wide, ffc = wj.shape[1], ww.shape[1]
    hd = back.shape[0] - ffc
    whole = lambda a: pl.BlockSpec(a.shape, lambda i: (0, 0))
    tall = lambda n: pl.BlockSpec((own, n), lambda i: (first + i, 0))
    shapes = [(width, BF16), (wide, F32), (hd, F32), (ffc, BF16), (ffc, BF16), (width, BF16)]
    done = done or ()
    return pl.pallas_call(
        project_kernel,
        grid=(slots,),
        in_specs=[
            pl.BlockSpec((1, own, width), lambda i: (i, 0, 0)),
            pl.BlockSpec((1, own, width), lambda i: (i, 1, 0)),
            whole(wj), whole(ww), whole(add), whole(back)] + [pl.BlockSpec(memory_space=pl.ANY)] * len(done),
        out_specs=[tall(n) for n, _ in shapes],
        out_shape=[jax.ShapeDtypeStruct((rows, n), t) for n, t in shapes],
        input_output_aliases={6 + i: i for i in range(len(done))},
        compiler_params=pltpu.CompilerParams(vmem_limit_bytes=40 * 1024 * 1024),
        cost_estimate=pl.CostEstimate(flops=2 * slots * own * width * 832, bytes_accessed=slots << 20,
                                      transcendentals=slots * own * 512),
    )(group, group, wj, ww, add, back, *done)


def early_kernel(xhat_ref, up_ref, act_ref, wg_ref, out_ref):
    rows, n = xhat_ref.shape
    k = act_ref.shape[1]
    xhat, up, act, wg = xhat_ref[...], up_ref[...], act_ref[...], wg_ref[...]
    out_ref[0, 0:n, 0:k] = dot_tn(xhat, wg).astype(BF16)
    out_ref[0, 0:n, k:] = dot_tn(up, act).astype(BF16)
    ones = jnp.ones((16, rows), BF16)
    out_ref[0, n:, 0:k] = dot_nn(ones, wg).astype(BF16)
    out_ref[0, n:, k:k + n] = dot_nn(ones, up).astype(BF16)
    out_ref[0, n:, k + n:] = jnp.zeros((16, k - n), BF16)


def late_kernel(xhat_ref, up_ref, mixed_ref, out_ref):
    rows, n = xhat_ref.shape
    m = mixed_ref.shape[1]
    mixed = mixed_ref[...]
    lane = lax.broadcasted_iota(jnp.int32, (n, m), 1)
    out_ref[0, 0:n, :] = jnp.where(
        lane < 3 * (m // 4), dot_tn(xhat_ref[...], mixed), dot_tn(up_ref[...], mixed)).astype(BF16)
    out_ref[0, n:, :] = dot_nn(jnp.ones((16, rows), BF16), mixed).astype(BF16)


def grads(kernel, xhat, up, hidden, total):
    rows, width = xhat.shape
    n = width // N_FSDP
    return pl.pallas_call(
        kernel,
        grid=(N_FSDP,),
        in_specs=[pl.BlockSpec((rows, n), lambda i: (0, i))] * 2
        + [pl.BlockSpec(h.shape, lambda i: (0, 0)) for h in hidden],
        out_specs=pl.BlockSpec((1, n + 16, total), lambda i: (i, 0, 0)),
        out_shape=jax.ShapeDtypeStruct((N_FSDP, n + 16, total), BF16),
        compiler_params=pltpu.CompilerParams(vmem_limit_bytes=40 * 1024 * 1024),
        cost_estimate=pl.CostEstimate(flops=2 * rows * width * total, bytes_accessed=10 << 20, transcendentals=0),
    )(xhat, up, *hidden)


def spread_kernel(chip_ref, mixed_ref, wg_ref, act_ref, wj_ref, ww_ref, dense_ref, narrow_ref, mine_ref, other_ref):
    width = wj_ref.shape[0]
    half = mine_ref.shape[1]
    both = lambda ref: ref[...].reshape(2 * half, ref.shape[2])
    mixed = both(mixed_ref)
    u = (dot_nt(mixed, wj_ref[...]) + dot_nt(both(wg_ref), ww_ref[...])).astype(BF16)
    out = (dot_nn(mixed, dense_ref[...]) + dot_nn(both(act_ref), narrow_ref[...])).astype(BF16)
    for ref, at in ((mine_ref, 0), (other_ref, half)):
        ref[0, :, :width] = u[at:at + half]
        ref[0, :, width:] = out[at:at + half]


def spread(chip, mixed, wg, act, wj, ww, dense, narrow):
    rows, width = mixed.shape[0], wj.shape[0]
    own = rows // N_CTX
    whole = lambda a: pl.BlockSpec(a.shape, lambda i, chip: (0, 0))
    split = lambda a: a.reshape(2, rows // 2, a.shape[1])
    tall = lambda a: pl.BlockSpec((2, own, a.shape[1]), lambda i, chip: (0, i, 0))
    shape = jax.ShapeDtypeStruct((N_CTX // 2, own, 2 * width), BF16)
    return pl.pallas_call(
        spread_kernel,
        grid_spec=pltpu.PrefetchScalarGridSpec(
            num_scalar_prefetch=1,
            grid=(N_CTX // 2,),
            in_specs=[tall(mixed), tall(wg), tall(act), whole(wj), whole(ww), whole(dense), whole(narrow)],
            out_specs=[pl.BlockSpec((1, own, 2 * width), lambda i, chip: (chip[i], 0, 0))] * 2),
        out_shape=[shape, shape],
        compiler_params=pltpu.CompilerParams(vmem_limit_bytes=40 * 1024 * 1024),
        cost_estimate=pl.CostEstimate(flops=2 * rows * width * 1024, bytes_accessed=14 << 20, transcendentals=0),
    )(chip, split(mixed), split(wg), split(act), wj, ww, dense, narrow)


def finish_early_kernel(core_ref, mine_ref, other_ref, weight_ref, gain_ref, shift_ref,
                        widen_ref, narrow_ref, gain_out, shift_out, bias_out):
    n = weight_ref.shape[0]
    k = mine_ref.shape[2] // 2
    even = core_ref[0] == 0
    gain, shift = gain_ref[...], shift_ref[...]
    g_sum = jnp.zeros((n, k), F32)
    s_sum = jnp.zeros((n, k), F32)
    for q in range(mine_ref.shape[0]):
        for b in range(2):
            part = jnp.where(even == (b == 0), mine_ref[q], other_ref[q]).astype(F32)
            at = (2 * q + b) * k
            m, bias = part[:n, :k], part[n:n + 1, :k]
            w = weight_ref[:, at:at + k].astype(F32)
            widen_ref[:, at:at + k] = gain * m + shift * bias
            g_sum += w * m
            s_sum += w * bias
            bias_out[:, at:at + k] = part[n:n + 8, :k]
            narrow_ref[b * k:(b + 1) * k, q * n:(q + 1) * n] = part[:n, k:].T
    gain_out[...] = jnp.sum(g_sum, axis=1, keepdims=True)
    shift_out[...] = jnp.sum(s_sum, axis=1, keepdims=True)


def finish_late_kernel(core_ref, mine_ref, other_ref, weight_ref, gain_ref, shift_ref,
                       joint_ref, dense_ref, gain_out, shift_out, bias_out):
    n = weight_ref.shape[0]
    hd = mine_ref.shape[2] // 4
    width = weight_ref.shape[1] // 3
    even = core_ref[0] == 0
    gain, shift = gain_ref[...], shift_ref[...]
    g_sum = jnp.zeros((n, 2 * hd), F32)
    s_sum = jnp.zeros((n, 2 * hd), F32)
    for q in range(mine_ref.shape[0]):
        mine, other = mine_ref[q].astype(F32), other_ref[q].astype(F32)
        pair = [jnp.where(even, mine, other), jnp.where(even, other, mine)]
        for k in range(3):
            full = jnp.concatenate([p[:, k * hd:(k + 1) * hd] for p in pair], axis=1)
            at = k * width + q * 2 * hd
            m, bias = full[:n], full[n:n + 1]
            w = weight_ref[:, at:at + 2 * hd].astype(F32)
            joint_ref[:, at:at + 2 * hd] = gain * m + shift * bias
            g_sum += w * m
            s_sum += w * bias
            bias_out[:, at:at + 2 * hd] = full[n:n + 8]
        for b in range(2):
            dense_ref[b * hd:(b + 1) * hd, q * n:(q + 1) * n] = pair[b][:n].T[3 * hd:]
    gain_out[...] = jnp.sum(g_sum, axis=1, keepdims=True)
    shift_out[...] = jnp.sum(s_sum, axis=1, keepdims=True)


def finish(kernel, core, mine, other, weight, gain, shift, side):
    n = weight.shape[0]
    vmem = pl.BlockSpec(memory_space=pltpu.VMEM)
    column = jax.ShapeDtypeStruct((n, 1), F32)
    wide = lambda v: v.astype(F32)[:, None]
    return pl.pallas_call(
        kernel,
        in_specs=[pl.BlockSpec(memory_space=pltpu.SMEM)] + [vmem] * 5,
        out_specs=[vmem] * 5,
        out_shape=[jax.ShapeDtypeStruct(weight.shape, F32), jax.ShapeDtypeStruct(side, F32), column, column,
                   jax.ShapeDtypeStruct((8, weight.shape[1]), F32)],
        compiler_params=pltpu.CompilerParams(vmem_limit_bytes=40 * 1024 * 1024),
        cost_estimate=pl.CostEstimate(flops=8 * weight.size, bytes_accessed=12 * weight.size, transcendentals=0),
    )(core, mine, other, weight, wide(gain), wide(shift))


def attention_kernel(order_ref, joint_ref, table_ref, grad_ref, out_ref,
                     joint_s, table_s, grad_s, k_s, v_s, qT_s, kT_s, vT_s, gT_s,
                     oT_s, dqT_s, dkT_s, dvT_s, cosT_s, sinT_s, out_s):
    rows, hd = joint_ref.shape[0], joint_ref.shape[1] // 4
    slots, half, tile = N_CTX, rows // (2 * N_CTX), 256
    last = 2 * slots - 1
    for j in range(slots):
        p = order_ref[j]
        for h in range(2):
            src = pl.ds(j * 2 * half + h * half, half)
            dst = pl.ds(pl.multiple_of((p if h == 0 else last - p) * half, half), half)
            joint_s[dst, :] = joint_ref[src, :]
            table_s[dst, :] = table_ref[src, :]
            grad_s[dst, :] = grad_ref[src, :]
    scale = hd ** -0.5

    def spin(t, c, s):
        return jnp.concatenate([t[0:8] * c - t[8:16] * s, t[8:16] * c + t[0:8] * s, t[16:]], axis=0)

    for i in range(rows // tile):
        at = pl.ds(i * tile, tile)
        jT = joint_s[at, :].T
        tT = table_s[at, :].T
        c, s = tT[0:8], tT[8:16]
        cosT_s[:, at] = c
        sinT_s[:, at] = s
        qT = spin(jT[0:hd], c, s).astype(BF16)
        kT = spin(jT[hd:2 * hd], c, s).astype(BF16)
        vT = jT[2 * hd:3 * hd].astype(BF16)
        qT_s[:, at] = (qT.astype(F32) * scale).astype(BF16)
        kT_s[:, at] = kT
        vT_s[:, at] = vT
        k_s[at, :] = kT.astype(F32).T.astype(BF16)
        v_s[at, :] = vT.astype(F32).T.astype(BF16)
        gT_s[:, at] = grad_s[at, :].T.astype(BF16)
    dkT_s[...] = jnp.zeros_like(dkT_s)
    dvT_s[...] = jnp.zeros_like(dvT_s)
    key_at = lax.broadcasted_iota(jnp.int32, (tile, tile), 0)
    query_at = lax.broadcasted_iota(jnp.int32, (tile, tile), 1)
    seen = key_at <= query_at
    dot = lambda a, b: jnp.dot(a, b, preferred_element_type=F32)
    dot_nt = lambda a, b: lax.dot_general(a, b, (((1,), (1,)), ((), ())), preferred_element_type=F32)
    for i in range(rows // tile):
        at = pl.ds(i * tile, tile)
        span = (i + 1) * tile
        upto = pl.ds(0, span)
        qT, gT = qT_s[:, at], gT_s[:, at]
        sT = dot(k_s[upto, :], qT)
        edge = jnp.where(seen, sT[i * tile:], NEGATIVE)
        sT = edge if i == 0 else jnp.concatenate([sT[:i * tile], edge], axis=0)
        largest = jnp.max(sT, axis=0, keepdims=True)
        e = jnp.exp(sT - largest)
        pT = e * (1.0 / jnp.sum(e, axis=0, keepdims=True))
        pT_low = pT.astype(BF16)
        dpT = dot(v_s[upto, :], gT)
        balance = jnp.sum(dpT * pT, axis=0, keepdims=True)
        dsT = (pT * (dpT - balance)).astype(BF16)
        oT_s[:, at] = dot(vT_s[:, upto], pT_low)
        dqT_s[:, at] = dot(kT_s[:, upto], dsT) * scale
        dkT_s[:, upto] += dot_nt(qT, dsT)
        dvT_s[:, upto] += dot_nt(gT, pT_low)
    for i in range(rows // tile):
        at = pl.ds(i * tile, tile)
        c, s = cosT_s[:, at], -sinT_s[:, at]
        full = jnp.concatenate(
            [spin(dqT_s[:, at], c, s), spin(dkT_s[:, at], c, s), dvT_s[:, at], oT_s[:, at]], axis=0)
        out_s[at, :] = full.T.astype(BF16)
    for j in range(slots):
        p = order_ref[j]
        for h in range(2):
            dst = pl.ds(j * 2 * half + h * half, half)
            src = pl.ds(pl.multiple_of((p if h == 0 else last - p) * half, half), half)
            out_ref[dst, :] = out_s[src, :]


def attention(order, joint, table, grad):
    rows, hd = joint.shape[0], joint.shape[1] // 4
    vmem = pl.BlockSpec(memory_space=pltpu.VMEM)
    return pl.pallas_call(
        attention_kernel,
        out_shape=jax.ShapeDtypeStruct((rows, 4 * hd), BF16),
        in_specs=[pl.BlockSpec(memory_space=pltpu.SMEM), vmem, vmem, vmem],
        out_specs=vmem,
        scratch_shapes=[
            pltpu.VMEM((rows, 4 * hd), F32),
            pltpu.VMEM((rows, 16), F32),
            pltpu.VMEM((rows, hd), F32),
            pltpu.VMEM((rows, hd), BF16),
            pltpu.VMEM((rows, hd), BF16),
            pltpu.VMEM((hd, rows), BF16),
            pltpu.VMEM((hd, rows), BF16),
            pltpu.VMEM((hd, rows), BF16),
            pltpu.VMEM((hd, rows), BF16),
            pltpu.VMEM((hd, rows), F32),
            pltpu.VMEM((hd, rows), F32),
            pltpu.VMEM((hd, rows), F32),
            pltpu.VMEM((hd, rows), F32),
            pltpu.VMEM((8, rows), F32),
            pltpu.VMEM((8, rows), F32),
            pltpu.VMEM((rows, 4 * hd), BF16),
        ],
        compiler_params=pltpu.CompilerParams(vmem_limit_bytes=48 * 1024 * 1024),
        cost_estimate=pl.CostEstimate(flops=7 * rows * rows * hd, bytes_accessed=8 << 20, transcendentals=rows * rows // 2),
    )(order, joint, table, grad)


def shards(
    tokens, upstream, block_pairs, rotary_place,
    first_gain, first_shift, joint_weight, joint_bias, dense_weight, dense_bias,
    second_gain, second_shift, widen_weight, widen_bias, narrow_weight, narrow_bias,
):
    own_rows, width = tokens.shape[1], tokens.shape[2]
    hd = width // HEADS
    ff = widen_weight.shape[1]
    ffc = ff // N_CTX
    rows = own_rows * N_CTX
    c = lax.axis_index("ctx")
    f = lax.axis_index("fsdp")
    own_tokens, own_up = tokens[0], upstream[0]
    d_own = width // N_FSDP

    joint_part = lax.dynamic_index_in_dim(joint_weight.reshape(d_own, 3, HEADS, hd), c, 2, keepdims=False)
    vectors = jnp.concatenate(
        [v[:, None] for v in (first_gain, first_shift, second_gain, second_shift, dense_bias, narrow_bias)]
        + [joint_bias.reshape(d_own, 3), widen_bias.reshape(d_own, 4), jnp.zeros((d_own, 51), BF16)], axis=1)
    widen_part = lax.dynamic_slice_in_dim(widen_weight, c * ffc, ffc, axis=1)
    part = jnp.concatenate([joint_part.reshape(d_own, 3 * hd), vectors, widen_part], axis=1)
    slices = lax.all_to_all(jnp.broadcast_to(part[None], (N_FSDP,) + part.shape), "fsdp", 0, 0, tiled=True)
    odd = c % 2
    back_w = turn(jnp.concatenate([
        lax.dynamic_slice_in_dim(dense_weight, odd * hd, hd, axis=0),
        lax.dynamic_slice_in_dim(narrow_weight, odd * ffc, ffc, axis=0)], axis=0))

    place = rotary_place[0]
    extra = jnp.concatenate([place // 64, place % 64]).astype(BF16)
    extra = jnp.pad(extra[None, :], ((0, 15), (0, width - 2 * own_rows)))
    own = jnp.concatenate([own_tokens, own_up, extra], axis=0)
    b10, b30, b01 = move(own, UP_Z), move(own, DOWN_Z), move(own, ACROSS_Y)
    e0 = move(own, OTHER_CORE)
    b10, b30, b01, slices = lax.optimization_barrier((b10, b30, b01, slices))
    slices = slices.reshape(width, part.shape[1])
    m1 = jnp.stack([b10, b30, b01])
    b20, b31, b11 = move(b10, UP_Z), move(b01, DOWN_Z), move(b10, ACROSS_Y)
    e1 = move(m1, OTHER_CORE)
    b20, b31, b11, back_w = lax.optimization_barrier((b20, b31, b11, back_w))
    dense_w, narrow_w = back_w[:hd], back_w[hd:]
    m2 = jnp.stack([b20, b31, b11])
    m3 = jnp.concatenate(
        [move(b20[:96], ACROSS_Y), move(b11[96:192], UP_Z), move(b31[192:], DOWN_Z)], axis=0)[None]
    e2 = move(m2, OTHER_CORE)
    e3 = move(m3, OTHER_CORE)

    groups = [own[None], m1, m2, m3, e0[None], e1, e2, e3]
    coded = jnp.concatenate([g[:, 2 * own_rows, :2 * own_rows] for g in groups], axis=0).astype(F32)
    place_all = (coded[:, :own_rows] * 64.0 + coded[:, own_rows:]).reshape(rows)
    steps = jnp.arange(8, dtype=F32)
    angles = place_all[:, None] * (ROTARY_BASE ** (-2.0 * steps / 16))
    table = jnp.concatenate([jnp.cos(angles), jnp.sin(angles)], axis=1)
    chip = jnp.stack([((c // 4 + dz) % 4) * 2 + ((c // 2) % 2 + dy) % 2 for dz, dy in CHIPS]).astype(jnp.int32)
    source = jnp.concatenate([2 * chip + c % 2, 2 * chip + 1 - c % 2])
    slot = jnp.arange(N_CTX)
    order = jnp.sum((source[:, None] == slot[None, :]) * block_pairs[0][None, :], axis=1).astype(jnp.int32)

    wj = slices[:, :4 * hd].astype(F32)
    ww = slices[:, 4 * hd:].astype(F32)
    vec = slices[:, 3 * hd:4 * hd].astype(F32)
    g1, s1, g2, s2 = vec[:, 0:1], vec[:, 1:2], vec[:, 2:3], vec[:, 3:4]
    dense_b, narrow_b = vec[:, 4], vec[:, 5]
    jb_full = vec[:, 6:9].reshape(3, HEADS, hd)
    wb_full = vec[:, 9:13].reshape(ff)
    jb_own = lax.dynamic_index_in_dim(jb_full, c, 1, keepdims=False).reshape(3 * hd)
    wb_own = lax.dynamic_slice_in_dim(wb_full, c * ffc, ffc)
    wj = jnp.where(jnp.arange(4 * hd)[None, :] < 3 * hd, wj, 0.0)
    wj_g = (g1 * wj).astype(BF16)
    ww_g = (g2 * ww).astype(BF16)
    shifted = jnp.concatenate([
        jnp.sum(s1 * wj, axis=0) + jnp.pad(jb_own, (0, hd)), jnp.sum(s2 * ww, axis=0) + wb_own])[None, :]
    dense_p = jnp.pad(dense_w, ((3 * hd, 0), (0, 0)))

    done = None
    for first, group in ((0, groups[0]), (8, groups[4]), (1, groups[1]), (9, groups[5]),
                         (4, groups[2]), (12, groups[6]), (7, groups[3]), (15, groups[7])):
        done = project(group, first, wj_g, ww_g, shifted, back_w, done)
    xhat, joint, att_grad, act, wg, up_all = done

    def to_owners(parts):
        parts = jnp.sum(lax.all_to_all(parts, "fsdp", 0, 0, tiled=True).astype(F32), axis=0)
        return parts, parts.astype(BF16)

    early = grads(early_kernel, xhat, up_all, (act, wg), 2 * ffc)
    early, joint = lax.optimization_barrier((early, joint))
    early, low = to_owners(early)
    bias_grad = early[d_own, ffc:ffc + d_own]
    early = jnp.concatenate([low[:, :ffc], turn(low[:, ffc:])], axis=1)

    mixed = attention(order, joint, table, att_grad)

    mine, other = spread(chip, mixed, wg, act, wj_g, ww_g, dense_p, narrow_w)
    pair = (mine.astype(F32) + move(other, OTHER_CORE).astype(F32)).astype(BF16)
    summed = lax.all_to_all(pair, "ctx", 0, 0, tiled=True, axis_index_groups=SAME_CORE)
    summed = jnp.sum(summed.astype(F32), axis=0)
    u_own, out_own = summed[:, :width], summed[:, width:]

    late, low = to_owners(grads(late_kernel, xhat, up_all, (mixed,), 4 * hd))
    late = jnp.concatenate([low[:, :3 * hd], turn(low[:, 3 * hd:])], axis=1)

    own_x = own_tokens.astype(F32)
    block_out = (own_x + out_own + dense_b + narrow_b).astype(BF16)
    own_center = own_x - jnp.mean(own_x, axis=-1, keepdims=True)
    own_rstd = lax.rsqrt(jnp.mean(own_center * own_center, axis=-1, keepdims=True) + EPSILON)
    own_xhat = own_center * own_rstd
    tokens_grad = own_up.astype(F32) + own_rstd * (
        u_own - jnp.mean(u_own, axis=-1, keepdims=True)
        - own_xhat * jnp.mean(u_own * own_xhat, axis=-1, keepdims=True))

    core = (c % 2)[None]
    widen_grad, narrow_grad, g2_grad, s2_grad, wb_grad = finish(
        finish_early_kernel, core, *gather_chips(early), widen_weight, second_gain, second_shift, (2 * ffc, width))
    joint_grad, dense_grad, g1_grad, s1_grad, jb_grad = finish(
        finish_late_kernel, core, *gather_chips(late), joint_weight, first_gain, first_shift, (2 * hd, width))
    jb_shard = lax.dynamic_slice_in_dim(jb_grad[0], f * (3 * d_own), 3 * d_own)
    wb_shard = lax.dynamic_slice_in_dim(wb_grad[0], f * (ff // N_FSDP), ff // N_FSDP)
    return (
        block_out[None], tokens_grad[None], g1_grad[:, 0], s1_grad[:, 0], joint_grad, jb_shard,
        dense_grad, bias_grad, g2_grad[:, 0], s2_grad[:, 0], widen_grad, wb_shard, narrow_grad, bias_grad,
    )


def solution(mesh):
    rows = P("fsdp", "ctx", None)
    vec, mat = P("fsdp"), P("fsdp", None)
    in_specs = (rows, rows, mat, P("fsdp", "ctx"), vec, vec, mat, vec, mat, vec, vec, vec, mat, vec, mat, vec)
    out_specs = (rows, rows, vec, vec, mat, vec, mat, vec, vec, vec, mat, vec, mat, vec)
    return jax.shard_map(shards, mesh=mesh, in_specs=in_specs, out_specs=out_specs, check_vma=False)
```

```python
import jax
import jax.numpy as jnp
from jax import lax
from jax.experimental import pallas as pl
from jax.experimental.pallas import tpu as pltpu
from jax.sharding import PartitionSpec as P

HEADS = 16
EPSILON = 1e-05
NEGATIVE = -1e30
ROTARY_BASE = 10000.0
N_CTX = 16
VMEM = 60 * 1024 * 1024
N_FSDP = 8
F32 = jnp.float32
BF16 = jnp.bfloat16

OTHER_CORE = [(i ^ 1, i) for i in range(16)]
SAME_CORE = [list(range(0, 16, 2)), list(range(1, 16, 2))]
TURN = [(c * 8 + f, (2 * f + (c & 1)) * 8 + (c >> 1)) for c in range(16) for f in range(8)]


def tie(*arrays):
    return lax.optimization_barrier(arrays)


def turn(v):
    return lax.ppermute(v, ("ctx", "fsdp"), TURN)


def gather_chips(own):
    mine = lax.all_to_all(jnp.broadcast_to(own[None], (N_CTX // 2,) + own.shape), "ctx", 0, 0, tiled=True,
                          axis_index_groups=SAME_CORE)
    return mine, lax.ppermute(mine, "ctx", OTHER_CORE)


def dot_tn(a, b):
    return lax.dot_general(a, b, (((0,), (0,)), ((), ())), preferred_element_type=F32)


def dot_nt(a, b):
    return lax.dot_general(a, b, (((1,), (1,)), ((), ())), preferred_element_type=F32)


def dot_nn(a, b):
    return jnp.dot(a, b, preferred_element_type=F32)


def project_kernel(x_ref, up_ref, wj_ref, ww_ref, add_ref, back_ref,
                   xhat_ref, joint_ref, grad_ref, act_ref, wg_ref, early_ref, widen_s, narrow_s, wg_sum_s, up_sum_s):
    block, width = x_ref.shape[0] * x_ref.shape[1], x_ref.shape[2]
    i = pl.program_id(0)

    @pl.when(i == 0)
    def _():
        for ref in (widen_s, narrow_s, wg_sum_s, up_sum_s):
            ref[...] = jnp.zeros_like(ref)

    x = x_ref[...].reshape(block, width).astype(F32)
    center = x - jnp.mean(x, axis=-1, keepdims=True)
    xhat = (center * lax.rsqrt(jnp.mean(center * center, axis=-1, keepdims=True) + EPSILON)).astype(BF16)
    xhat_ref[...] = xhat
    wide = wj_ref.shape[1]
    joint_ref[...] = dot_nn(xhat, wj_ref[...]) + add_ref[0:1, :wide]
    widened = dot_nn(xhat, ww_ref[...]) + add_ref[0:1, wide:]
    phi = 0.5 * (1.0 + lax.erf(widened * (0.5 ** 0.5)))
    act = (widened * phi).astype(BF16)
    act_ref[...] = act
    slope = phi + widened * jnp.exp(-0.5 * widened * widened) * 0.3989422804014327
    up = up_ref[...].reshape(block, width)
    k = ww_ref.shape[1]
    hd = back_ref.shape[0] - k
    grad_ref[...] = dot_nt(up, back_ref[0:hd, :])
    wg = (dot_nt(up, back_ref[hd:, :]) * slope).astype(BF16)
    wg_ref[...] = wg
    widen_s[...] += dot_nn(wg.T, xhat)
    narrow_s[...] += dot_nn(act.T, up)
    ones = jnp.ones((16, block), BF16)
    wg_sum_s[...] += dot_nn(ones, wg)
    up_sum_s[...] += dot_nn(ones, up)

    @pl.when(i == pl.num_programs(0) - 1)
    def _():
        n = early_ref.shape[1] - 16
        per = k // N_FSDP
        for f in range(N_FSDP):
            early_ref[f, 0:n, 0:k] = widen_s[:, f * n:(f + 1) * n].T.astype(BF16)
            for q in range(width // k):
                early_ref[f, q * per:(q + 1) * per, k:] = (
                    narrow_s[f * per:(f + 1) * per, q * k:(q + 1) * k].astype(BF16))
            early_ref[f, n:, 0:k] = wg_sum_s[...].astype(BF16)
            early_ref[f, n:, k:k + n] = up_sum_s[:, f * n:(f + 1) * n].astype(BF16)
            early_ref[f, n:, k + n:] = jnp.zeros((16, k - n), BF16)


def project(both, wj, ww, add, back):
    slots, _, width = both.shape
    own, per = 128, 4
    rows, block = slots * own, per * own
    n = width // N_FSDP
    wide, ffc = wj.shape[1], ww.shape[1]
    hd = back.shape[0] - ffc
    whole = lambda a: pl.BlockSpec(a.shape, lambda i: (0, 0))
    tall = lambda n: pl.BlockSpec((block, n), lambda i: (i, 0))
    payload = (N_FSDP, n + 16, 2 * ffc)
    return pl.pallas_call(
        project_kernel,
        grid=(slots // per,),
        in_specs=[
            pl.BlockSpec((per, own, width), lambda i: (i, 0, 0)),
            pl.BlockSpec((per, own, width), lambda i: (i, 1, 0)),
            whole(wj), whole(ww), whole(add), whole(back)],
        out_specs=[tall(width), tall(wide), tall(hd), tall(ffc), tall(ffc),
                   pl.BlockSpec(payload, lambda i: (0, 0, 0))],
        out_shape=[
            jax.ShapeDtypeStruct((rows, width), BF16), jax.ShapeDtypeStruct((rows, wide), F32),
            jax.ShapeDtypeStruct((rows, hd), F32), jax.ShapeDtypeStruct((rows, ffc), BF16),
            jax.ShapeDtypeStruct((rows, ffc), BF16), jax.ShapeDtypeStruct(payload, BF16)],
        scratch_shapes=[pltpu.VMEM((ffc, width), F32), pltpu.VMEM((ffc, width), F32),
                        pltpu.VMEM((16, ffc), F32), pltpu.VMEM((16, width), F32)],
        compiler_params=pltpu.CompilerParams(vmem_limit_bytes=VMEM),
        cost_estimate=pl.CostEstimate(flops=2 * rows * width * 1344, bytes_accessed=20 << 20, transcendentals=rows * 512),
    )(both, both, wj, ww, add, back)


def late_kernel(xhat_ref, up_ref, mixed_ref, out_ref, mixedT_s, sum_s):
    rows, block = xhat_ref.shape
    m = mixed_ref.shape[1]
    n = out_ref.shape[1] - 16
    hd = m // 4

    @pl.when(pl.program_id(0) == 0)
    def _():
        mixedT_s[...] = mixed_ref[...].T
        sum_s[...] = dot_nn(jnp.ones((16, rows), BF16), mixed_ref[...]).astype(BF16)

    joint = dot_nn(mixedT_s[0:3 * hd, :], xhat_ref[...])
    dense = dot_nn(mixedT_s[3 * hd:, :], up_ref[...].reshape(rows, block))
    full = jnp.concatenate([joint, dense], axis=0).T.astype(BF16)
    for b in range(block // n):
        out_ref[b, 0:n, :] = full[b * n:(b + 1) * n]
        out_ref[b, n:, :] = sum_s[...]


def late_grads(xhat, both, mixed):
    rows, width = xhat.shape
    n, m = width // N_FSDP, mixed.shape[1]
    block = 2 * n
    return pl.pallas_call(
        late_kernel,
        grid=(width // block,),
        in_specs=[
            pl.BlockSpec((rows, block), lambda i: (0, i)),
            pl.BlockSpec((both.shape[0], 128, block), lambda i: (0, 1, i)),
            pl.BlockSpec(mixed.shape, lambda i: (0, 0))],
        out_specs=pl.BlockSpec((2, n + 16, m), lambda i: (i, 0, 0)),
        out_shape=jax.ShapeDtypeStruct((N_FSDP, n + 16, m), BF16),
        scratch_shapes=[pltpu.VMEM((m, rows), BF16), pltpu.VMEM((16, m), BF16)],
        compiler_params=pltpu.CompilerParams(vmem_limit_bytes=VMEM),
        cost_estimate=pl.CostEstimate(flops=2 * rows * width * m, bytes_accessed=10 << 20, transcendentals=0),
    )(xhat, both, mixed)


def spread_kernel(parity_ref, mixed_ref, wg_ref, act_ref, wj_ref, ww_ref, dense_ref, narrow_ref, *refs):
    out_ref = refs[-1]
    width = wj_ref.shape[0]
    chips, own = out_ref.shape[0], out_ref.shape[1]
    flat = lambda ref: ref[...].reshape(chips * own, ref.shape[3])
    mixed = flat(mixed_ref)
    u = dot_nt(mixed, wj_ref[...]) + dot_nt(flat(wg_ref), ww_ref[...])
    out = dot_nn(mixed, dense_ref[...]) + dot_nn(flat(act_ref), narrow_ref[...])
    for q in range(chips):
        rows = slice(q * own, (q + 1) * own)
        for value, at in ((u[rows], slice(0, width)), (out[rows], slice(width, 2 * width))):
            if len(refs) == 2:
                value = value + refs[0][q, :, at].astype(F32)
            out_ref[q, :, at] = value.astype(BF16)


def spread(parity, mixed, wg, act, wj, ww, dense, narrow, got=None):
    rows, width = mixed.shape[0], wj.shape[0]
    own, chips, per = rows // N_CTX, N_CTX // 2, 2
    whole = lambda a: pl.BlockSpec(a.shape, lambda i, parity: (0, 0))
    split = lambda a: a.reshape(chips, 2, own, a.shape[1])
    tall = lambda a: pl.BlockSpec((per, 1, own, a.shape[1]), lambda i, parity: (i, parity[0], 0, 0))
    block = pl.BlockSpec((per, own, 2 * width), lambda i, parity: (i, 0, 0))
    more = [] if got is None else [got]
    return pl.pallas_call(
        spread_kernel,
        grid_spec=pltpu.PrefetchScalarGridSpec(
            num_scalar_prefetch=1,
            grid=(chips // per,),
            in_specs=[tall(mixed), tall(wg), tall(act), whole(wj), whole(ww), whole(dense), whole(narrow)]
            + [block] * len(more),
            out_specs=block),
        out_shape=jax.ShapeDtypeStruct((chips, own, 2 * width), BF16),
        compiler_params=pltpu.CompilerParams(vmem_limit_bytes=VMEM),
        cost_estimate=pl.CostEstimate(flops=rows * width * 1024, bytes_accessed=9 << 20, transcendentals=0),
    )(parity, split(mixed), split(wg), split(act), wj, ww, dense, narrow, *more)


def finish_early_kernel(f_ref, all_ref, weight_ref, gain_ref, shift_ref,
                        widen_ref, narrow_ref, gain_out, shift_out, bias_out, bias_s):
    n, ff = weight_ref.shape
    k = all_ref.shape[2] // 2
    per = k // N_FSDP
    gain, shift = gain_ref[...], shift_ref[...]
    g_sum = jnp.zeros((n, n), F32)
    s_sum = jnp.zeros((n, n), F32)
    for c in range(N_CTX):
        for q in range(narrow_ref.shape[1] // k):
            narrow_ref[c * per:(c + 1) * per, q * k:(q + 1) * k] = all_ref[c, q * per:(q + 1) * per, k:].astype(F32)
    group = n // per
    for h in range(N_CTX // group):
        parts = [all_ref[h * group + i, :, :k].astype(F32) for i in range(group)]
        for f in range(N_FSDP):
            full = jnp.concatenate([p[:, f * per:(f + 1) * per] for p in parts], axis=1)
            m, bias = full[:n], full[n:n + 1]
            at = f * (ff // N_FSDP) + h * n
            w = weight_ref[:, at:at + n].astype(F32)
            widen_ref[:, at:at + n] = gain * m + shift * bias
            g_sum += w * m
            s_sum += w * bias
            bias_s[:, at:at + n] = full[n:n + 8]
    gain_out[...] = jnp.sum(g_sum.T, axis=0, keepdims=True)
    shift_out[...] = jnp.sum(s_sum.T, axis=0, keepdims=True)
    own = bias_out.shape[1]
    bias_out[...] = bias_s[:, pl.ds(pl.multiple_of(f_ref[0] * own, own), own)][0:1]


def finish_late_kernel(f_ref, core_ref, mine_ref, other_ref, weight_ref, gain_ref, shift_ref,
                       joint_ref, dense_ref, gain_out, shift_out, bias_out, bias_s):
    n = weight_ref.shape[0]
    hd = mine_ref.shape[2] // 4
    width = weight_ref.shape[1] // 3
    even = core_ref[0] == 0
    gain, shift = gain_ref[...], shift_ref[...]
    g_sum = jnp.zeros((n, 2 * hd), F32)
    s_sum = jnp.zeros((n, 2 * hd), F32)
    for q in range(mine_ref.shape[0]):
        mine, other = mine_ref[q].astype(F32), other_ref[q].astype(F32)
        pair = [jnp.where(even, mine, other), jnp.where(even, other, mine)]
        for k in range(3):
            full = jnp.concatenate([p[:, k * hd:(k + 1) * hd] for p in pair], axis=1)
            at = k * width + q * (2 * hd)
            m, bias = full[:n], full[n:n + 1]
            w = weight_ref[:, at:at + 2 * hd].astype(F32)
            joint_ref[:, at:at + 2 * hd] = gain * m + shift * bias
            g_sum += w * m
            s_sum += w * bias
            bias_s[:, at:at + 2 * hd] = full[n:n + 8]
        for b in range(2):
            dense_ref[b * hd:(b + 1) * hd, q * n:(q + 1) * n] = pair[b][:n].T[3 * hd:]
    gain_out[...] = jnp.sum(g_sum.T, axis=0, keepdims=True)
    shift_out[...] = jnp.sum(s_sum.T, axis=0, keepdims=True)
    own = bias_out.shape[1]
    bias_out[...] = bias_s[:, pl.ds(pl.multiple_of(f_ref[0] * own, 128), own)][0:1]


def finish(kernel, places, gathered, weight, gain, shift, side):
    n, columns = weight.shape
    vmem = pl.BlockSpec(memory_space=pltpu.VMEM)
    row = lambda m: jax.ShapeDtypeStruct((1, m), F32)
    wide = lambda v: v.astype(F32)[:, None]
    out = pl.pallas_call(
        kernel,
        in_specs=[pl.BlockSpec(memory_space=pltpu.SMEM)] * len(places) + [vmem] * (len(gathered) + 3),
        out_specs=[vmem] * 5,
        out_shape=[jax.ShapeDtypeStruct(weight.shape, F32), jax.ShapeDtypeStruct(side, F32), row(n), row(n),
                   row(columns // N_FSDP)],
        scratch_shapes=[pltpu.VMEM((8, columns), F32)],
        compiler_params=pltpu.CompilerParams(vmem_limit_bytes=VMEM),
        cost_estimate=pl.CostEstimate(flops=8 * weight.size, bytes_accessed=12 * weight.size, transcendentals=0),
    )(*places, *gathered, weight, wide(gain), wide(shift))
    return out[0], out[1], out[2][0], out[3][0], out[4][0]


def attention_kernel(order_ref, joint_ref, table_ref, grad_ref, out_ref,
                     joint_s, table_s, grad_s, k_s, v_s, qT_s, kT_s, vT_s, gT_s,
                     oT_s, dqT_s, dkT_s, dvT_s, cosT_s, sinT_s, out_s):
    rows, hd = joint_ref.shape[0], joint_ref.shape[1] // 4
    slots, half, tile = N_CTX, rows // (2 * N_CTX), 256
    last = 2 * slots - 1
    for j in range(slots):
        p = order_ref[j]
        for h in range(2):
            src = pl.ds(j * 2 * half + h * half, half)
            dst = pl.ds(pl.multiple_of((p if h == 0 else last - p) * half, half), half)
            joint_s[dst, :] = joint_ref[src, :]
            table_s[dst, :] = table_ref[src, :]
            grad_s[dst, :] = grad_ref[src, :]
    scale = hd ** -0.5

    def spin(t, c, s):
        return jnp.concatenate([t[0:8] * c - t[8:16] * s, t[8:16] * c + t[0:8] * s, t[16:]], axis=0)

    for i in range(rows // tile):
        at = pl.ds(i * tile, tile)
        jT = joint_s[at, :].T
        tT = table_s[at, :].T
        c, s = tT[0:8], tT[8:16]
        cosT_s[:, at] = c
        sinT_s[:, at] = s
        qT = spin(jT[0:hd], c, s).astype(BF16)
        kT = spin(jT[hd:2 * hd], c, s).astype(BF16)
        vT = jT[2 * hd:3 * hd].astype(BF16)
        qT_s[:, at] = (qT.astype(F32) * scale).astype(BF16)
        kT_s[:, at] = kT
        vT_s[:, at] = vT
        k_s[at, :] = kT.astype(F32).T.astype(BF16)
        v_s[at, :] = vT.astype(F32).T.astype(BF16)
        gT_s[:, at] = grad_s[at, :].T.astype(BF16)
    dkT_s[...] = jnp.zeros_like(dkT_s)
    dvT_s[...] = jnp.zeros_like(dvT_s)
    key_at = lax.broadcasted_iota(jnp.int32, (tile, tile), 0)
    query_at = lax.broadcasted_iota(jnp.int32, (tile, tile), 1)
    seen = key_at <= query_at
    dot = lambda a, b: jnp.dot(a, b, preferred_element_type=F32)
    dot_nt = lambda a, b: lax.dot_general(a, b, (((1,), (1,)), ((), ())), preferred_element_type=F32)
    for i in range(rows // tile):
        at = pl.ds(i * tile, tile)
        span = (i + 1) * tile
        upto = pl.ds(0, span)
        qT, gT = qT_s[:, at], gT_s[:, at]
        sT = dot(k_s[upto, :], qT)
        edge = jnp.where(seen, sT[i * tile:], NEGATIVE)
        sT = edge if i == 0 else jnp.concatenate([sT[:i * tile], edge], axis=0)
        largest = jnp.max(sT, axis=0, keepdims=True)
        e = jnp.exp(sT - largest)
        pT = e * (1.0 / jnp.sum(e, axis=0, keepdims=True))
        pT_low = pT.astype(BF16)
        dpT = dot(v_s[upto, :], gT)
        balance = jnp.sum(dpT * pT, axis=0, keepdims=True)
        dsT = (pT * (dpT - balance)).astype(BF16)
        oT_s[:, at] = dot(vT_s[:, upto], pT_low)
        dqT_s[:, at] = dot(kT_s[:, upto], dsT) * scale
        dkT_s[:, upto] += dot_nt(qT, dsT)
        dvT_s[:, upto] += dot_nt(gT, pT_low)
    for i in range(rows // tile):
        at = pl.ds(i * tile, tile)
        c, s = cosT_s[:, at], -sinT_s[:, at]
        full = jnp.concatenate(
            [spin(dqT_s[:, at], c, s), spin(dkT_s[:, at], c, s), dvT_s[:, at], oT_s[:, at]], axis=0)
        out_s[at, :] = full.T.astype(BF16)
    for j in range(slots):
        p = order_ref[j]
        for h in range(2):
            dst = pl.ds(j * 2 * half + h * half, half)
            src = pl.ds(pl.multiple_of((p if h == 0 else last - p) * half, half), half)
            out_ref[dst, :] = out_s[src, :]


def attention(order, joint, table, grad):
    rows, hd = joint.shape[0], joint.shape[1] // 4
    vmem = pl.BlockSpec(memory_space=pltpu.VMEM)
    return pl.pallas_call(
        attention_kernel,
        out_shape=jax.ShapeDtypeStruct((rows, 4 * hd), BF16),
        in_specs=[pl.BlockSpec(memory_space=pltpu.SMEM), vmem, vmem, vmem],
        out_specs=vmem,
        scratch_shapes=[
            pltpu.VMEM((rows, 4 * hd), F32),
            pltpu.VMEM((rows, 16), F32),
            pltpu.VMEM((rows, hd), F32),
            pltpu.VMEM((rows, hd), BF16),
            pltpu.VMEM((rows, hd), BF16),
            pltpu.VMEM((hd, rows), BF16),
            pltpu.VMEM((hd, rows), BF16),
            pltpu.VMEM((hd, rows), BF16),
            pltpu.VMEM((hd, rows), BF16),
            pltpu.VMEM((hd, rows), F32),
            pltpu.VMEM((hd, rows), F32),
            pltpu.VMEM((hd, rows), F32),
            pltpu.VMEM((hd, rows), F32),
            pltpu.VMEM((8, rows), F32),
            pltpu.VMEM((8, rows), F32),
            pltpu.VMEM((rows, 4 * hd), BF16),
        ],
        compiler_params=pltpu.CompilerParams(vmem_limit_bytes=VMEM),
        cost_estimate=pl.CostEstimate(flops=7 * rows * rows * hd, bytes_accessed=8 << 20, transcendentals=rows * rows // 2),
    )(order, joint, table, grad)


def shards(
    tokens, upstream, block_pairs, rotary_place,
    first_gain, first_shift, joint_weight, joint_bias, dense_weight, dense_bias,
    second_gain, second_shift, widen_weight, widen_bias, narrow_weight, narrow_bias,
):
    own_rows, width = tokens.shape[1], tokens.shape[2]
    hd = width // HEADS
    ff = widen_weight.shape[1]
    ffc = ff // N_CTX
    rows = own_rows * N_CTX
    c = lax.axis_index("ctx")
    f = lax.axis_index("fsdp")
    own_tokens, own_up = tokens[0], upstream[0]
    d_own = width // N_FSDP

    per = ffc // N_FSDP
    both = lax.all_gather(jnp.concatenate([own_tokens, own_up], axis=0), "ctx", axis=0)
    joint_part = lax.dynamic_index_in_dim(joint_weight.reshape(d_own, 3, HEADS, hd), c, 2, keepdims=False)
    vectors = jnp.concatenate(
        [v[:, None] for v in (first_gain, first_shift, second_gain, second_shift, dense_bias, narrow_bias)]
        + [joint_bias.reshape(d_own, 3), widen_bias.reshape(d_own, 4), jnp.zeros((d_own, 51), BF16)], axis=1)
    widen_part = [lax.dynamic_slice_in_dim(widen_weight, g * (ff // N_FSDP) + c * per, per, axis=1)
                  for g in range(N_FSDP)]
    narrow_part = lax.dynamic_slice_in_dim(narrow_weight, c * per, per, axis=0)
    narrow_part = jnp.concatenate([narrow_part[:, q * ffc:(q + 1) * ffc] for q in range(width // ffc)], axis=0)
    part = jnp.concatenate([joint_part.reshape(d_own, 3 * hd), vectors] + widen_part + [narrow_part], axis=1)
    slices = lax.all_to_all(jnp.broadcast_to(part[None], (N_FSDP,) + part.shape), "fsdp", 0, 0, tiled=True)
    dense_w = turn(lax.dynamic_slice_in_dim(dense_weight, (c % 2) * hd, hd, axis=0))
    place_all = lax.all_gather(rotary_place[0], "ctx", axis=0, tiled=True).astype(F32)
    narrow_w = jnp.concatenate(
        [slices[:, q * per:(q + 1) * per, 4 * hd + ffc:] for q in range(width // ffc)], axis=2).reshape(ffc, width)
    slices = slices.reshape(width, part.shape[1])
    back_w = jnp.concatenate([dense_w, narrow_w], axis=0)

    steps = jnp.arange(8, dtype=F32)
    angles = place_all[:, None] * (ROTARY_BASE ** (-2.0 * steps / 16))
    table = jnp.concatenate([jnp.cos(angles), jnp.sin(angles)], axis=1)
    order = block_pairs[0]

    wj = slices[:, :4 * hd].astype(F32)
    ww = slices[:, 4 * hd:4 * hd + ffc].astype(F32)
    vec = slices[:, 3 * hd:4 * hd].astype(F32)
    g1, s1, g2, s2 = vec[:, 0:1], vec[:, 1:2], vec[:, 2:3], vec[:, 3:4]
    dense_b, narrow_b = vec[:, 4], vec[:, 5]
    jb_full = vec[:, 6:9].reshape(3, HEADS, hd)
    wb_full = vec[:, 9:13].reshape(ff)
    jb_own = lax.dynamic_index_in_dim(jb_full, c, 1, keepdims=False).reshape(3 * hd)
    wb_own = lax.dynamic_index_in_dim(wb_full.reshape(N_FSDP, N_CTX, per), c, 1, keepdims=False).reshape(ffc)
    wj = jnp.where(jnp.arange(4 * hd)[None, :] < 3 * hd, wj, 0.0)
    wj_g = (g1 * wj).astype(BF16)
    ww_g = (g2 * ww).astype(BF16)
    shifted = jnp.concatenate([
        jnp.sum(s1 * wj, axis=0) + jnp.pad(jb_own, (0, hd)), jnp.sum(s2 * ww, axis=0) + wb_own])[None, :]
    dense_p = jnp.pad(dense_w, ((3 * hd, 0), (0, 0)))

    both, table, dense_p = tie(both, table, dense_p)
    xhat, joint, att_grad, act, wg, early = project(both, wj_g, ww_g, shifted, back_w)
    early = lax.all_to_all(early, "fsdp", 0, 0, tiled=True)

    mixed = attention(order, joint, table, att_grad)
    core = (c % 2)[None]
    shares = (mixed, wg, act, wj_g, ww_g, dense_p, narrow_w)
    other = spread(1 - core, *shares)
    other, early = tie(other, early)

    early = jnp.sum(early.astype(F32), axis=0)
    bias_grad = early[d_own, ffc:ffc + d_own]
    early_all = lax.all_gather(early.astype(BF16), "ctx", axis=0)
    late, other = tie(late_grads(xhat, both, mixed), lax.ppermute(other, "ctx", OTHER_CORE))
    pair = spread(core, *shares, other)
    late, pair = tie(lax.all_to_all(late, "fsdp", 0, 0, tiled=True), pair)
    low = jnp.sum(late.astype(F32), axis=0).astype(BF16)

    summed = lax.all_to_all(pair, "ctx", 0, 0, tiled=True, axis_index_groups=SAME_CORE)
    widen_grad, narrow_grad, g2_grad, s2_grad, wb_shard = finish(
        finish_early_kernel, (f[None],), (early_all,), widen_weight, second_gain, second_shift, (2 * ffc, width))
    low, summed, wb_shard = tie(
        jnp.concatenate([low[:, :3 * hd], turn(low[:, 3 * hd:])], axis=1), summed, wb_shard)
    late_all = gather_chips(low)
    summed = jnp.sum(summed.astype(F32), axis=0)
    u_own, out_own = summed[:, :width], summed[:, width:]

    own_x = own_tokens.astype(F32)
    block_out = (own_x + out_own + dense_b + narrow_b).astype(BF16)
    own_center = own_x - jnp.mean(own_x, axis=-1, keepdims=True)
    own_rstd = lax.rsqrt(jnp.mean(own_center * own_center, axis=-1, keepdims=True) + EPSILON)
    own_xhat = own_center * own_rstd
    tokens_grad = own_up.astype(F32) + own_rstd * (
        u_own - jnp.mean(u_own, axis=-1, keepdims=True)
        - own_xhat * jnp.mean(u_own * own_xhat, axis=-1, keepdims=True))

    joint_grad, dense_grad, g1_grad, s1_grad, jb_shard = finish(
        finish_late_kernel, (f[None], core), late_all, joint_weight, first_gain, first_shift, (2 * hd, width))
    return (
        block_out[None], tokens_grad[None], g1_grad, s1_grad, joint_grad, jb_shard,
        dense_grad, bias_grad, g2_grad, s2_grad, widen_grad, wb_shard, narrow_grad, bias_grad,
    )


def solution(mesh):
    rows = P("fsdp", "ctx", None)
    vec, mat = P("fsdp"), P("fsdp", None)
    in_specs = (rows, rows, mat, P("fsdp", "ctx"), vec, vec, mat, vec, mat, vec, vec, vec, mat, vec, mat, vec)
    out_specs = (rows, rows, vec, vec, mat, vec, mat, vec, vec, vec, mat, vec, mat, vec)
    return jax.shard_map(shards, mesh=mesh, in_specs=in_specs, out_specs=out_specs, check_vma=False)
```

```python
import jax
import jax.numpy as jnp
from jax import lax
from jax.experimental import pallas as pl
from jax.experimental.pallas import tpu as pltpu
from jax.sharding import PartitionSpec as P

HEADS = 16
EPSILON = 1e-05
NEGATIVE = -1e30
ROTARY_BASE = 10000.0
N_CTX = 16
VMEM = 60 * 1024 * 1024
N_FSDP = 8
F32 = jnp.float32
BF16 = jnp.bfloat16

ACROSS_Y = [(i ^ 2, i) for i in range(16)]
OTHER_CORE = [(i ^ 1, i) for i in range(16)]
AHEAD_Z = [[(i, (i + 4 * d) % 16) for i in range(16)] for d in range(4)]
SAME_CORE = [list(range(0, 16, 2)), list(range(1, 16, 2))]
TURN = [(c * 8 + f, (2 * f + (c & 1)) * 8 + (c >> 1)) for c in range(16) for f in range(8)]


def tie(*arrays):
    return lax.optimization_barrier(arrays)


def turn(v):
    return lax.ppermute(v, ("ctx", "fsdp"), TURN)


def move(v, way):
    return lax.ppermute(v, "ctx", way)


def gather_chips(own):
    return lax.all_to_all(jnp.broadcast_to(own[None], (N_CTX // 2,) + own.shape), "ctx", 0, 0, tiled=True,
                          axis_index_groups=SAME_CORE)


def dot_tn(a, b):
    return lax.dot_general(a, b, (((0,), (0,)), ((), ())), preferred_element_type=F32)


def dot_nt(a, b):
    return lax.dot_general(a, b, (((1,), (1,)), ((), ())), preferred_element_type=F32)


def dot_nn(a, b):
    return jnp.dot(a, b, preferred_element_type=F32)


def project_kernel(x_ref, up_ref, wj_ref, ww_ref, add_ref, back_ref,
                   xhat_ref, joint_ref, grad_ref, act_ref, wg_ref, early_ref, widen_s, narrow_s, wg_sum_s, up_sum_s):
    block, width = x_ref.shape[0] * x_ref.shape[1], x_ref.shape[2]
    i = pl.program_id(0)

    @pl.when(i == 0)
    def _():
        for ref in (widen_s, narrow_s, wg_sum_s, up_sum_s):
            ref[...] = jnp.zeros_like(ref)

    x = x_ref[...].reshape(block, width).astype(F32)
    center = x - jnp.mean(x, axis=-1, keepdims=True)
    xhat = (center * lax.rsqrt(jnp.mean(center * center, axis=-1, keepdims=True) + EPSILON)).astype(BF16)
    xhat_ref[...] = xhat
    wide = wj_ref.shape[1]
    joint_ref[...] = dot_nn(xhat, wj_ref[...]) + add_ref[0:1, :wide]
    widened = dot_nn(xhat, ww_ref[...]) + add_ref[0:1, wide:]
    phi = 0.5 * (1.0 + lax.erf(widened * (0.5 ** 0.5)))
    act = (widened * phi).astype(BF16)
    act_ref[...] = act
    slope = phi + widened * jnp.exp(-0.5 * widened * widened) * 0.3989422804014327
    up = up_ref[...].reshape(block, width)
    k = ww_ref.shape[1]
    hd = back_ref.shape[0] - k
    grad_ref[...] = dot_nt(up, back_ref[0:hd, :])
    wg = (dot_nt(up, back_ref[hd:, :]) * slope).astype(BF16)
    wg_ref[...] = wg
    widen_s[...] += dot_nn(wg.T, xhat)
    narrow_s[...] += dot_nn(act.T, up)
    ones = jnp.ones((16, block), BF16)
    wg_sum_s[...] += dot_nn(ones, wg)
    up_sum_s[...] += dot_nn(ones, up)

    @pl.when(i == pl.num_programs(0) - 1)
    def _():
        n = early_ref.shape[1] - 16
        per = k // N_FSDP
        for f in range(N_FSDP):
            early_ref[f, 0:n, 0:k] = widen_s[:, f * n:(f + 1) * n].T.astype(BF16)
            for q in range(width // k):
                early_ref[f, q * per:(q + 1) * per, k:] = (
                    narrow_s[f * per:(f + 1) * per, q * k:(q + 1) * k].astype(BF16))
            early_ref[f, n:, 0:k] = wg_sum_s[...].astype(BF16)
            early_ref[f, n:, k:k + n] = up_sum_s[:, f * n:(f + 1) * n].astype(BF16)
            early_ref[f, n:, k + n:] = jnp.zeros((16, k - n), BF16)


def project(both, wj, ww, add, back):
    slots, _, width = both.shape
    own, per = 128, 4
    rows, block = slots * own, per * own
    n = width // N_FSDP
    wide, ffc = wj.shape[1], ww.shape[1]
    hd = back.shape[0] - ffc
    whole = lambda a: pl.BlockSpec(a.shape, lambda i: (0, 0))
    tall = lambda n: pl.BlockSpec((block, n), lambda i: (i, 0))
    payload = (N_FSDP, n + 16, 2 * ffc)
    return pl.pallas_call(
        project_kernel,
        grid=(slots // per,),
        in_specs=[
            pl.BlockSpec((per, own, width), lambda i: (i, 0, 0)),
            pl.BlockSpec((per, own, width), lambda i: (i, 1, 0)),
            whole(wj), whole(ww), whole(add), whole(back)],
        out_specs=[tall(width), tall(wide), tall(hd), tall(ffc), tall(ffc),
                   pl.BlockSpec(payload, lambda i: (0, 0, 0))],
        out_shape=[
            jax.ShapeDtypeStruct((rows, width), BF16), jax.ShapeDtypeStruct((rows, wide), F32),
            jax.ShapeDtypeStruct((rows, hd), F32), jax.ShapeDtypeStruct((rows, ffc), BF16),
            jax.ShapeDtypeStruct((rows, ffc), BF16), jax.ShapeDtypeStruct(payload, BF16)],
        scratch_shapes=[pltpu.VMEM((ffc, width), F32), pltpu.VMEM((ffc, width), F32),
                        pltpu.VMEM((16, ffc), F32), pltpu.VMEM((16, width), F32)],
        compiler_params=pltpu.CompilerParams(vmem_limit_bytes=VMEM),
        cost_estimate=pl.CostEstimate(flops=2 * rows * width * 1344, bytes_accessed=20 << 20, transcendentals=rows * 512),
    )(both, both, wj, ww, add, back)


def late_kernel(xhat_ref, up_ref, mixed_ref, out_ref, mixedT_s, sum_s):
    rows, block = xhat_ref.shape
    m = mixed_ref.shape[1]
    n = out_ref.shape[1] - 16
    hd = m // 4

    @pl.when(pl.program_id(0) == 0)
    def _():
        mixedT_s[...] = mixed_ref[...].T
        sum_s[...] = dot_nn(jnp.ones((16, rows), BF16), mixed_ref[...]).astype(BF16)

    joint = dot_nn(mixedT_s[0:3 * hd, :], xhat_ref[...])
    dense = dot_nn(mixedT_s[3 * hd:, :], up_ref[...].reshape(rows, block))
    full = jnp.concatenate([joint, dense], axis=0).T.astype(BF16)
    for b in range(block // n):
        out_ref[b, 0:n, :] = full[b * n:(b + 1) * n]
        out_ref[b, n:, :] = sum_s[...]


def late_grads(xhat, both, mixed):
    rows, width = xhat.shape
    n, m = width // N_FSDP, mixed.shape[1]
    block = 2 * n
    return pl.pallas_call(
        late_kernel,
        grid=(width // block,),
        in_specs=[
            pl.BlockSpec((rows, block), lambda i: (0, i)),
            pl.BlockSpec((both.shape[0], 128, block), lambda i: (0, 1, i)),
            pl.BlockSpec(mixed.shape, lambda i: (0, 0))],
        out_specs=pl.BlockSpec((2, n + 16, m), lambda i: (i, 0, 0)),
        out_shape=jax.ShapeDtypeStruct((N_FSDP, n + 16, m), BF16),
        scratch_shapes=[pltpu.VMEM((m, rows), BF16), pltpu.VMEM((16, m), BF16)],
        compiler_params=pltpu.CompilerParams(vmem_limit_bytes=VMEM),
        cost_estimate=pl.CostEstimate(flops=2 * rows * width * m, bytes_accessed=10 << 20, transcendentals=0),
    )(xhat, both, mixed)


def spread_kernel(place_ref, mixed_ref, wg_ref, act_ref, wj_ref, ww_ref, dense_ref, narrow_ref, *refs):
    chips, own = mixed_ref.shape[0], mixed_ref.shape[2]
    flat = lambda ref: ref[...].reshape(chips * own, ref.shape[3])
    mixed = flat(mixed_ref)
    u = dot_nt(mixed, wj_ref[...]) + dot_nt(flat(wg_ref), ww_ref[...])
    out = dot_nn(mixed, dense_ref[...]) + dot_nn(flat(act_ref), narrow_ref[...])
    u = [u[q * own:(q + 1) * own] for q in range(chips)]
    out = [out[q * own:(q + 1) * own] for q in range(chips)]
    far = [q ^ place_ref[1] for q in range(chips)]
    if len(refs) == 1:
        for q in range(chips):
            refs[0][0, far[q]] = u[q].astype(BF16)
            refs[0][1, far[q]] = out[q].astype(BF16)
        return
    got_ref, near_ref, far_ref = refs[:3]
    u = [(u[q] + got_ref[0, far[q]].astype(F32)).astype(BF16) for q in range(chips)]
    out = [(out[q] + got_ref[1, far[q]].astype(F32)).astype(BF16) for q in range(chips)]
    low = place_ref[1] == 0
    near_ref[0] = jnp.where(low, u[0], u[1])
    far_ref[0] = jnp.where(low, u[1], u[0])
    for d, ref in enumerate(refs[3:]):
        @pl.when(pl.program_id(0) == d)
        def _():
            ref[0] = jnp.where(low, out[0], out[1])
            ref[1] = jnp.where(low, out[1], out[0])


def spread(place, mixed, wg, act, wj, ww, dense, narrow, got=None):
    rows, width = mixed.shape[0], wj.shape[0]
    own, chips, per = rows // N_CTX, N_CTX // 2, 2
    deep = chips // per
    whole = lambda a: pl.BlockSpec(a.shape, lambda i, place: (0, 0))
    split = lambda a: a.reshape(chips, 2, own, a.shape[1])
    tall = lambda a: pl.BlockSpec((per, 1, own, a.shape[1]), lambda i, place: ((place[0] + i) % deep, place[2], 0, 0))
    pair = pl.BlockSpec((2, per, own, width), lambda i, place: (0, i, 0, 0))
    shape = lambda *lead: jax.ShapeDtypeStruct(lead + (own, width), BF16)
    if got is None:
        more, out_specs, out_shape = [], pair, shape(2, chips)
    else:
        more = [got]
        out_specs = ([pl.BlockSpec((1, own, width), lambda i, place: (i, 0, 0))] * 2
                     + [pl.BlockSpec((per, own, width), lambda i, place: (0, 0, 0))] * deep)
        out_shape = [shape(deep)] * 2 + [shape(per)] * deep
    return pl.pallas_call(
        spread_kernel,
        grid_spec=pltpu.PrefetchScalarGridSpec(
            num_scalar_prefetch=1,
            grid=(deep,),
            in_specs=[tall(mixed), tall(wg), tall(act), whole(wj), whole(ww), whole(dense), whole(narrow)]
            + [pair] * len(more),
            out_specs=out_specs),
        out_shape=out_shape,
        compiler_params=pltpu.CompilerParams(vmem_limit_bytes=VMEM),
        cost_estimate=pl.CostEstimate(flops=rows * width * 1024, bytes_accessed=9 << 20, transcendentals=0),
    )(place, split(mixed), split(wg), split(act), wj, ww, dense, narrow, *more)


def finish_early_kernel(f_ref, all_ref, weight_ref, gain_ref, shift_ref,
                        widen_ref, narrow_ref, gain_out, shift_out, bias_out, bias_s):
    n, ff = weight_ref.shape
    k = all_ref.shape[2] // 2
    per = k // N_FSDP
    gain, shift = gain_ref[...], shift_ref[...]
    g_sum = jnp.zeros((n, n), F32)
    s_sum = jnp.zeros((n, n), F32)
    for c in range(N_CTX):
        for q in range(narrow_ref.shape[1] // k):
            narrow_ref[c * per:(c + 1) * per, q * k:(q + 1) * k] = all_ref[c, q * per:(q + 1) * per, k:].astype(F32)
    group = n // per
    for h in range(N_CTX // group):
        parts = [all_ref[h * group + i, :, :k].astype(F32) for i in range(group)]
        for f in range(N_FSDP):
            full = jnp.concatenate([p[:, f * per:(f + 1) * per] for p in parts], axis=1)
            m, bias = full[:n], full[n:n + 1]
            at = f * (ff // N_FSDP) + h * n
            w = weight_ref[:, at:at + n].astype(F32)
            widen_ref[:, at:at + n] = gain * m + shift * bias
            g_sum += w * m
            s_sum += w * bias
            bias_s[:, at:at + n] = full[n:n + 8]
    gain_out[...] = jnp.sum(g_sum.T, axis=0, keepdims=True)
    shift_out[...] = jnp.sum(s_sum.T, axis=0, keepdims=True)
    own = bias_out.shape[1]
    bias_out[...] = bias_s[:, pl.ds(pl.multiple_of(f_ref[0] * own, own), own)][0:1]


def finish_late_kernel(f_ref, core_ref, mine_ref, other_ref, weight_ref, gain_ref, shift_ref,
                       joint_ref, dense_ref, gain_out, shift_out, bias_out, bias_s):
    n = weight_ref.shape[0]
    hd = mine_ref.shape[2] // 4
    width = weight_ref.shape[1] // 3
    even = core_ref[0] == 0
    gain, shift = gain_ref[...], shift_ref[...]
    g_sum = jnp.zeros((n, 2 * hd), F32)
    s_sum = jnp.zeros((n, 2 * hd), F32)
    for q in range(mine_ref.shape[0]):
        mine, other = mine_ref[q].astype(F32), other_ref[q].astype(F32)
        pair = [jnp.where(even, mine, other), jnp.where(even, other, mine)]
        for k in range(3):
            full = jnp.concatenate([p[:, k * hd:(k + 1) * hd] for p in pair], axis=1)
            at = k * width + q * (2 * hd)
            m, bias = full[:n], full[n:n + 1]
            w = weight_ref[:, at:at + 2 * hd].astype(F32)
            joint_ref[:, at:at + 2 * hd] = gain * m + shift * bias
            g_sum += w * m
            s_sum += w * bias
            bias_s[:, at:at + 2 * hd] = full[n:n + 8]
        for b in range(2):
            dense_ref[b * hd:(b + 1) * hd, q * n:(q + 1) * n] = pair[b][:n].T[3 * hd:]
    gain_out[...] = jnp.sum(g_sum.T, axis=0, keepdims=True)
    shift_out[...] = jnp.sum(s_sum.T, axis=0, keepdims=True)
    own = bias_out.shape[1]
    bias_out[...] = bias_s[:, pl.ds(pl.multiple_of(f_ref[0] * own, 128), own)][0:1]


def finish(kernel, places, gathered, weight, gain, shift, side):
    n, columns = weight.shape
    vmem = pl.BlockSpec(memory_space=pltpu.VMEM)
    row = lambda m: jax.ShapeDtypeStruct((1, m), F32)
    wide = lambda v: v.astype(F32)[:, None]
    out = pl.pallas_call(
        kernel,
        in_specs=[pl.BlockSpec(memory_space=pltpu.SMEM)] * len(places) + [vmem] * (len(gathered) + 3),
        out_specs=[vmem] * 5,
        out_shape=[jax.ShapeDtypeStruct(weight.shape, F32), jax.ShapeDtypeStruct(side, F32), row(n), row(n),
                   row(columns // N_FSDP)],
        scratch_shapes=[pltpu.VMEM((8, columns), F32)],
        compiler_params=pltpu.CompilerParams(vmem_limit_bytes=VMEM),
        cost_estimate=pl.CostEstimate(flops=8 * weight.size, bytes_accessed=12 * weight.size, transcendentals=0),
    )(*places, *gathered, weight, wide(gain), wide(shift))
    return out[0], out[1], out[2][0], out[3][0], out[4][0]


def attention_kernel(order_ref, joint_ref, table_ref, grad_ref, out_ref,
                     joint_s, table_s, grad_s, k_s, v_s, qT_s, kT_s, vT_s, gT_s,
                     oT_s, dqT_s, dkT_s, dvT_s, cosT_s, sinT_s, out_s):
    rows, hd = joint_ref.shape[0], joint_ref.shape[1] // 4
    slots, half, tile = N_CTX, rows // (2 * N_CTX), 256
    last = 2 * slots - 1
    for j in range(slots):
        p = order_ref[j]
        for h in range(2):
            src = pl.ds(j * 2 * half + h * half, half)
            dst = pl.ds(pl.multiple_of((p if h == 0 else last - p) * half, half), half)
            joint_s[dst, :] = joint_ref[src, :]
            table_s[dst, :] = table_ref[src, :]
            grad_s[dst, :] = grad_ref[src, :]
    scale = hd ** -0.5

    def spin(t, c, s):
        return jnp.concatenate([t[0:8] * c - t[8:16] * s, t[8:16] * c + t[0:8] * s, t[16:]], axis=0)

    for i in range(rows // tile):
        at = pl.ds(i * tile, tile)
        jT = joint_s[at, :].T
        tT = table_s[at, :].T
        c, s = tT[0:8], tT[8:16]
        cosT_s[:, at] = c
        sinT_s[:, at] = s
        qT = spin(jT[0:hd], c, s).astype(BF16)
        kT = spin(jT[hd:2 * hd], c, s).astype(BF16)
        vT = jT[2 * hd:3 * hd].astype(BF16)
        qT_s[:, at] = (qT.astype(F32) * scale).astype(BF16)
        kT_s[:, at] = kT
        vT_s[:, at] = vT
        k_s[at, :] = kT.astype(F32).T.astype(BF16)
        v_s[at, :] = vT.astype(F32).T.astype(BF16)
        gT_s[:, at] = grad_s[at, :].T.astype(BF16)
    dkT_s[...] = jnp.zeros_like(dkT_s)
    dvT_s[...] = jnp.zeros_like(dvT_s)
    key_at = lax.broadcasted_iota(jnp.int32, (tile, tile), 0)
    query_at = lax.broadcasted_iota(jnp.int32, (tile, tile), 1)
    seen = key_at <= query_at
    dot = lambda a, b: jnp.dot(a, b, preferred_element_type=F32)
    dot_nt = lambda a, b: lax.dot_general(a, b, (((1,), (1,)), ((), ())), preferred_element_type=F32)
    for i in range(rows // tile):
        at = pl.ds(i * tile, tile)
        span = (i + 1) * tile
        upto = pl.ds(0, span)
        qT, gT = qT_s[:, at], gT_s[:, at]
        sT = dot(k_s[upto, :], qT)
        edge = jnp.where(seen, sT[i * tile:], NEGATIVE)
        sT = edge if i == 0 else jnp.concatenate([sT[:i * tile], edge], axis=0)
        largest = jnp.max(sT, axis=0, keepdims=True)
        e = jnp.exp(sT - largest)
        pT = e * (1.0 / jnp.sum(e, axis=0, keepdims=True))
        pT_low = pT.astype(BF16)
        dpT = dot(v_s[upto, :], gT)
        balance = jnp.sum(dpT * pT, axis=0, keepdims=True)
        dsT = (pT * (dpT - balance)).astype(BF16)
        oT_s[:, at] = dot(vT_s[:, upto], pT_low)
        dqT_s[:, at] = dot(kT_s[:, upto], dsT) * scale
        dkT_s[:, upto] += dot_nt(qT, dsT)
        dvT_s[:, upto] += dot_nt(gT, pT_low)
    for i in range(rows // tile):
        at = pl.ds(i * tile, tile)
        c, s = cosT_s[:, at], -sinT_s[:, at]
        full = jnp.concatenate(
            [spin(dqT_s[:, at], c, s), spin(dkT_s[:, at], c, s), dvT_s[:, at], oT_s[:, at]], axis=0)
        out_s[at, :] = full.T.astype(BF16)
    for j in range(slots):
        p = order_ref[j]
        for h in range(2):
            dst = pl.ds(j * 2 * half + h * half, half)
            src = pl.ds(pl.multiple_of((p if h == 0 else last - p) * half, half), half)
            out_ref[dst, :] = out_s[src, :]


def attention(order, joint, table, grad):
    rows, hd = joint.shape[0], joint.shape[1] // 4
    vmem = pl.BlockSpec(memory_space=pltpu.VMEM)
    return pl.pallas_call(
        attention_kernel,
        out_shape=jax.ShapeDtypeStruct((rows, 4 * hd), BF16),
        in_specs=[pl.BlockSpec(memory_space=pltpu.SMEM), vmem, vmem, vmem],
        out_specs=vmem,
        scratch_shapes=[
            pltpu.VMEM((rows, 4 * hd), F32),
            pltpu.VMEM((rows, 16), F32),
            pltpu.VMEM((rows, hd), F32),
            pltpu.VMEM((rows, hd), BF16),
            pltpu.VMEM((rows, hd), BF16),
            pltpu.VMEM((hd, rows), BF16),
            pltpu.VMEM((hd, rows), BF16),
            pltpu.VMEM((hd, rows), BF16),
            pltpu.VMEM((hd, rows), BF16),
            pltpu.VMEM((hd, rows), F32),
            pltpu.VMEM((hd, rows), F32),
            pltpu.VMEM((hd, rows), F32),
            pltpu.VMEM((hd, rows), F32),
            pltpu.VMEM((8, rows), F32),
            pltpu.VMEM((8, rows), F32),
            pltpu.VMEM((rows, 4 * hd), BF16),
        ],
        compiler_params=pltpu.CompilerParams(vmem_limit_bytes=VMEM),
        cost_estimate=pl.CostEstimate(flops=7 * rows * rows * hd, bytes_accessed=8 << 20, transcendentals=rows * rows // 2),
    )(order, joint, table, grad)


def shards(
    tokens, upstream, block_pairs, rotary_place,
    first_gain, first_shift, joint_weight, joint_bias, dense_weight, dense_bias,
    second_gain, second_shift, widen_weight, widen_bias, narrow_weight, narrow_bias,
):
    own_rows, width = tokens.shape[1], tokens.shape[2]
    hd = width // HEADS
    ff = widen_weight.shape[1]
    ffc = ff // N_CTX
    rows = own_rows * N_CTX
    c = lax.axis_index("ctx")
    f = lax.axis_index("fsdp")
    own_tokens, own_up = tokens[0], upstream[0]
    d_own = width // N_FSDP

    per = ffc // N_FSDP
    both = lax.all_gather(jnp.concatenate([own_tokens, own_up], axis=0), "ctx", axis=0)
    joint_part = lax.dynamic_index_in_dim(joint_weight.reshape(d_own, 3, HEADS, hd), c, 2, keepdims=False)
    vectors = jnp.concatenate(
        [v[:, None] for v in (first_gain, first_shift, second_gain, second_shift, dense_bias, narrow_bias)]
        + [joint_bias.reshape(d_own, 3), widen_bias.reshape(d_own, 4), jnp.zeros((d_own, 51), BF16)], axis=1)
    widen_part = [lax.dynamic_slice_in_dim(widen_weight, g * (ff // N_FSDP) + c * per, per, axis=1)
                  for g in range(N_FSDP)]
    narrow_part = lax.dynamic_slice_in_dim(narrow_weight, c * per, per, axis=0)
    narrow_part = jnp.concatenate([narrow_part[:, q * ffc:(q + 1) * ffc] for q in range(width // ffc)], axis=0)
    part = jnp.concatenate([joint_part.reshape(d_own, 3 * hd), vectors] + widen_part + [narrow_part], axis=1)
    slices = lax.all_to_all(jnp.broadcast_to(part[None], (N_FSDP,) + part.shape), "fsdp", 0, 0, tiled=True)
    dense_w = turn(lax.dynamic_slice_in_dim(dense_weight, (c % 2) * hd, hd, axis=0))
    place_all = lax.all_gather(rotary_place[0], "ctx", axis=0, tiled=True).astype(F32)
    narrow_w = jnp.concatenate(
        [slices[:, q * per:(q + 1) * per, 4 * hd + ffc:] for q in range(width // ffc)], axis=2).reshape(ffc, width)
    slices = slices.reshape(width, part.shape[1])
    back_w = jnp.concatenate([dense_w, narrow_w], axis=0)

    steps = jnp.arange(8, dtype=F32)
    angles = place_all[:, None] * (ROTARY_BASE ** (-2.0 * steps / 16))
    table = jnp.concatenate([jnp.cos(angles), jnp.sin(angles)], axis=1)
    order = block_pairs[0]

    wj = slices[:, :4 * hd].astype(F32)
    ww = slices[:, 4 * hd:4 * hd + ffc].astype(F32)
    vec = slices[:, 3 * hd:4 * hd].astype(F32)
    g1, s1, g2, s2 = vec[:, 0:1], vec[:, 1:2], vec[:, 2:3], vec[:, 3:4]
    dense_b, narrow_b = vec[:, 4], vec[:, 5]
    jb_full = vec[:, 6:9].reshape(3, HEADS, hd)
    wb_full = vec[:, 9:13].reshape(ff)
    jb_own = lax.dynamic_index_in_dim(jb_full, c, 1, keepdims=False).reshape(3 * hd)
    wb_own = lax.dynamic_index_in_dim(wb_full.reshape(N_FSDP, N_CTX, per), c, 1, keepdims=False).reshape(ffc)
    wj = jnp.where(jnp.arange(4 * hd)[None, :] < 3 * hd, wj, 0.0)
    wj_g = (g1 * wj).astype(BF16)
    ww_g = (g2 * ww).astype(BF16)
    shifted = jnp.concatenate([
        jnp.sum(s1 * wj, axis=0) + jnp.pad(jb_own, (0, hd)), jnp.sum(s2 * ww, axis=0) + wb_own])[None, :]
    dense_p = jnp.pad(dense_w, ((3 * hd, 0), (0, 0)))

    both, table, dense_p = tie(both, table, dense_p)
    xhat, joint, att_grad, act, wg, early = project(both, wj_g, ww_g, shifted, back_w)
    early = lax.all_to_all(early, "fsdp", 0, 0, tiled=True)

    mixed = attention(order, joint, table, att_grad)
    core = (c % 2)[None]
    shares = (mixed, wg, act, wj_g, ww_g, dense_p, narrow_w)
    place = lambda parity: jnp.stack([c // 4, (c // 2) % 2, parity]).astype(jnp.int32)
    other = spread(place(1 - c % 2), *shares)
    other, early = tie(other, early)

    early = jnp.sum(early.astype(F32), axis=0)
    bias_grad = early[d_own, ffc:ffc + d_own]
    early_all = lax.all_gather(early.astype(BF16), "ctx", axis=0)
    late, other = tie(late_grads(xhat, both, mixed), move(other, OTHER_CORE))
    near, far, *outs = spread(place(c % 2), *shares, other)

    late, near, far, *outs = tie(lax.all_to_all(late, "fsdp", 0, 0, tiled=True), near, far, *outs)

    wide = lambda v: v.astype(F32)
    low = jnp.sum(wide(late), axis=0).astype(BF16)
    low = jnp.concatenate([low[:, :3 * hd], turn(low[:, 3 * hd:])], axis=1)
    late_mine, far, *outs[1:] = tie(
        gather_chips(low), move(far, ACROSS_Y), *[move(outs[d], AHEAD_Z[d]) for d in range(1, 4)])
    late_all = late_mine, move(late_mine, OTHER_CORE)
    near = (wide(near) + wide(far)).astype(BF16)
    out_own = sum(wide(v) for v in outs)
    across = out_own[1].astype(BF16)
    u_own = wide(near[0]) + sum(wide(move(near[d], AHEAD_Z[d])) for d in range(1, 4))
    out_own = out_own[0] + wide(move(across, ACROSS_Y))

    widen_grad, narrow_grad, g2_grad, s2_grad, wb_shard = finish(
        finish_early_kernel, (f[None],), (early_all,), widen_weight, second_gain, second_shift, (2 * ffc, width))

    own_x = own_tokens.astype(F32)
    block_out = (own_x + out_own + dense_b + narrow_b).astype(BF16)
    own_center = own_x - jnp.mean(own_x, axis=-1, keepdims=True)
    own_rstd = lax.rsqrt(jnp.mean(own_center * own_center, axis=-1, keepdims=True) + EPSILON)
    own_xhat = own_center * own_rstd
    tokens_grad = own_up.astype(F32) + own_rstd * (
        u_own - jnp.mean(u_own, axis=-1, keepdims=True)
        - own_xhat * jnp.mean(u_own * own_xhat, axis=-1, keepdims=True))

    joint_grad, dense_grad, g1_grad, s1_grad, jb_shard = finish(
        finish_late_kernel, (f[None], core), late_all, joint_weight, first_gain, first_shift, (2 * hd, width))
    return (
        block_out[None], tokens_grad[None], g1_grad, s1_grad, joint_grad, jb_shard,
        dense_grad, bias_grad, g2_grad, s2_grad, widen_grad, wb_shard, narrow_grad, bias_grad,
    )


def solution(mesh):
    rows = P("fsdp", "ctx", None)
    vec, mat = P("fsdp"), P("fsdp", None)
    in_specs = (rows, rows, mat, P("fsdp", "ctx"), vec, vec, mat, vec, mat, vec, vec, vec, mat, vec, mat, vec)
    out_specs = (rows, rows, vec, vec, mat, vec, mat, vec, vec, vec, mat, vec, mat, vec)
    return jax.shard_map(shards, mesh=mesh, in_specs=in_specs, out_specs=out_specs, check_vma=False)
```

```python
import jax
import jax.numpy as jnp
from jax import lax
from jax.experimental import pallas as pl
from jax.experimental.pallas import tpu as pltpu
from jax.sharding import PartitionSpec as P

HEADS = 16
EPSILON = 1e-05
NEGATIVE = -1e30
ROTARY_BASE = 10000.0
N_CTX = 16
VMEM = 60 * 1024 * 1024
N_FSDP = 8
F32 = jnp.float32
BF16 = jnp.bfloat16

ACROSS_Y = [(i ^ 2, i) for i in range(16)]
OTHER_CORE = [(i ^ 1, i) for i in range(16)]
AHEAD_Z = [[(i, (i + 4 * d) % 16) for i in range(16)] for d in range(4)]
SAME_CORE = [list(range(0, 16, 2)), list(range(1, 16, 2))]
TURN = [(c * 8 + f, (2 * f + (c & 1)) * 8 + (c >> 1)) for c in range(16) for f in range(8)]


def tie(*arrays):
    return lax.optimization_barrier(arrays)


def turn(v):
    return lax.ppermute(v, ("ctx", "fsdp"), TURN)


def move(v, way):
    return lax.ppermute(v, "ctx", way)


def gather_chips(own):
    return lax.all_to_all(jnp.broadcast_to(own[None], (N_CTX // 2,) + own.shape), "ctx", 0, 0, tiled=True,
                          axis_index_groups=SAME_CORE)


def dot_tn(a, b):
    return lax.dot_general(a, b, (((0,), (0,)), ((), ())), preferred_element_type=F32)


def dot_nt(a, b):
    return lax.dot_general(a, b, (((1,), (1,)), ((), ())), preferred_element_type=F32)


def dot_nn(a, b):
    return jnp.dot(a, b, preferred_element_type=F32)


def project_kernel(x_ref, up_ref, wj_ref, ww_ref, add_ref, back_ref,
                   xhat_ref, joint_ref, grad_ref, act_ref, wg_ref, early_ref, widen_s, narrow_s, wg_sum_s, up_sum_s):
    block, width = x_ref.shape[0] * x_ref.shape[1], x_ref.shape[2]
    i = pl.program_id(0)

    @pl.when(i == 0)
    def _():
        for ref in (widen_s, narrow_s, wg_sum_s, up_sum_s):
            ref[...] = jnp.zeros_like(ref)

    x = x_ref[...].reshape(block, width).astype(F32)
    center = x - jnp.mean(x, axis=-1, keepdims=True)
    xhat = (center * lax.rsqrt(jnp.mean(center * center, axis=-1, keepdims=True) + EPSILON)).astype(BF16)
    xhat_ref[...] = xhat
    wide = wj_ref.shape[1]
    joint_ref[...] = dot_nn(xhat, wj_ref[...]) + add_ref[0:1, :wide]
    widened = dot_nn(xhat, ww_ref[...]) + add_ref[0:1, wide:]
    phi = 0.5 * (1.0 + lax.erf(widened * (0.5 ** 0.5)))
    act = (widened * phi).astype(BF16)
    act_ref[...] = act
    slope = phi + widened * jnp.exp(-0.5 * widened * widened) * 0.3989422804014327
    up = up_ref[...].reshape(block, width)
    k = ww_ref.shape[1]
    hd = back_ref.shape[0] - k
    grad_ref[...] = dot_nt(up, back_ref[0:hd, :])
    wg = (dot_nt(up, back_ref[hd:, :]) * slope).astype(BF16)
    wg_ref[...] = wg
    widen_s[...] += dot_nn(wg.T, xhat)
    narrow_s[...] += dot_nn(act.T, up)
    ones = jnp.ones((16, block), BF16)
    wg_sum_s[...] += dot_nn(ones, wg)
    up_sum_s[...] += dot_nn(ones, up)

    @pl.when(i == pl.num_programs(0) - 1)
    def _():
        n = early_ref.shape[1] - 16
        per = k // N_FSDP
        for f in range(N_FSDP):
            early_ref[f, 0:n, 0:k] = widen_s[:, f * n:(f + 1) * n].T.astype(BF16)
            for q in range(width // k):
                early_ref[f, q * per:(q + 1) * per, k:] = (
                    narrow_s[f * per:(f + 1) * per, q * k:(q + 1) * k].astype(BF16))
            early_ref[f, n:, 0:k] = wg_sum_s[...].astype(BF16)
            early_ref[f, n:, k:k + n] = up_sum_s[:, f * n:(f + 1) * n].astype(BF16)
            early_ref[f, n:, k + n:] = jnp.zeros((16, k - n), BF16)


def project(both, wj, ww, add, back):
    slots, _, width = both.shape
    own, per = 128, 4
    rows, block = slots * own, per * own
    n = width // N_FSDP
    wide, ffc = wj.shape[1], ww.shape[1]
    hd = back.shape[0] - ffc
    whole = lambda a: pl.BlockSpec(a.shape, lambda i: (0, 0))
    tall = lambda n: pl.BlockSpec((block, n), lambda i: (i, 0))
    payload = (N_FSDP, n + 16, 2 * ffc)
    return pl.pallas_call(
        project_kernel,
        grid=(slots // per,),
        in_specs=[
            pl.BlockSpec((per, own, width), lambda i: (i, 0, 0)),
            pl.BlockSpec((per, own, width), lambda i: (i, 1, 0)),
            whole(wj), whole(ww), whole(add), whole(back)],
        out_specs=[tall(width), tall(wide), tall(hd), tall(ffc), tall(ffc),
                   pl.BlockSpec(payload, lambda i: (0, 0, 0))],
        out_shape=[
            jax.ShapeDtypeStruct((rows, width), BF16), jax.ShapeDtypeStruct((rows, wide), F32),
            jax.ShapeDtypeStruct((rows, hd), F32), jax.ShapeDtypeStruct((rows, ffc), BF16),
            jax.ShapeDtypeStruct((rows, ffc), BF16), jax.ShapeDtypeStruct(payload, BF16)],
        scratch_shapes=[pltpu.VMEM((ffc, width), F32), pltpu.VMEM((ffc, width), F32),
                        pltpu.VMEM((16, ffc), F32), pltpu.VMEM((16, width), F32)],
        compiler_params=pltpu.CompilerParams(vmem_limit_bytes=VMEM),
        cost_estimate=pl.CostEstimate(flops=2 * rows * width * 1344, bytes_accessed=20 << 20, transcendentals=rows * 512),
    )(both, both, wj, ww, add, back)


def late_kernel(xhat_ref, up_ref, mixed_ref, out_ref, mixedT_s, sum_s):
    rows, block = xhat_ref.shape
    m = mixed_ref.shape[1]
    n = out_ref.shape[1] - 16
    hd = m // 4

    @pl.when(pl.program_id(0) == 0)
    def _():
        mixedT_s[...] = mixed_ref[...].T
        sum_s[...] = dot_nn(jnp.ones((16, rows), BF16), mixed_ref[...]).astype(BF16)

    joint = dot_nn(mixedT_s[0:3 * hd, :], xhat_ref[...])
    dense = dot_nn(mixedT_s[3 * hd:, :], up_ref[...].reshape(rows, block))
    full = jnp.concatenate([joint, dense], axis=0).T.astype(BF16)
    for b in range(block // n):
        out_ref[b, 0:n, :] = full[b * n:(b + 1) * n]
        out_ref[b, n:, :] = sum_s[...]


def late_grads(xhat, both, mixed):
    rows, width = xhat.shape
    n, m = width // N_FSDP, mixed.shape[1]
    block = 2 * n
    return pl.pallas_call(
        late_kernel,
        grid=(width // block,),
        in_specs=[
            pl.BlockSpec((rows, block), lambda i: (0, i)),
            pl.BlockSpec((both.shape[0], 128, block), lambda i: (0, 1, i)),
            pl.BlockSpec(mixed.shape, lambda i: (0, 0))],
        out_specs=pl.BlockSpec((2, n + 16, m), lambda i: (i, 0, 0)),
        out_shape=jax.ShapeDtypeStruct((N_FSDP, n + 16, m), BF16),
        scratch_shapes=[pltpu.VMEM((m, rows), BF16), pltpu.VMEM((16, m), BF16)],
        compiler_params=pltpu.CompilerParams(vmem_limit_bytes=VMEM),
        cost_estimate=pl.CostEstimate(flops=2 * rows * width * m, bytes_accessed=10 << 20, transcendentals=0),
    )(xhat, both, mixed)


def spread_kernel(place_ref, mixed_ref, wg_ref, act_ref, wj_ref, ww_ref, dense_ref, narrow_ref, *refs):
    chips, own = mixed_ref.shape[0], mixed_ref.shape[2]
    flat = lambda ref: ref[...].reshape(chips * own, ref.shape[3])
    mixed = flat(mixed_ref)
    u = dot_nt(mixed, wj_ref[...]) + dot_nt(flat(wg_ref), ww_ref[...])
    out = dot_nn(mixed, dense_ref[...]) + dot_nn(flat(act_ref), narrow_ref[...])
    u = [u[q * own:(q + 1) * own] for q in range(chips)]
    out = [out[q * own:(q + 1) * own] for q in range(chips)]
    far = [q ^ place_ref[1] for q in range(chips)]
    if len(refs) == 1:
        for q in range(chips):
            refs[0][0, far[q]] = u[q].astype(BF16)
            refs[0][1, far[q]] = out[q].astype(BF16)
        return
    got_ref, near_ref, far_ref = refs[:3]
    u = [(u[q] + got_ref[0, far[q]].astype(F32)).astype(BF16) for q in range(chips)]
    out = [(out[q] + got_ref[1, far[q]].astype(F32)).astype(BF16) for q in range(chips)]
    low = place_ref[1] == 0
    near_ref[0] = jnp.where(low, u[0], u[1])
    far_ref[0] = jnp.where(low, u[1], u[0])
    for d, ref in enumerate(refs[3:]):
        @pl.when(pl.program_id(0) == d)
        def _():
            ref[0] = jnp.where(low, out[0], out[1])
            ref[1] = jnp.where(low, out[1], out[0])


def spread(place, mixed, wg, act, wj, ww, dense, narrow, got=None):
    rows, width = mixed.shape[0], wj.shape[0]
    own, chips, per = rows // N_CTX, N_CTX // 2, 2
    deep = chips // per
    whole = lambda a: pl.BlockSpec(a.shape, lambda i, place: (0, 0))
    split = lambda a: a.reshape(chips, 2, own, a.shape[1])
    tall = lambda a: pl.BlockSpec((per, 1, own, a.shape[1]), lambda i, place: ((place[0] + i) % deep, place[2], 0, 0))
    pair = pl.BlockSpec((2, per, own, width), lambda i, place: (0, i, 0, 0))
    shape = lambda *lead: jax.ShapeDtypeStruct(lead + (own, width), BF16)
    if got is None:
        more, out_specs, out_shape = [], pair, shape(2, chips)
    else:
        more = [got]
        out_specs = ([pl.BlockSpec((1, own, width), lambda i, place: (i, 0, 0))] * 2
                     + [pl.BlockSpec((per, own, width), lambda i, place: (0, 0, 0))] * deep)
        out_shape = [shape(deep)] * 2 + [shape(per)] * deep
    return pl.pallas_call(
        spread_kernel,
        grid_spec=pltpu.PrefetchScalarGridSpec(
            num_scalar_prefetch=1,
            grid=(deep,),
            in_specs=[tall(mixed), tall(wg), tall(act), whole(wj), whole(ww), whole(dense), whole(narrow)]
            + [pair] * len(more),
            out_specs=out_specs),
        out_shape=out_shape,
        compiler_params=pltpu.CompilerParams(vmem_limit_bytes=VMEM),
        cost_estimate=pl.CostEstimate(flops=rows * width * 1024, bytes_accessed=9 << 20, transcendentals=0),
    )(place, split(mixed), split(wg), split(act), wj, ww, dense, narrow, *more)


def finish_early_kernel(f_ref, all_ref, weight_ref, gain_ref, shift_ref,
                        widen_ref, narrow_ref, gain_out, shift_out, bias_out, bias_s):
    n, ff = weight_ref.shape
    k = all_ref.shape[2] // 2
    per = k // N_FSDP
    gain, shift = gain_ref[...], shift_ref[...]
    g_sum = jnp.zeros((n, n), F32)
    s_sum = jnp.zeros((n, n), F32)
    for c in range(N_CTX):
        for q in range(narrow_ref.shape[1] // k):
            narrow_ref[c * per:(c + 1) * per, q * k:(q + 1) * k] = all_ref[c, q * per:(q + 1) * per, k:].astype(F32)
    group = n // per
    for h in range(N_CTX // group):
        parts = [all_ref[h * group + i, :, :k].astype(F32) for i in range(group)]
        for f in range(N_FSDP):
            full = jnp.concatenate([p[:, f * per:(f + 1) * per] for p in parts], axis=1)
            m, bias = full[:n], full[n:n + 1]
            at = f * (ff // N_FSDP) + h * n
            w = weight_ref[:, at:at + n].astype(F32)
            widen_ref[:, at:at + n] = gain * m + shift * bias
            g_sum += w * m
            s_sum += w * bias
            bias_s[:, at:at + n] = full[n:n + 8]
    gain_out[...] = jnp.sum(g_sum.T, axis=0, keepdims=True)
    shift_out[...] = jnp.sum(s_sum.T, axis=0, keepdims=True)
    own = bias_out.shape[1]
    bias_out[...] = bias_s[:, pl.ds(pl.multiple_of(f_ref[0] * own, own), own)][0:1]


def finish_late_kernel(f_ref, core_ref, mine_ref, other_ref, weight_ref, gain_ref, shift_ref,
                       joint_ref, dense_ref, gain_out, shift_out, bias_out, bias_s):
    n = weight_ref.shape[0]
    hd = mine_ref.shape[2] // 4
    width = weight_ref.shape[1] // 3
    even = core_ref[0] == 0
    gain, shift = gain_ref[...], shift_ref[...]
    g_sum = jnp.zeros((n, 2 * hd), F32)
    s_sum = jnp.zeros((n, 2 * hd), F32)
    for q in range(mine_ref.shape[0]):
        mine, other = mine_ref[q].astype(F32), other_ref[q].astype(F32)
        pair = [jnp.where(even, mine, other), jnp.where(even, other, mine)]
        for k in range(3):
            full = jnp.concatenate([p[:, k * hd:(k + 1) * hd] for p in pair], axis=1)
            at = k * width + q * (2 * hd)
            m, bias = full[:n], full[n:n + 1]
            w = weight_ref[:, at:at + 2 * hd].astype(F32)
            joint_ref[:, at:at + 2 * hd] = gain * m + shift * bias
            g_sum += w * m
            s_sum += w * bias
            bias_s[:, at:at + 2 * hd] = full[n:n + 8]
        for b in range(2):
            dense_ref[b * hd:(b + 1) * hd, q * n:(q + 1) * n] = pair[b][:n].T[3 * hd:]
    gain_out[...] = jnp.sum(g_sum.T, axis=0, keepdims=True)
    shift_out[...] = jnp.sum(s_sum.T, axis=0, keepdims=True)
    own = bias_out.shape[1]
    bias_out[...] = bias_s[:, pl.ds(pl.multiple_of(f_ref[0] * own, 128), own)][0:1]


def finish(kernel, places, gathered, weight, gain, shift, side):
    n, columns = weight.shape
    vmem = pl.BlockSpec(memory_space=pltpu.VMEM)
    row = lambda m: jax.ShapeDtypeStruct((1, m), F32)
    wide = lambda v: v.astype(F32)[:, None]
    out = pl.pallas_call(
        kernel,
        in_specs=[pl.BlockSpec(memory_space=pltpu.SMEM)] * len(places) + [vmem] * (len(gathered) + 3),
        out_specs=[vmem] * 5,
        out_shape=[jax.ShapeDtypeStruct(weight.shape, F32), jax.ShapeDtypeStruct(side, F32), row(n), row(n),
                   row(columns // N_FSDP)],
        scratch_shapes=[pltpu.VMEM((8, columns), F32)],
        compiler_params=pltpu.CompilerParams(vmem_limit_bytes=VMEM),
        cost_estimate=pl.CostEstimate(flops=8 * weight.size, bytes_accessed=12 * weight.size, transcendentals=0),
    )(*places, *gathered, weight, wide(gain), wide(shift))
    return out[0], out[1], out[2][0], out[3][0], out[4][0]


def attention_kernel(order_ref, joint_ref, table_ref, grad_ref, out_ref,
                     joint_s, table_s, grad_s, k_s, v_s, qT_s, kT_s, vT_s, gT_s,
                     oT_s, dqT_s, dkT_s, dvT_s, cosT_s, sinT_s, out_s):
    rows, hd = joint_ref.shape[0], joint_ref.shape[1] // 4
    slots, half, tile = N_CTX, rows // (2 * N_CTX), 256
    last = 2 * slots - 1
    for j in range(slots):
        p = order_ref[j]
        for h in range(2):
            src = pl.ds(j * 2 * half + h * half, half)
            dst = pl.ds(pl.multiple_of((p if h == 0 else last - p) * half, half), half)
            joint_s[dst, :] = joint_ref[src, :]
            table_s[dst, :] = table_ref[src, 0:16]
            grad_s[dst, :] = grad_ref[src, :]
    scale = hd ** -0.5

    def spin(t, c, s):
        return jnp.concatenate([t[0:8] * c - t[8:16] * s, t[8:16] * c + t[0:8] * s, t[16:]], axis=0)

    for i in range(rows // tile):
        at = pl.ds(i * tile, tile)
        jT = joint_s[at, :].T
        tT = table_s[at, :].T
        c, s = tT[0:8], tT[8:16]
        cosT_s[:, at] = c
        sinT_s[:, at] = s
        qT = spin(jT[0:hd], c, s).astype(BF16)
        kT = spin(jT[hd:2 * hd], c, s).astype(BF16)
        vT = jT[2 * hd:3 * hd].astype(BF16)
        qT_s[:, at] = (qT.astype(F32) * scale).astype(BF16)
        kT_s[:, at] = kT
        vT_s[:, at] = vT
        k_s[at, :] = kT.astype(F32).T.astype(BF16)
        v_s[at, :] = vT.astype(F32).T.astype(BF16)
        gT_s[:, at] = grad_s[at, :].T.astype(BF16)
    dkT_s[...] = jnp.zeros_like(dkT_s)
    dvT_s[...] = jnp.zeros_like(dvT_s)
    key_at = lax.broadcasted_iota(jnp.int32, (tile, tile), 0)
    query_at = lax.broadcasted_iota(jnp.int32, (tile, tile), 1)
    seen = key_at <= query_at
    dot = lambda a, b: jnp.dot(a, b, preferred_element_type=F32)
    dot_nt = lambda a, b: lax.dot_general(a, b, (((1,), (1,)), ((), ())), preferred_element_type=F32)
    for i in range(rows // tile):
        at = pl.ds(i * tile, tile)
        span = (i + 1) * tile
        upto = pl.ds(0, span)
        qT, gT = qT_s[:, at], gT_s[:, at]
        sT = dot(k_s[upto, :], qT)
        edge = jnp.where(seen, sT[i * tile:], NEGATIVE)
        sT = edge if i == 0 else jnp.concatenate([sT[:i * tile], edge], axis=0)
        largest = jnp.max(sT, axis=0, keepdims=True)
        e = jnp.exp(sT - largest)
        pT = e * (1.0 / jnp.sum(e, axis=0, keepdims=True))
        pT_low = pT.astype(BF16)
        dpT = dot(v_s[upto, :], gT)
        balance = jnp.sum(dpT * pT, axis=0, keepdims=True)
        dsT = (pT * (dpT - balance)).astype(BF16)
        oT_s[:, at] = dot(vT_s[:, upto], pT_low)
        dqT_s[:, at] = dot(kT_s[:, upto], dsT) * scale
        dkT_s[:, upto] += dot_nt(qT, dsT)
        dvT_s[:, upto] += dot_nt(gT, pT_low)
    for i in range(rows // tile):
        at = pl.ds(i * tile, tile)
        c, s = cosT_s[:, at], -sinT_s[:, at]
        full = jnp.concatenate(
            [spin(dqT_s[:, at], c, s), spin(dkT_s[:, at], c, s), dvT_s[:, at], oT_s[:, at]], axis=0)
        out_s[at, :] = full.T.astype(BF16)
    for j in range(slots):
        p = order_ref[j]
        for h in range(2):
            dst = pl.ds(j * 2 * half + h * half, half)
            src = pl.ds(pl.multiple_of((p if h == 0 else last - p) * half, half), half)
            out_ref[dst, :] = out_s[src, :]


def attention(order, joint, table, grad):
    rows, hd = joint.shape[0], joint.shape[1] // 4
    vmem = pl.BlockSpec(memory_space=pltpu.VMEM)
    return pl.pallas_call(
        attention_kernel,
        out_shape=jax.ShapeDtypeStruct((rows, 4 * hd), BF16),
        in_specs=[pl.BlockSpec(memory_space=pltpu.SMEM), vmem, vmem, vmem],
        out_specs=vmem,
        scratch_shapes=[
            pltpu.VMEM((rows, 4 * hd), F32),
            pltpu.VMEM((rows, 16), F32),
            pltpu.VMEM((rows, hd), F32),
            pltpu.VMEM((rows, hd), BF16),
            pltpu.VMEM((rows, hd), BF16),
            pltpu.VMEM((hd, rows), BF16),
            pltpu.VMEM((hd, rows), BF16),
            pltpu.VMEM((hd, rows), BF16),
            pltpu.VMEM((hd, rows), BF16),
            pltpu.VMEM((hd, rows), F32),
            pltpu.VMEM((hd, rows), F32),
            pltpu.VMEM((hd, rows), F32),
            pltpu.VMEM((hd, rows), F32),
            pltpu.VMEM((8, rows), F32),
            pltpu.VMEM((8, rows), F32),
            pltpu.VMEM((rows, 4 * hd), BF16),
        ],
        compiler_params=pltpu.CompilerParams(vmem_limit_bytes=VMEM),
        cost_estimate=pl.CostEstimate(flops=7 * rows * rows * hd, bytes_accessed=8 << 20, transcendentals=rows * rows // 2),
    )(order, joint, table, grad)


def shards(
    tokens, upstream, block_pairs, rotary_place,
    first_gain, first_shift, joint_weight, joint_bias, dense_weight, dense_bias,
    second_gain, second_shift, widen_weight, widen_bias, narrow_weight, narrow_bias,
):
    own_rows, width = tokens.shape[1], tokens.shape[2]
    hd = width // HEADS
    ff = widen_weight.shape[1]
    ffc = ff // N_CTX
    rows = own_rows * N_CTX
    c = lax.axis_index("ctx")
    f = lax.axis_index("fsdp")
    own_tokens, own_up = tokens[0], upstream[0]
    d_own = width // N_FSDP

    per = ffc // N_FSDP
    both = lax.all_gather(jnp.concatenate([own_tokens, own_up], axis=0), "ctx", axis=0)
    joint_part = lax.dynamic_index_in_dim(joint_weight.reshape(d_own, 3, HEADS, hd), c, 2, keepdims=False)
    vectors = jnp.concatenate(
        [v[:, None] for v in (first_gain, first_shift, second_gain, second_shift, dense_bias, narrow_bias)]
        + [joint_bias.reshape(d_own, 3), widen_bias.reshape(d_own, 4), jnp.zeros((d_own, 51), BF16)], axis=1)
    widen_part = [lax.dynamic_slice_in_dim(widen_weight, g * (ff // N_FSDP) + c * per, per, axis=1)
                  for g in range(N_FSDP)]
    narrow_part = lax.dynamic_slice_in_dim(narrow_weight, c * per, per, axis=0)
    narrow_part = jnp.concatenate([narrow_part[:, q * ffc:(q + 1) * ffc] for q in range(width // ffc)], axis=0)
    part = jnp.concatenate([joint_part.reshape(d_own, 3 * hd), vectors] + widen_part + [narrow_part], axis=1)
    slices = lax.all_to_all(jnp.broadcast_to(part[None], (N_FSDP,) + part.shape), "fsdp", 0, 0, tiled=True)
    dense_w = turn(lax.dynamic_slice_in_dim(dense_weight, (c % 2) * hd, hd, axis=0))
    place_all = lax.all_gather(rotary_place[0], "ctx", axis=0, tiled=True).astype(F32)
    narrow_w = jnp.concatenate(
        [slices[:, q * per:(q + 1) * per, 4 * hd + ffc:] for q in range(width // ffc)], axis=2).reshape(ffc, width)
    slices = slices.reshape(width, part.shape[1])
    back_w = jnp.concatenate([dense_w, narrow_w], axis=0)

    lane = jnp.arange(128)[None, :]
    angles = place_all[:, None] * (ROTARY_BASE ** (-2.0 * (lane % 8).astype(F32) / 16))
    table = jnp.where(lane < 8, jnp.cos(angles), jnp.sin(angles))
    order = block_pairs[0]

    wj = slices[:, :4 * hd].astype(F32)
    ww = slices[:, 4 * hd:4 * hd + ffc].astype(F32)
    vec = slices[:, 3 * hd:4 * hd].astype(F32)
    g1, s1, g2, s2 = vec[:, 0:1], vec[:, 1:2], vec[:, 2:3], vec[:, 3:4]
    dense_b, narrow_b = vec[:, 4], vec[:, 5]
    jb_full = vec[:, 6:9].reshape(3, HEADS, hd)
    wb_full = vec[:, 9:13].reshape(ff)
    jb_own = lax.dynamic_index_in_dim(jb_full, c, 1, keepdims=False).reshape(3 * hd)
    wb_own = lax.dynamic_index_in_dim(wb_full.reshape(N_FSDP, N_CTX, per), c, 1, keepdims=False).reshape(ffc)
    wj = jnp.where(jnp.arange(4 * hd)[None, :] < 3 * hd, wj, 0.0)
    wj_g = (g1 * wj).astype(BF16)
    ww_g = (g2 * ww).astype(BF16)
    shifted = jnp.concatenate([
        jnp.sum(s1 * wj, axis=0) + jnp.pad(jb_own, (0, hd)), jnp.sum(s2 * ww, axis=0) + wb_own])[None, :]
    dense_p = jnp.pad(dense_w, ((3 * hd, 0), (0, 0)))

    both, table, dense_p = tie(both, table, dense_p)
    xhat, joint, att_grad, act, wg, early = project(both, wj_g, ww_g, shifted, back_w)
    early = lax.all_to_all(early, "fsdp", 0, 0, tiled=True)

    mixed = attention(order, joint, table, att_grad)
    core = (c % 2)[None]
    shares = (mixed, wg, act, wj_g, ww_g, dense_p, narrow_w)
    place = lambda parity: jnp.stack([c // 4, (c // 2) % 2, parity]).astype(jnp.int32)
    other = spread(place(1 - c % 2), *shares)
    other, early = tie(other, early)

    early = jnp.sum(early.astype(F32), axis=0)
    bias_grad = early[d_own, ffc:ffc + d_own]
    early_all = lax.all_gather(early.astype(BF16), "ctx", axis=0)
    late, other = tie(late_grads(xhat, both, mixed), move(other, OTHER_CORE))
    near, far, *outs = spread(place(c % 2), *shares, other)

    late, near, far, *outs = tie(lax.all_to_all(late, "fsdp", 0, 0, tiled=True), near, far, *outs)

    wide = lambda v: v.astype(F32)
    low = jnp.sum(wide(late), axis=0).astype(BF16)
    low = jnp.concatenate([low[:, :3 * hd], turn(low[:, 3 * hd:])], axis=1)
    late_mine, far, *outs[1:] = tie(
        gather_chips(low), move(far, ACROSS_Y), *[move(outs[d], AHEAD_Z[d]) for d in range(1, 4)])
    late_all = late_mine, move(late_mine, OTHER_CORE)
    near = (wide(near) + wide(far)).astype(BF16)
    out_own = sum(wide(v) for v in outs)
    across = out_own[1].astype(BF16)
    widen_grad, narrow_grad, g2_grad, s2_grad, wb_shard = finish(
        finish_early_kernel, (f[None],), (early_all,), widen_weight, second_gain, second_shift, (2 * ffc, width))

    joint_grad, dense_grad, g1_grad, s1_grad, jb_shard = finish(
        finish_late_kernel, (f[None], core), late_all, joint_weight, first_gain, first_shift, (2 * hd, width))

    moved = [move(near[d], AHEAD_Z[d]) for d in range(1, 4)]
    across, wb_shard, jb_shard, *moved = tie(move(across, ACROSS_Y), wb_shard, jb_shard, *moved)
    u_own = wide(near[0]) + sum(wide(v) for v in moved)
    out_own = out_own[0] + wide(across)
    own_x = own_tokens.astype(F32)
    block_out = (own_x + out_own + dense_b + narrow_b).astype(BF16)
    own_center = own_x - jnp.mean(own_x, axis=-1, keepdims=True)
    own_rstd = lax.rsqrt(jnp.mean(own_center * own_center, axis=-1, keepdims=True) + EPSILON)
    own_xhat = own_center * own_rstd
    tokens_grad = own_up.astype(F32) + own_rstd * (
        u_own - jnp.mean(u_own, axis=-1, keepdims=True)
        - own_xhat * jnp.mean(u_own * own_xhat, axis=-1, keepdims=True))

    return (
        block_out[None], tokens_grad[None], g1_grad, s1_grad, joint_grad, jb_shard,
        dense_grad, bias_grad, g2_grad, s2_grad, widen_grad, wb_shard, narrow_grad, bias_grad,
    )


def solution(mesh):
    rows = P("fsdp", "ctx", None)
    vec, mat = P("fsdp"), P("fsdp", None)
    in_specs = (rows, rows, mat, P("fsdp", "ctx"), vec, vec, mat, vec, mat, vec, vec, vec, mat, vec, mat, vec)
    out_specs = (rows, rows, vec, vec, mat, vec, mat, vec, vec, vec, mat, vec, mat, vec)
    return jax.shard_map(shards, mesh=mesh, in_specs=in_specs, out_specs=out_specs, check_vma=False)
```

```python
import jax
import jax.numpy as jnp
from jax import lax
from jax.experimental import pallas as pl
from jax.experimental.pallas import tpu as pltpu
from jax.sharding import PartitionSpec as P

HEADS = 16
EPSILON = 1e-05
NEGATIVE = -1e30
ROTARY_BASE = 10000.0
N_CTX = 16
VMEM = 60 * 1024 * 1024
N_FSDP = 8
F32 = jnp.float32
BF16 = jnp.bfloat16

ACROSS_Y = [(i ^ 2, i) for i in range(16)]
OTHER_CORE = [(i ^ 1, i) for i in range(16)]
AHEAD_Z = [[(i, (i + 4 * d) % 16) for i in range(16)] for d in range(4)]
SAME_CORE = [list(range(0, 16, 2)), list(range(1, 16, 2))]
TURN = [(c * 8 + f, (2 * f + (c & 1)) * 8 + (c >> 1)) for c in range(16) for f in range(8)]


def tie(*arrays):
    return lax.optimization_barrier(arrays)


def turn(v):
    return lax.ppermute(v, ("ctx", "fsdp"), TURN)


def move(v, way):
    return lax.ppermute(v, "ctx", way)


def gather_chips(own):
    return lax.all_to_all(jnp.broadcast_to(own[None], (N_CTX // 2,) + own.shape), "ctx", 0, 0, tiled=True,
                          axis_index_groups=SAME_CORE)


def dot_tn(a, b):
    return lax.dot_general(a, b, (((0,), (0,)), ((), ())), preferred_element_type=F32)


def dot_nt(a, b):
    return lax.dot_general(a, b, (((1,), (1,)), ((), ())), preferred_element_type=F32)


def dot_nn(a, b):
    return jnp.dot(a, b, preferred_element_type=F32)


def project_kernel(x_ref, up_ref, wj_ref, ww_ref, add_ref, back_ref,
                   xhat_ref, joint_ref, grad_ref, act_ref, wg_ref, early_ref, widen_s, narrow_s, wg_sum_s, up_sum_s):
    block, width = x_ref.shape[0] * x_ref.shape[1], x_ref.shape[2]
    i = pl.program_id(0)

    @pl.when(i == 0)
    def _():
        for ref in (widen_s, narrow_s, wg_sum_s, up_sum_s):
            ref[...] = jnp.zeros_like(ref)

    x = x_ref[...].reshape(block, width).astype(F32)
    center = x - jnp.mean(x, axis=-1, keepdims=True)
    xhat = (center * lax.rsqrt(jnp.mean(center * center, axis=-1, keepdims=True) + EPSILON)).astype(BF16)
    xhat_ref[...] = xhat
    wide = wj_ref.shape[1]
    joint_ref[...] = dot_nn(xhat, wj_ref[...]) + add_ref[0:1, :wide]
    widened = dot_nn(xhat, ww_ref[...]) + add_ref[0:1, wide:]
    phi = 0.5 * (1.0 + lax.erf(widened * (0.5 ** 0.5)))
    act = (widened * phi).astype(BF16)
    act_ref[...] = act
    slope = phi + widened * jnp.exp(-0.5 * widened * widened) * 0.3989422804014327
    up = up_ref[...].reshape(block, width)
    k = ww_ref.shape[1]
    hd = back_ref.shape[0] - k
    grad_ref[...] = dot_nt(up, back_ref[0:hd, :])
    wg = (dot_nt(up, back_ref[hd:, :]) * slope).astype(BF16)
    wg_ref[...] = wg
    widen_s[...] += dot_nn(wg.T, xhat)
    narrow_s[...] += dot_nn(act.T, up)
    ones = jnp.ones((16, block), BF16)
    wg_sum_s[...] += dot_nn(ones, wg)
    up_sum_s[...] += dot_nn(ones, up)

    @pl.when(i == pl.num_programs(0) - 1)
    def _():
        n = early_ref.shape[1] - 16
        per = k // N_FSDP
        for f in range(N_FSDP):
            early_ref[f, 0:n, 0:k] = widen_s[:, f * n:(f + 1) * n].T.astype(BF16)
            for q in range(width // k):
                early_ref[f, q * per:(q + 1) * per, k:] = (
                    narrow_s[f * per:(f + 1) * per, q * k:(q + 1) * k].astype(BF16))
            early_ref[f, n:, 0:k] = wg_sum_s[...].astype(BF16)
            early_ref[f, n:, k:k + n] = up_sum_s[:, f * n:(f + 1) * n].astype(BF16)
            early_ref[f, n:, k + n:] = jnp.zeros((16, k - n), BF16)


def project(both, wj, ww, add, back):
    slots, _, width = both.shape
    own, per = 128, 4
    rows, block = slots * own, per * own
    n = width // N_FSDP
    wide, ffc = wj.shape[1], ww.shape[1]
    hd = back.shape[0] - ffc
    whole = lambda a: pl.BlockSpec(a.shape, lambda i: (0, 0))
    tall = lambda n: pl.BlockSpec((block, n), lambda i: (i, 0))
    payload = (N_FSDP, n + 16, 2 * ffc)
    return pl.pallas_call(
        project_kernel,
        grid=(slots // per,),
        in_specs=[
            pl.BlockSpec((per, own, width), lambda i: (i, 0, 0)),
            pl.BlockSpec((per, own, width), lambda i: (i, 1, 0)),
            whole(wj), whole(ww), whole(add), whole(back)],
        out_specs=[tall(width), tall(wide), tall(hd), tall(ffc), tall(ffc),
                   pl.BlockSpec(payload, lambda i: (0, 0, 0))],
        out_shape=[
            jax.ShapeDtypeStruct((rows, width), BF16), jax.ShapeDtypeStruct((rows, wide), F32),
            jax.ShapeDtypeStruct((rows, hd), F32), jax.ShapeDtypeStruct((rows, ffc), BF16),
            jax.ShapeDtypeStruct((rows, ffc), BF16), jax.ShapeDtypeStruct(payload, BF16)],
        scratch_shapes=[pltpu.VMEM((ffc, width), F32), pltpu.VMEM((ffc, width), F32),
                        pltpu.VMEM((16, ffc), F32), pltpu.VMEM((16, width), F32)],
        compiler_params=pltpu.CompilerParams(vmem_limit_bytes=VMEM),
        cost_estimate=pl.CostEstimate(flops=2 * rows * width * 1344, bytes_accessed=20 << 20, transcendentals=rows * 512),
    )(both, both, wj, ww, add, back)


def late_kernel(xhat_ref, up_ref, mixed_ref, out_ref, mixedT_s, sum_s):
    rows, block = xhat_ref.shape
    m = mixed_ref.shape[1]
    n = out_ref.shape[1] - 16
    hd = m // 4

    @pl.when(pl.program_id(0) == 0)
    def _():
        mixedT_s[...] = mixed_ref[...].T
        sum_s[...] = dot_nn(jnp.ones((16, rows), BF16), mixed_ref[...]).astype(BF16)

    joint = dot_nn(mixedT_s[0:3 * hd, :], xhat_ref[...])
    dense = dot_nn(mixedT_s[3 * hd:, :], up_ref[...].reshape(rows, block))
    full = jnp.concatenate([joint, dense], axis=0).T.astype(BF16)
    for b in range(block // n):
        out_ref[b, 0:n, :] = full[b * n:(b + 1) * n]
        out_ref[b, n:, :] = sum_s[...]


def late_grads(xhat, both, mixed):
    rows, width = xhat.shape
    n, m = width // N_FSDP, mixed.shape[1]
    block = 2 * n
    return pl.pallas_call(
        late_kernel,
        grid=(width // block,),
        in_specs=[
            pl.BlockSpec((rows, block), lambda i: (0, i)),
            pl.BlockSpec((both.shape[0], 128, block), lambda i: (0, 1, i)),
            pl.BlockSpec(mixed.shape, lambda i: (0, 0))],
        out_specs=pl.BlockSpec((2, n + 16, m), lambda i: (i, 0, 0)),
        out_shape=jax.ShapeDtypeStruct((N_FSDP, n + 16, m), BF16),
        scratch_shapes=[pltpu.VMEM((m, rows), BF16), pltpu.VMEM((16, m), BF16)],
        compiler_params=pltpu.CompilerParams(vmem_limit_bytes=VMEM),
        cost_estimate=pl.CostEstimate(flops=2 * rows * width * m, bytes_accessed=10 << 20, transcendentals=0),
    )(xhat, both, mixed)


def spread_kernel(place_ref, mixed_ref, wg_ref, act_ref, wj_ref, ww_ref, dense_ref, narrow_ref, *refs):
    chips, own = mixed_ref.shape[0], mixed_ref.shape[2]
    flat = lambda ref: ref[...].reshape(chips * own, ref.shape[3])
    mixed = flat(mixed_ref)
    u = dot_nt(mixed, wj_ref[...]) + dot_nt(flat(wg_ref), ww_ref[...])
    out = dot_nn(mixed, dense_ref[...]) + dot_nn(flat(act_ref), narrow_ref[...])
    u = [u[q * own:(q + 1) * own] for q in range(chips)]
    out = [out[q * own:(q + 1) * own] for q in range(chips)]
    far = [q ^ place_ref[1] for q in range(chips)]
    if len(refs) == 1:
        for q in range(chips):
            refs[0][0, far[q]] = u[q].astype(BF16)
            refs[0][1, far[q]] = out[q].astype(BF16)
        return
    got_ref, near_ref, far_ref = refs[:3]
    u = [(u[q] + got_ref[0, far[q]].astype(F32)).astype(BF16) for q in range(chips)]
    out = [(out[q] + got_ref[1, far[q]].astype(F32)).astype(BF16) for q in range(chips)]
    low = place_ref[1] == 0
    near_ref[0] = jnp.where(low, u[0], u[1])
    far_ref[0] = jnp.where(low, u[1], u[0])
    for d, ref in enumerate(refs[3:]):
        @pl.when(pl.program_id(0) == d)
        def _():
            ref[0] = jnp.where(low, out[0], out[1])
            ref[1] = jnp.where(low, out[1], out[0])


def spread(place, mixed, wg, act, wj, ww, dense, narrow, got=None):
    rows, width = mixed.shape[0], wj.shape[0]
    own, chips, per = rows // N_CTX, N_CTX // 2, 2
    deep = chips // per
    whole = lambda a: pl.BlockSpec(a.shape, lambda i, place: (0, 0))
    split = lambda a: a.reshape(chips, 2, own, a.shape[1])
    tall = lambda a: pl.BlockSpec((per, 1, own, a.shape[1]), lambda i, place: ((place[0] + i) % deep, place[2], 0, 0))
    pair = pl.BlockSpec((2, per, own, width), lambda i, place: (0, i, 0, 0))
    shape = lambda *lead: jax.ShapeDtypeStruct(lead + (own, width), BF16)
    if got is None:
        more, out_specs, out_shape = [], pair, shape(2, chips)
    else:
        more = [got]
        out_specs = ([pl.BlockSpec((1, own, width), lambda i, place: (i, 0, 0))] * 2
                     + [pl.BlockSpec((per, own, width), lambda i, place: (0, 0, 0))] * deep)
        out_shape = [shape(deep)] * 2 + [shape(per)] * deep
    return pl.pallas_call(
        spread_kernel,
        grid_spec=pltpu.PrefetchScalarGridSpec(
            num_scalar_prefetch=1,
            grid=(deep,),
            in_specs=[tall(mixed), tall(wg), tall(act), whole(wj), whole(ww), whole(dense), whole(narrow)]
            + [pair] * len(more),
            out_specs=out_specs),
        out_shape=out_shape,
        compiler_params=pltpu.CompilerParams(vmem_limit_bytes=VMEM),
        cost_estimate=pl.CostEstimate(flops=rows * width * 1024, bytes_accessed=9 << 20, transcendentals=0),
    )(place, split(mixed), split(wg), split(act), wj, ww, dense, narrow, *more)


def finish_early_kernel(f_ref, all_ref, weight_ref, gain_ref, shift_ref,
                        widen_ref, narrow_ref, gain_out, shift_out, bias_out, bias_s):
    n, ff = weight_ref.shape
    k = all_ref.shape[2] // 2
    per = k // N_FSDP
    gain, shift = gain_ref[...], shift_ref[...]
    g_sum = jnp.zeros((n, n), F32)
    s_sum = jnp.zeros((n, n), F32)
    for c in range(N_CTX):
        for q in range(narrow_ref.shape[1] // k):
            narrow_ref[c * per:(c + 1) * per, q * k:(q + 1) * k] = all_ref[c, q * per:(q + 1) * per, k:].astype(F32)
    group = n // per
    for h in range(N_CTX // group):
        parts = [all_ref[h * group + i, :, :k].astype(F32) for i in range(group)]
        for f in range(N_FSDP):
            full = jnp.concatenate([p[:, f * per:(f + 1) * per] for p in parts], axis=1)
            m, bias = full[:n], full[n:n + 1]
            at = f * (ff // N_FSDP) + h * n
            w = weight_ref[:, at:at + n].astype(F32)
            widen_ref[:, at:at + n] = gain * m + shift * bias
            g_sum += w * m
            s_sum += w * bias
            bias_s[:, at:at + n] = full[n:n + 8]
    gain_out[...] = jnp.sum(g_sum.T, axis=0, keepdims=True)
    shift_out[...] = jnp.sum(s_sum.T, axis=0, keepdims=True)
    own = bias_out.shape[1]
    bias_out[...] = bias_s[:, pl.ds(pl.multiple_of(f_ref[0] * own, own), own)][0:1]


def finish_late_kernel(f_ref, core_ref, mine_ref, other_ref, weight_ref, gain_ref, shift_ref,
                       joint_ref, dense_ref, gain_out, shift_out, bias_out, bias_s):
    n = weight_ref.shape[0]
    hd = mine_ref.shape[2] // 4
    width = weight_ref.shape[1] // 3
    even = core_ref[0] == 0
    gain, shift = gain_ref[...], shift_ref[...]
    g_sum = jnp.zeros((n, 2 * hd), F32)
    s_sum = jnp.zeros((n, 2 * hd), F32)
    for q in range(mine_ref.shape[0]):
        mine, other = mine_ref[q].astype(F32), other_ref[q].astype(F32)
        pair = [jnp.where(even, mine, other), jnp.where(even, other, mine)]
        for k in range(3):
            full = jnp.concatenate([p[:, k * hd:(k + 1) * hd] for p in pair], axis=1)
            at = k * width + q * (2 * hd)
            m, bias = full[:n], full[n:n + 1]
            w = weight_ref[:, at:at + 2 * hd].astype(F32)
            joint_ref[:, at:at + 2 * hd] = gain * m + shift * bias
            g_sum += w * m
            s_sum += w * bias
            bias_s[:, at:at + 2 * hd] = full[n:n + 8]
        for b in range(2):
            dense_ref[b * hd:(b + 1) * hd, q * n:(q + 1) * n] = pair[b][:n].T[3 * hd:]
    gain_out[...] = jnp.sum(g_sum.T, axis=0, keepdims=True)
    shift_out[...] = jnp.sum(s_sum.T, axis=0, keepdims=True)
    own = bias_out.shape[1]
    bias_out[...] = bias_s[:, pl.ds(pl.multiple_of(f_ref[0] * own, 128), own)][0:1]


def finish(kernel, places, gathered, weight, gain, shift, side):
    n, columns = weight.shape
    vmem = pl.BlockSpec(memory_space=pltpu.VMEM)
    row = lambda m: jax.ShapeDtypeStruct((1, m), F32)
    wide = lambda v: v.astype(F32)[:, None]
    out = pl.pallas_call(
        kernel,
        in_specs=[pl.BlockSpec(memory_space=pltpu.SMEM)] * len(places) + [vmem] * (len(gathered) + 3),
        out_specs=[vmem] * 5,
        out_shape=[jax.ShapeDtypeStruct(weight.shape, F32), jax.ShapeDtypeStruct(side, F32), row(n), row(n),
                   row(columns // N_FSDP)],
        scratch_shapes=[pltpu.VMEM((8, columns), F32)],
        compiler_params=pltpu.CompilerParams(vmem_limit_bytes=VMEM),
        cost_estimate=pl.CostEstimate(flops=8 * weight.size, bytes_accessed=12 * weight.size, transcendentals=0),
    )(*places, *gathered, weight, wide(gain), wide(shift))
    return out[0], out[1], out[2][0], out[3][0], out[4][0]


def attention_kernel(order_ref, joint_ref, table_ref, grad_ref, out_ref,
                     joint_s, table_s, grad_s, k_s, v_s, qT_s, kT_s, vT_s, gT_s,
                     oT_s, dqT_s, dkT_s, dvT_s, cosT_s, sinT_s, out_s):
    rows, hd = joint_ref.shape[0], joint_ref.shape[1] // 4
    slots, half, tile = N_CTX, rows // (2 * N_CTX), 256
    last = 2 * slots - 1
    for j in range(slots):
        p = order_ref[j]
        for h in range(2):
            src = pl.ds(j * 2 * half + h * half, half)
            dst = pl.ds(pl.multiple_of((p if h == 0 else last - p) * half, half), half)
            joint_s[dst, :] = joint_ref[src, :]
            table_s[dst, :] = table_ref[src, 0:16]
            grad_s[dst, :] = grad_ref[src, :]
    scale = hd ** -0.5

    def spin(t, c, s):
        return jnp.concatenate([t[0:8] * c - t[8:16] * s, t[8:16] * c + t[0:8] * s, t[16:]], axis=0)

    for i in range(rows // tile):
        at = pl.ds(i * tile, tile)
        jT = joint_s[at, :].T
        tT = table_s[at, :].T
        c, s = tT[0:8], tT[8:16]
        cosT_s[:, at] = c
        sinT_s[:, at] = s
        qT = spin(jT[0:hd], c, s).astype(BF16)
        kT = spin(jT[hd:2 * hd], c, s).astype(BF16)
        vT = jT[2 * hd:3 * hd].astype(BF16)
        qT_s[:, at] = (qT.astype(F32) * scale).astype(BF16)
        kT_s[:, at] = kT
        vT_s[:, at] = vT
        k_s[at, :] = kT.astype(F32).T.astype(BF16)
        v_s[at, :] = vT.astype(F32).T.astype(BF16)
        gT_s[:, at] = grad_s[at, :].T.astype(BF16)
    dkT_s[...] = jnp.zeros_like(dkT_s)
    dvT_s[...] = jnp.zeros_like(dvT_s)
    key_at = lax.broadcasted_iota(jnp.int32, (tile, tile), 0)
    query_at = lax.broadcasted_iota(jnp.int32, (tile, tile), 1)
    seen = key_at <= query_at
    dot = lambda a, b: jnp.dot(a, b, preferred_element_type=F32)
    dot_nt = lambda a, b: lax.dot_general(a, b, (((1,), (1,)), ((), ())), preferred_element_type=F32)
    for i in range(rows // tile):
        at = pl.ds(i * tile, tile)
        span = (i + 1) * tile
        upto = pl.ds(0, span)
        qT, gT = qT_s[:, at], gT_s[:, at]
        sT = dot(k_s[upto, :], qT)
        edge = jnp.where(seen, sT[i * tile:], NEGATIVE)
        sT = edge if i == 0 else jnp.concatenate([sT[:i * tile], edge], axis=0)
        largest = jnp.max(sT, axis=0, keepdims=True)
        e = jnp.exp(sT - largest)
        pT = e * (1.0 / jnp.sum(e, axis=0, keepdims=True))
        pT_low = pT.astype(BF16)
        dpT = dot(v_s[upto, :], gT)
        balance = jnp.sum(dpT * pT, axis=0, keepdims=True)
        dsT = (pT * (dpT - balance)).astype(BF16)
        oT_s[:, at] = dot(vT_s[:, upto], pT_low)
        dqT_s[:, at] = dot(kT_s[:, upto], dsT) * scale
        dkT_s[:, upto] += dot_nt(qT, dsT)
        dvT_s[:, upto] += dot_nt(gT, pT_low)
    for i in range(rows // tile):
        at = pl.ds(i * tile, tile)
        c, s = cosT_s[:, at], -sinT_s[:, at]
        full = jnp.concatenate(
            [spin(dqT_s[:, at], c, s), spin(dkT_s[:, at], c, s), dvT_s[:, at], oT_s[:, at]], axis=0)
        out_s[at, :] = full.T.astype(BF16)
    for j in range(slots):
        p = order_ref[j]
        for h in range(2):
            dst = pl.ds(j * 2 * half + h * half, half)
            src = pl.ds(pl.multiple_of((p if h == 0 else last - p) * half, half), half)
            out_ref[dst, :] = out_s[src, :]


def attention(order, joint, table, grad):
    rows, hd = joint.shape[0], joint.shape[1] // 4
    vmem = pl.BlockSpec(memory_space=pltpu.VMEM)
    return pl.pallas_call(
        attention_kernel,
        out_shape=jax.ShapeDtypeStruct((rows, 4 * hd), BF16),
        in_specs=[pl.BlockSpec(memory_space=pltpu.SMEM), vmem, vmem, vmem],
        out_specs=vmem,
        scratch_shapes=[
            pltpu.VMEM((rows, 4 * hd), F32),
            pltpu.VMEM((rows, 16), F32),
            pltpu.VMEM((rows, hd), F32),
            pltpu.VMEM((rows, hd), BF16),
            pltpu.VMEM((rows, hd), BF16),
            pltpu.VMEM((hd, rows), BF16),
            pltpu.VMEM((hd, rows), BF16),
            pltpu.VMEM((hd, rows), BF16),
            pltpu.VMEM((hd, rows), BF16),
            pltpu.VMEM((hd, rows), F32),
            pltpu.VMEM((hd, rows), F32),
            pltpu.VMEM((hd, rows), F32),
            pltpu.VMEM((hd, rows), F32),
            pltpu.VMEM((8, rows), F32),
            pltpu.VMEM((8, rows), F32),
            pltpu.VMEM((rows, 4 * hd), BF16),
        ],
        compiler_params=pltpu.CompilerParams(vmem_limit_bytes=VMEM),
        cost_estimate=pl.CostEstimate(flops=7 * rows * rows * hd, bytes_accessed=8 << 20, transcendentals=rows * rows // 2),
    )(order, joint, table, grad)


def shards(
    tokens, upstream, block_pairs, rotary_place,
    first_gain, first_shift, joint_weight, joint_bias, dense_weight, dense_bias,
    second_gain, second_shift, widen_weight, widen_bias, narrow_weight, narrow_bias,
):
    own_rows, width = tokens.shape[1], tokens.shape[2]
    hd = width // HEADS
    ff = widen_weight.shape[1]
    ffc = ff // N_CTX
    rows = own_rows * N_CTX
    c = lax.axis_index("ctx")
    f = lax.axis_index("fsdp")
    own_tokens, own_up = tokens[0], upstream[0]
    d_own = width // N_FSDP

    per = ffc // N_FSDP
    both = lax.all_gather(jnp.concatenate([own_tokens, own_up], axis=0), "ctx", axis=0)
    joint_part = lax.dynamic_index_in_dim(joint_weight.reshape(d_own, 3, HEADS, hd), c, 2, keepdims=False)
    vectors = jnp.concatenate(
        [v[:, None] for v in (first_gain, first_shift, second_gain, second_shift, dense_bias, narrow_bias)]
        + [joint_bias.reshape(d_own, 3), widen_bias.reshape(d_own, 4), jnp.zeros((d_own, 51), BF16)], axis=1)
    widen_part = [lax.dynamic_slice_in_dim(widen_weight, g * (ff // N_FSDP) + c * per, per, axis=1)
                  for g in range(N_FSDP)]
    narrow_part = lax.dynamic_slice_in_dim(narrow_weight, c * per, per, axis=0)
    narrow_part = jnp.concatenate([narrow_part[:, q * ffc:(q + 1) * ffc] for q in range(width // ffc)], axis=0)
    part = jnp.concatenate([joint_part.reshape(d_own, 3 * hd), vectors] + widen_part + [narrow_part], axis=1)
    slices = lax.all_to_all(jnp.broadcast_to(part[None], (N_FSDP,) + part.shape), "fsdp", 0, 0, tiled=True)
    dense_w = turn(lax.dynamic_slice_in_dim(dense_weight, (c % 2) * hd, hd, axis=0))
    place_all = lax.all_gather(rotary_place[0], "ctx", axis=0, tiled=True).astype(F32)
    narrow_w = jnp.concatenate(
        [slices[:, q * per:(q + 1) * per, 4 * hd + ffc:] for q in range(width // ffc)], axis=2).reshape(ffc, width)
    slices = slices.reshape(width, part.shape[1])
    back_w = jnp.concatenate([dense_w, narrow_w], axis=0)

    lane = jnp.arange(128)[None, :]
    angles = place_all[:, None] * (ROTARY_BASE ** (-2.0 * (lane % 8).astype(F32) / 16))
    table = jnp.where(lane < 8, jnp.cos(angles), jnp.sin(angles))
    order = block_pairs[0]

    wj = slices[:, :4 * hd].astype(F32)
    ww = slices[:, 4 * hd:4 * hd + ffc].astype(F32)
    vec = slices[:, 3 * hd:4 * hd].astype(F32)
    g1, s1, g2, s2 = vec[:, 0:1], vec[:, 1:2], vec[:, 2:3], vec[:, 3:4]
    dense_b, narrow_b = vec[:, 4], vec[:, 5]
    jb_full = vec[:, 6:9].reshape(3, HEADS, hd)
    wb_full = vec[:, 9:13].reshape(ff)
    jb_own = lax.dynamic_index_in_dim(jb_full, c, 1, keepdims=False).reshape(3 * hd)
    wb_own = lax.dynamic_index_in_dim(wb_full.reshape(N_FSDP, N_CTX, per), c, 1, keepdims=False).reshape(ffc)
    wj = jnp.where(jnp.arange(4 * hd)[None, :] < 3 * hd, wj, 0.0)
    wj_g = (g1 * wj).astype(BF16)
    ww_g = (g2 * ww).astype(BF16)
    shifted = jnp.concatenate([
        jnp.sum(s1 * wj, axis=0) + jnp.pad(jb_own, (0, hd)), jnp.sum(s2 * ww, axis=0) + wb_own])[None, :]
    dense_p = jnp.pad(dense_w, ((3 * hd, 0), (0, 0)))

    both, table, dense_p = tie(both, table, dense_p)
    xhat, joint, att_grad, act, wg, early = project(both, wj_g, ww_g, shifted, back_w)
    early = lax.all_to_all(early, "fsdp", 0, 0, tiled=True)

    mixed = attention(order, joint, table, att_grad)
    core = (c % 2)[None]
    shares = (mixed, wg, act, wj_g, ww_g, dense_p, narrow_w)
    place = lambda parity: jnp.stack([c // 4, (c // 2) % 2, parity]).astype(jnp.int32)
    other = spread(place(1 - c % 2), *shares)
    other, early = tie(other, early)

    early = jnp.sum(early.astype(F32), axis=0)
    bias_grad = early[d_own, ffc:ffc + d_own]
    early_all = lax.all_gather(early.astype(BF16), "ctx", axis=0)
    late, other = tie(late_grads(xhat, both, mixed), move(other, OTHER_CORE))
    near, far, *outs = spread(place(c % 2), *shares, other)

    late, near, far, *outs = tie(lax.all_to_all(late, "fsdp", 0, 0, tiled=True), near, far, *outs)

    wide = lambda v: v.astype(F32)
    low = jnp.sum(wide(late), axis=0).astype(BF16)
    low = jnp.concatenate([low[:, :3 * hd], turn(low[:, 3 * hd:])], axis=1)
    widen_grad, narrow_grad, g2_grad, s2_grad, wb_shard = finish(
        finish_early_kernel, (f[None],), (early_all,), widen_weight, second_gain, second_shift, (2 * ffc, width))
    late_mine, wb_shard, far, *outs[1:] = tie(
        gather_chips(low), wb_shard, move(far, ACROSS_Y), *[move(outs[d], AHEAD_Z[d]) for d in range(1, 4)])
    late_all = late_mine, move(late_mine, OTHER_CORE)
    near = (wide(near) + wide(far)).astype(BF16)
    out_own = sum(wide(v) for v in outs)
    across = out_own[1].astype(BF16)
    joint_grad, dense_grad, g1_grad, s1_grad, jb_shard = finish(
        finish_late_kernel, (f[None], core), late_all, joint_weight, first_gain, first_shift, (2 * hd, width))

    moved = [move(near[d], AHEAD_Z[d]) for d in range(1, 4)]
    across, jb_shard, *moved = tie(move(across, ACROSS_Y), jb_shard, *moved)
    u_own = wide(near[0]) + sum(wide(v) for v in moved)
    out_own = out_own[0] + wide(across)
    own_x = own_tokens.astype(F32)
    block_out = (own_x + out_own + dense_b + narrow_b).astype(BF16)
    own_center = own_x - jnp.mean(own_x, axis=-1, keepdims=True)
    own_rstd = lax.rsqrt(jnp.mean(own_center * own_center, axis=-1, keepdims=True) + EPSILON)
    own_xhat = own_center * own_rstd
    tokens_grad = own_up.astype(F32) + own_rstd * (
        u_own - jnp.mean(u_own, axis=-1, keepdims=True)
        - own_xhat * jnp.mean(u_own * own_xhat, axis=-1, keepdims=True))

    return (
        block_out[None], tokens_grad[None], g1_grad, s1_grad, joint_grad, jb_shard,
        dense_grad, bias_grad, g2_grad, s2_grad, widen_grad, wb_shard, narrow_grad, bias_grad,
    )


def solution(mesh):
    rows = P("fsdp", "ctx", None)
    vec, mat = P("fsdp"), P("fsdp", None)
    in_specs = (rows, rows, mat, P("fsdp", "ctx"), vec, vec, mat, vec, mat, vec, vec, vec, mat, vec, mat, vec)
    out_specs = (rows, rows, vec, vec, mat, vec, mat, vec, vec, vec, mat, vec, mat, vec)
    return jax.shard_map(shards, mesh=mesh, in_specs=in_specs, out_specs=out_specs, check_vma=False)
```

```python
import jax
import jax.numpy as jnp
from jax import lax
from jax.experimental import pallas as pl
from jax.experimental.pallas import tpu as pltpu
from jax.sharding import PartitionSpec as P

HEADS = 16
EPSILON = 1e-05
NEGATIVE = -1e30
ROTARY_BASE = 10000.0
N_CTX = 16
VMEM = 60 * 1024 * 1024
N_FSDP = 8
F32 = jnp.float32
BF16 = jnp.bfloat16

ACROSS_Y = [(i ^ 2, i) for i in range(16)]
OTHER_CORE = [(i ^ 1, i) for i in range(16)]
AHEAD_Z = [[(i, (i + 4 * d) % 16) for i in range(16)] for d in range(4)]
SAME_CORE = [list(range(0, 16, 2)), list(range(1, 16, 2))]
TURN = [(c * 8 + f, (2 * f + (c & 1)) * 8 + (c >> 1)) for c in range(16) for f in range(8)]


def tie(*arrays):
    return lax.optimization_barrier(arrays)


def turn(v):
    return lax.ppermute(v, ("ctx", "fsdp"), TURN)


def move(v, way):
    return lax.ppermute(v, "ctx", way)


def gather_chips(own):
    return lax.all_to_all(jnp.broadcast_to(own[None], (N_CTX // 2,) + own.shape), "ctx", 0, 0, tiled=True,
                          axis_index_groups=SAME_CORE)


def dot_tn(a, b):
    return lax.dot_general(a, b, (((0,), (0,)), ((), ())), preferred_element_type=F32)


def dot_nt(a, b):
    return lax.dot_general(a, b, (((1,), (1,)), ((), ())), preferred_element_type=F32)


def dot_nn(a, b):
    return jnp.dot(a, b, preferred_element_type=F32)


def project_kernel(x_ref, up_ref, wj_ref, ww_ref, add_ref, back_ref, table_ref,
                   xhat_ref, joint_ref, act_ref, wg_ref, early_ref, widen_s, narrow_s, wg_sum_s, up_sum_s):
    block, width = x_ref.shape[0] * x_ref.shape[1], x_ref.shape[2]
    i = pl.program_id(0)

    @pl.when(i == 0)
    def _():
        for ref in (widen_s, narrow_s, wg_sum_s, up_sum_s):
            ref[...] = jnp.zeros_like(ref)

    x = x_ref[...].reshape(block, width).astype(F32)
    center = x - jnp.mean(x, axis=-1, keepdims=True)
    xhat = (center * lax.rsqrt(jnp.mean(center * center, axis=-1, keepdims=True) + EPSILON)).astype(BF16)
    xhat_ref[...] = xhat
    wide = wj_ref.shape[1]
    joint_ref[:, :wide] = dot_nn(xhat, wj_ref[...]) + add_ref[0:1, :wide]
    widened = dot_nn(xhat, ww_ref[...]) + add_ref[0:1, wide:]
    phi = 0.5 * (1.0 + lax.erf(widened * (0.5 ** 0.5)))
    act = (widened * phi).astype(BF16)
    act_ref[...] = act
    slope = phi + widened * jnp.exp(-0.5 * widened * widened) * 0.3989422804014327
    up = up_ref[...].reshape(block, width)
    k = ww_ref.shape[1]
    hd = back_ref.shape[0] - k
    joint_ref[:, 3 * hd:4 * hd] = dot_nt(up, back_ref[0:hd, :])
    joint_ref[:, wide:wide + table_ref.shape[1]] = table_ref[...]
    wg = (dot_nt(up, back_ref[hd:, :]) * slope).astype(BF16)
    wg_ref[...] = wg
    widen_s[...] += dot_nn(wg.T, xhat)
    narrow_s[...] += dot_nn(act.T, up)
    ones = jnp.ones((16, block), BF16)
    wg_sum_s[...] += dot_nn(ones, wg)
    up_sum_s[...] += dot_nn(ones, up)

    @pl.when(i == pl.num_programs(0) - 1)
    def _():
        n = early_ref.shape[1] - 16
        per = k // N_FSDP
        for f in range(N_FSDP):
            early_ref[f, 0:n, 0:k] = widen_s[:, f * n:(f + 1) * n].T.astype(BF16)
            for q in range(width // k):
                early_ref[f, q * per:(q + 1) * per, k:] = (
                    narrow_s[f * per:(f + 1) * per, q * k:(q + 1) * k].astype(BF16))
            early_ref[f, n:, 0:k] = wg_sum_s[...].astype(BF16)
            early_ref[f, n:, k:k + n] = up_sum_s[:, f * n:(f + 1) * n].astype(BF16)
            early_ref[f, n:, k + n:] = jnp.zeros((16, k - n), BF16)


def project(both, wj, ww, add, back, table):
    slots, _, width = both.shape
    own, per = 128, 4
    rows, block = slots * own, per * own
    n = width // N_FSDP
    wide, ffc = wj.shape[1], ww.shape[1]
    whole = lambda a: pl.BlockSpec(a.shape, lambda i: (0, 0))
    tall = lambda n: pl.BlockSpec((block, n), lambda i: (i, 0))
    payload = (N_FSDP, n + 16, 2 * ffc)
    return pl.pallas_call(
        project_kernel,
        grid=(slots // per,),
        in_specs=[
            pl.BlockSpec((per, own, width), lambda i: (i, 0, 0)),
            pl.BlockSpec((per, own, width), lambda i: (i, 1, 0)),
            whole(wj), whole(ww), whole(add), whole(back), tall(table.shape[1])],
        out_specs=[tall(width), tall(wide + 128), tall(ffc), tall(ffc),
                   pl.BlockSpec(payload, lambda i: (0, 0, 0))],
        out_shape=[
            jax.ShapeDtypeStruct((rows, width), BF16), jax.ShapeDtypeStruct((rows, wide + 128), F32),
            jax.ShapeDtypeStruct((rows, ffc), BF16),
            jax.ShapeDtypeStruct((rows, ffc), BF16), jax.ShapeDtypeStruct(payload, BF16)],
        scratch_shapes=[pltpu.VMEM((ffc, width), F32), pltpu.VMEM((ffc, width), F32),
                        pltpu.VMEM((16, ffc), F32), pltpu.VMEM((16, width), F32)],
        compiler_params=pltpu.CompilerParams(vmem_limit_bytes=VMEM),
        cost_estimate=pl.CostEstimate(flops=2 * rows * width * 1344, bytes_accessed=20 << 20, transcendentals=rows * 512),
    )(both, both, wj, ww, add, back, table)


def spread_kernel(place_ref, mixed_ref, wg_ref, act_ref, wj_ref, ww_ref, dense_ref, narrow_ref, *refs):
    chips, own = mixed_ref.shape[0], mixed_ref.shape[2]
    flat = lambda ref: ref[...].reshape(chips * own, ref.shape[3])
    mixed = flat(mixed_ref)
    u = dot_nt(mixed, wj_ref[...]) + dot_nt(flat(wg_ref), ww_ref[...])
    out = dot_nn(mixed, dense_ref[...]) + dot_nn(flat(act_ref), narrow_ref[...])
    u = [u[q * own:(q + 1) * own] for q in range(chips)]
    out = [out[q * own:(q + 1) * own] for q in range(chips)]
    far = [q ^ place_ref[1] for q in range(chips)]
    if len(refs) == 1:
        for q in range(chips):
            refs[0][0, far[q]] = u[q].astype(BF16)
            refs[0][1, far[q]] = out[q].astype(BF16)
        return
    got_ref, near_ref, far_ref = refs[:3]
    u = [(u[q] + got_ref[0, far[q]].astype(F32)).astype(BF16) for q in range(chips)]
    out = [(out[q] + got_ref[1, far[q]].astype(F32)).astype(BF16) for q in range(chips)]
    low = place_ref[1] == 0
    near_ref[0] = jnp.where(low, u[0], u[1])
    far_ref[0] = jnp.where(low, u[1], u[0])
    for d, ref in enumerate(refs[3:]):
        @pl.when(pl.program_id(0) == d)
        def _():
            ref[0] = jnp.where(low, out[0], out[1])
            ref[1] = jnp.where(low, out[1], out[0])


def spread(place, mixed, wg, act, wj, ww, dense, narrow, got=None):
    rows, width = mixed.shape[0], wj.shape[0]
    own, chips, per = rows // N_CTX, N_CTX // 2, 2
    deep = chips // per
    whole = lambda a: pl.BlockSpec(a.shape, lambda i, place: (0, 0))
    split = lambda a: a.reshape(chips, 2, own, a.shape[1])
    tall = lambda a: pl.BlockSpec((per, 1, own, a.shape[1]), lambda i, place: ((place[0] + i) % deep, place[2], 0, 0))
    pair = pl.BlockSpec((2, per, own, width), lambda i, place: (0, i, 0, 0))
    shape = lambda *lead: jax.ShapeDtypeStruct(lead + (own, width), BF16)
    if got is None:
        more, out_specs, out_shape = [], pair, shape(2, chips)
    else:
        more = [got]
        out_specs = ([pl.BlockSpec((1, own, width), lambda i, place: (i, 0, 0))] * 2
                     + [pl.BlockSpec((per, own, width), lambda i, place: (0, 0, 0))] * deep)
        out_shape = [shape(deep)] * 2 + [shape(per)] * deep
    return pl.pallas_call(
        spread_kernel,
        grid_spec=pltpu.PrefetchScalarGridSpec(
            num_scalar_prefetch=1,
            grid=(deep,),
            in_specs=[tall(mixed), tall(wg), tall(act), whole(wj), whole(ww), whole(dense), whole(narrow)]
            + [pair] * len(more),
            out_specs=out_specs),
        out_shape=out_shape,
        compiler_params=pltpu.CompilerParams(vmem_limit_bytes=VMEM),
        cost_estimate=pl.CostEstimate(flops=rows * width * 1024, bytes_accessed=9 << 20, transcendentals=0),
    )(place, split(mixed), split(wg), split(act), wj, ww, dense, narrow, *more)


def finish_early_kernel(f_ref, all_ref, weight_ref, gain_ref, shift_ref,
                        widen_ref, narrow_ref, gain_out, shift_out, bias_out, bias_s):
    n, ff = weight_ref.shape
    k = all_ref.shape[2] // 2
    per = k // N_FSDP
    gain, shift = gain_ref[...], shift_ref[...]
    g_sum = jnp.zeros((n, n), F32)
    s_sum = jnp.zeros((n, n), F32)
    for c in range(N_CTX):
        for q in range(narrow_ref.shape[1] // k):
            narrow_ref[c * per:(c + 1) * per, q * k:(q + 1) * k] = all_ref[c, q * per:(q + 1) * per, k:].astype(F32)
    group = n // per
    for h in range(N_CTX // group):
        parts = [all_ref[h * group + i, :, :k].astype(F32) for i in range(group)]
        for f in range(N_FSDP):
            full = jnp.concatenate([p[:, f * per:(f + 1) * per] for p in parts], axis=1)
            m, bias = full[:n], full[n:n + 1]
            at = f * (ff // N_FSDP) + h * n
            w = weight_ref[:, at:at + n].astype(F32)
            widen_ref[:, at:at + n] = gain * m + shift * bias
            g_sum += w * m
            s_sum += w * bias
            bias_s[:, at:at + n] = full[n:n + 8]
    gain_out[...] = jnp.sum(g_sum.T, axis=0, keepdims=True)
    shift_out[...] = jnp.sum(s_sum.T, axis=0, keepdims=True)
    own = bias_out.shape[1]
    bias_out[...] = bias_s[:, pl.ds(pl.multiple_of(f_ref[0] * own, own), own)][0:1]


def finish_late_kernel(f_ref, core_ref, mine_ref, other_ref, weight_ref, gain_ref, shift_ref,
                       joint_ref, dense_ref, gain_out, shift_out, bias_out, bias_s):
    n = weight_ref.shape[0]
    hd = mine_ref.shape[2] // 4
    width = weight_ref.shape[1] // 3
    even = core_ref[0] == 0
    gain, shift = gain_ref[...], shift_ref[...]
    g_sum = jnp.zeros((n, 2 * hd), F32)
    s_sum = jnp.zeros((n, 2 * hd), F32)
    for q in range(mine_ref.shape[0]):
        mine, other = mine_ref[q].astype(F32), other_ref[q].astype(F32)
        pair = [jnp.where(even, mine, other), jnp.where(even, other, mine)]
        for k in range(3):
            full = jnp.concatenate([p[:, k * hd:(k + 1) * hd] for p in pair], axis=1)
            at = k * width + q * (2 * hd)
            m, bias = full[:n], full[n:n + 1]
            w = weight_ref[:, at:at + 2 * hd].astype(F32)
            joint_ref[:, at:at + 2 * hd] = gain * m + shift * bias
            g_sum += w * m
            s_sum += w * bias
            bias_s[:, at:at + 2 * hd] = full[n:n + 8]
        for b in range(2):
            dense_ref[b * hd:(b + 1) * hd, q * n:(q + 1) * n] = pair[b][:n].T[3 * hd:]
    gain_out[...] = jnp.sum(g_sum.T, axis=0, keepdims=True)
    shift_out[...] = jnp.sum(s_sum.T, axis=0, keepdims=True)
    own = bias_out.shape[1]
    bias_out[...] = bias_s[:, pl.ds(pl.multiple_of(f_ref[0] * own, 128), own)][0:1]


def finish(kernel, places, gathered, weight, gain, shift, side):
    n, columns = weight.shape
    vmem = pl.BlockSpec(memory_space=pltpu.VMEM)
    row = lambda m: jax.ShapeDtypeStruct((1, m), F32)
    wide = lambda v: v.astype(F32)[:, None]
    out = pl.pallas_call(
        kernel,
        in_specs=[pl.BlockSpec(memory_space=pltpu.SMEM)] * len(places) + [vmem] * (len(gathered) + 3),
        out_specs=[vmem] * 5,
        out_shape=[jax.ShapeDtypeStruct(weight.shape, F32), jax.ShapeDtypeStruct(side, F32), row(n), row(n),
                   row(columns // N_FSDP)],
        scratch_shapes=[pltpu.VMEM((8, columns), F32)],
        compiler_params=pltpu.CompilerParams(vmem_limit_bytes=VMEM),
        cost_estimate=pl.CostEstimate(flops=8 * weight.size, bytes_accessed=12 * weight.size, transcendentals=0),
    )(*places, *gathered, weight, wide(gain), wide(shift))
    return out[0], out[1], out[2][0], out[3][0], out[4][0]


def attention_kernel(order_ref, joint_ref, xhat_ref, both_ref, out_ref, late_ref,
                     xhat_s, up_s, sems, joint_s, k_s, v_s, qT_s, kT_s, vT_s, gT_s,
                     oT_s, dqT_s, dkT_s, dvT_s, cosT_s, sinT_s, out_s, mixedT_s):
    rows, hd = joint_ref.shape[0], out_ref.shape[1] // 4
    slots, half, tile = N_CTX, rows // (2 * N_CTX), 256
    own = rows // slots
    last = 2 * slots - 1
    xhat_copy = pltpu.make_async_copy(xhat_ref, xhat_s, sems.at[0])
    up_copy = pltpu.make_async_copy(both_ref.at[:, pl.ds(own, own), :], up_s, sems.at[1])
    xhat_copy.start()
    up_copy.start()
    for j in range(slots):
        p = order_ref[j]
        for h in range(2):
            src = pl.ds(j * 2 * half + h * half, half)
            dst = pl.ds(pl.multiple_of((p if h == 0 else last - p) * half, half), half)
            joint_s[dst, :] = joint_ref[src, :]
    scale = hd ** -0.5

    def spin(t, c, s):
        return jnp.concatenate([t[0:8] * c - t[8:16] * s, t[8:16] * c + t[0:8] * s, t[16:]], axis=0)

    for i in range(rows // tile):
        at = pl.ds(i * tile, tile)
        jT = joint_s[at, :].T
        c, s = jT[4 * hd:4 * hd + 8], jT[4 * hd + 8:4 * hd + 16]
        cosT_s[:, at] = c
        sinT_s[:, at] = s
        qT = spin(jT[0:hd], c, s).astype(BF16)
        kT = spin(jT[hd:2 * hd], c, s).astype(BF16)
        vT = jT[2 * hd:3 * hd].astype(BF16)
        qT_s[:, at] = (qT.astype(F32) * scale).astype(BF16)
        kT_s[:, at] = kT
        vT_s[:, at] = vT
        k_s[at, :] = kT.astype(F32).T.astype(BF16)
        v_s[at, :] = vT.astype(F32).T.astype(BF16)
        gT_s[:, at] = jT[3 * hd:4 * hd].astype(BF16)
    dkT_s[...] = jnp.zeros_like(dkT_s)
    dvT_s[...] = jnp.zeros_like(dvT_s)
    key_at = lax.broadcasted_iota(jnp.int32, (tile, tile), 0)
    query_at = lax.broadcasted_iota(jnp.int32, (tile, tile), 1)
    seen = key_at <= query_at
    dot = lambda a, b: jnp.dot(a, b, preferred_element_type=F32)
    dot_nt = lambda a, b: lax.dot_general(a, b, (((1,), (1,)), ((), ())), preferred_element_type=F32)
    for i in range(rows // tile):
        at = pl.ds(i * tile, tile)
        span = (i + 1) * tile
        upto = pl.ds(0, span)
        qT, gT = qT_s[:, at], gT_s[:, at]
        sT = dot(k_s[upto, :], qT)
        edge = jnp.where(seen, sT[i * tile:], NEGATIVE)
        sT = edge if i == 0 else jnp.concatenate([sT[:i * tile], edge], axis=0)
        largest = jnp.max(sT, axis=0, keepdims=True)
        e = jnp.exp(sT - largest)
        pT = e * (1.0 / jnp.sum(e, axis=0, keepdims=True))
        pT_low = pT.astype(BF16)
        dpT = dot(v_s[upto, :], gT)
        balance = jnp.sum(dpT * pT, axis=0, keepdims=True)
        dsT = (pT * (dpT - balance)).astype(BF16)
        oT_s[:, at] = dot(vT_s[:, upto], pT_low)
        dqT_s[:, at] = dot(kT_s[:, upto], dsT) * scale
        dkT_s[:, upto] += dot_nt(qT, dsT)
        dvT_s[:, upto] += dot_nt(gT, pT_low)
    for i in range(rows // tile):
        at = pl.ds(i * tile, tile)
        c, s = cosT_s[:, at], -sinT_s[:, at]
        full = jnp.concatenate(
            [spin(dqT_s[:, at], c, s), spin(dkT_s[:, at], c, s), dvT_s[:, at], oT_s[:, at]], axis=0)
        out_s[at, :] = full.T.astype(BF16)
    for j in range(slots):
        p = order_ref[j]
        for h in range(2):
            dst = pl.ds(j * 2 * half + h * half, half)
            src = pl.ds(pl.multiple_of((p if h == 0 else last - p) * half, half), half)
            out_ref[dst, :] = out_s[src, :]
    mixedT_s[...] = out_ref[...].T
    n = late_ref.shape[1] - 16
    sums = dot(jnp.ones((16, rows), BF16), out_ref[...]).astype(BF16)
    xhat_copy.wait()
    up_copy.wait()
    for i in range(late_ref.shape[0] * n // tile):
        at = slice(i * tile, (i + 1) * tile)
        joint = dot(mixedT_s[0:3 * hd, :], xhat_s[:, at])
        dense = dot(mixedT_s[3 * hd:, :], up_s[:, :, at].reshape(rows, tile))
        full = jnp.concatenate([joint, dense], axis=0).T.astype(BF16)
        for b in range(tile // n):
            late_ref[i * (tile // n) + b, 0:n, :] = full[b * n:(b + 1) * n]
            late_ref[i * (tile // n) + b, n:, :] = sums


def attention(order, joint, xhat, both):
    rows, width = xhat.shape
    hd = width // HEADS
    own = rows // N_CTX
    vmem = pl.BlockSpec(memory_space=pltpu.VMEM)
    anywhere = pl.BlockSpec(memory_space=pl.ANY)
    return pl.pallas_call(
        attention_kernel,
        out_shape=[jax.ShapeDtypeStruct((rows, 4 * hd), BF16),
                   jax.ShapeDtypeStruct((N_FSDP, width // N_FSDP + 16, 4 * hd), BF16)],
        in_specs=[pl.BlockSpec(memory_space=pltpu.SMEM), vmem, anywhere, anywhere],
        out_specs=[vmem, vmem],
        scratch_shapes=[
            pltpu.VMEM((rows, width), BF16),
            pltpu.VMEM((N_CTX, own, width), BF16),
            pltpu.SemaphoreType.DMA((2,)),
            pltpu.VMEM(joint.shape, F32),
            pltpu.VMEM((rows, hd), BF16),
            pltpu.VMEM((rows, hd), BF16),
            pltpu.VMEM((hd, rows), BF16),
            pltpu.VMEM((hd, rows), BF16),
            pltpu.VMEM((hd, rows), BF16),
            pltpu.VMEM((hd, rows), BF16),
            pltpu.VMEM((hd, rows), F32),
            pltpu.VMEM((hd, rows), F32),
            pltpu.VMEM((hd, rows), F32),
            pltpu.VMEM((hd, rows), F32),
            pltpu.VMEM((8, rows), F32),
            pltpu.VMEM((8, rows), F32),
            pltpu.VMEM((rows, 4 * hd), BF16),
            pltpu.VMEM((4 * hd, rows), BF16),
        ],
        compiler_params=pltpu.CompilerParams(vmem_limit_bytes=VMEM),
        cost_estimate=pl.CostEstimate(flops=8 * rows * rows * hd, bytes_accessed=14 << 20, transcendentals=rows * rows // 2),
    )(order, joint, xhat, both)


def shards(
    tokens, upstream, block_pairs, rotary_place,
    first_gain, first_shift, joint_weight, joint_bias, dense_weight, dense_bias,
    second_gain, second_shift, widen_weight, widen_bias, narrow_weight, narrow_bias,
):
    own_rows, width = tokens.shape[1], tokens.shape[2]
    hd = width // HEADS
    ff = widen_weight.shape[1]
    ffc = ff // N_CTX
    rows = own_rows * N_CTX
    c = lax.axis_index("ctx")
    f = lax.axis_index("fsdp")
    own_tokens, own_up = tokens[0], upstream[0]
    d_own = width // N_FSDP

    per = ffc // N_FSDP
    both = lax.all_gather(jnp.concatenate([own_tokens, own_up], axis=0), "ctx", axis=0)
    joint_part = lax.dynamic_index_in_dim(joint_weight.reshape(d_own, 3, HEADS, hd), c, 2, keepdims=False)
    vectors = jnp.concatenate(
        [v[:, None] for v in (first_gain, first_shift, second_gain, second_shift, dense_bias, narrow_bias)]
        + [joint_bias.reshape(d_own, 3), widen_bias.reshape(d_own, 4), jnp.zeros((d_own, 51), BF16)], axis=1)
    widen_part = [lax.dynamic_slice_in_dim(widen_weight, g * (ff // N_FSDP) + c * per, per, axis=1)
                  for g in range(N_FSDP)]
    narrow_part = lax.dynamic_slice_in_dim(narrow_weight, c * per, per, axis=0)
    narrow_part = jnp.concatenate([narrow_part[:, q * ffc:(q + 1) * ffc] for q in range(width // ffc)], axis=0)
    part = jnp.concatenate([joint_part.reshape(d_own, 3 * hd), vectors] + widen_part + [narrow_part], axis=1)
    slices = lax.all_to_all(jnp.broadcast_to(part[None], (N_FSDP,) + part.shape), "fsdp", 0, 0, tiled=True)
    dense_w = turn(lax.dynamic_slice_in_dim(dense_weight, (c % 2) * hd, hd, axis=0))
    place_all = lax.all_gather(rotary_place[0], "ctx", axis=0, tiled=True).astype(F32)
    narrow_w = jnp.concatenate(
        [slices[:, q * per:(q + 1) * per, 4 * hd + ffc:] for q in range(width // ffc)], axis=2).reshape(ffc, width)
    slices = slices.reshape(width, part.shape[1])
    back_w = jnp.concatenate([dense_w, narrow_w], axis=0)

    lane = jnp.arange(128)[None, :]
    angles = place_all[:, None] * (ROTARY_BASE ** (-2.0 * (lane % 8).astype(F32) / 16))
    table = jnp.where(lane < 8, jnp.cos(angles), jnp.sin(angles))
    order = block_pairs[0]

    wj = slices[:, :4 * hd].astype(F32)
    ww = slices[:, 4 * hd:4 * hd + ffc].astype(F32)
    vec = slices[:, 3 * hd:4 * hd].astype(F32)
    g1, s1, g2, s2 = vec[:, 0:1], vec[:, 1:2], vec[:, 2:3], vec[:, 3:4]
    dense_b, narrow_b = vec[:, 4], vec[:, 5]
    jb_full = vec[:, 6:9].reshape(3, HEADS, hd)
    wb_full = vec[:, 9:13].reshape(ff)
    jb_own = lax.dynamic_index_in_dim(jb_full, c, 1, keepdims=False).reshape(3 * hd)
    wb_own = lax.dynamic_index_in_dim(wb_full.reshape(N_FSDP, N_CTX, per), c, 1, keepdims=False).reshape(ffc)
    wj = jnp.where(jnp.arange(4 * hd)[None, :] < 3 * hd, wj, 0.0)
    wj_g = (g1 * wj).astype(BF16)
    ww_g = (g2 * ww).astype(BF16)
    shifted = jnp.concatenate([
        jnp.sum(s1 * wj, axis=0) + jnp.pad(jb_own, (0, hd)), jnp.sum(s2 * ww, axis=0) + wb_own])[None, :]
    dense_p = jnp.pad(dense_w, ((3 * hd, 0), (0, 0)))

    both, table, dense_p = tie(both, table, dense_p)
    xhat, joint, act, wg, early = project(both, wj_g, ww_g, shifted, back_w, table)
    early = lax.all_to_all(early, "fsdp", 0, 0, tiled=True)

    mixed, late = attention(order, joint, xhat, both)
    core = (c % 2)[None]
    shares = (mixed, wg, act, wj_g, ww_g, dense_p, narrow_w)
    place = lambda parity: jnp.stack([c // 4, (c // 2) % 2, parity]).astype(jnp.int32)
    other = spread(place(1 - c % 2), *shares)
    other, early, late = tie(other, early, late)

    early = jnp.sum(early.astype(F32), axis=0)
    bias_grad = early[d_own, ffc:ffc + d_own]
    early_all = lax.all_gather(early.astype(BF16), "ctx", axis=0)
    near, far, *outs = spread(place(c % 2), *shares, move(other, OTHER_CORE))

    late, near, far, *outs = tie(lax.all_to_all(late, "fsdp", 0, 0, tiled=True), near, far, *outs)

    wide = lambda v: v.astype(F32)
    low = jnp.sum(wide(late), axis=0).astype(BF16)
    low = jnp.concatenate([low[:, :3 * hd], turn(low[:, 3 * hd:])], axis=1)
    late_mine, far, *outs[1:] = tie(
        gather_chips(low), move(far, ACROSS_Y), *[move(outs[d], AHEAD_Z[d]) for d in range(1, 4)])
    late_all = late_mine, move(late_mine, OTHER_CORE)
    near = (wide(near) + wide(far)).astype(BF16)
    out_own = sum(wide(v) for v in outs)
    across = out_own[1].astype(BF16)
    u_own = wide(near[0]) + sum(wide(move(near[d], AHEAD_Z[d])) for d in range(1, 4))
    out_own = out_own[0] + wide(move(across, ACROSS_Y))

    widen_grad, narrow_grad, g2_grad, s2_grad, wb_shard = finish(
        finish_early_kernel, (f[None],), (early_all,), widen_weight, second_gain, second_shift, (2 * ffc, width))

    own_x = own_tokens.astype(F32)
    block_out = (own_x + out_own + dense_b + narrow_b).astype(BF16)
    own_center = own_x - jnp.mean(own_x, axis=-1, keepdims=True)
    own_rstd = lax.rsqrt(jnp.mean(own_center * own_center, axis=-1, keepdims=True) + EPSILON)
    own_xhat = own_center * own_rstd
    tokens_grad = own_up.astype(F32) + own_rstd * (
        u_own - jnp.mean(u_own, axis=-1, keepdims=True)
        - own_xhat * jnp.mean(u_own * own_xhat, axis=-1, keepdims=True))

    joint_grad, dense_grad, g1_grad, s1_grad, jb_shard = finish(
        finish_late_kernel, (f[None], core), late_all, joint_weight, first_gain, first_shift, (2 * hd, width))
    return (
        block_out[None], tokens_grad[None], g1_grad, s1_grad, joint_grad, jb_shard,
        dense_grad, bias_grad, g2_grad, s2_grad, widen_grad, wb_shard, narrow_grad, bias_grad,
    )


def solution(mesh):
    rows = P("fsdp", "ctx", None)
    vec, mat = P("fsdp"), P("fsdp", None)
    in_specs = (rows, rows, mat, P("fsdp", "ctx"), vec, vec, mat, vec, mat, vec, vec, vec, mat, vec, mat, vec)
    out_specs = (rows, rows, vec, vec, mat, vec, mat, vec, vec, vec, mat, vec, mat, vec)
    return jax.shard_map(shards, mesh=mesh, in_specs=in_specs, out_specs=out_specs, check_vma=False)
```
